32 devices in a mesh: seq: 4 (over y, core), dp: 8 (over z, x).
Axes of the slice: x: 2, y: 2, z: 4, core: 2. Of those that a mesh axis runs over, the one named last changes fastest.
Arguments:
- tokens: bfloat16 [16, 1024, 1024], P('dp', 'seq'), may hold values from -6 to 6
- first_values: bfloat16 [16, 1024, 1024], P('dp', 'seq'), may hold values from -6 to 6
- seq_counts: int32 [8], P('dp'), may hold values from 1 to 2, as said below
- norm1_gain: bfloat16 [1024], P('dp'), may hold values from 0.5 to 1.5
- query_weight: bfloat16 [1024, 1024], P('dp', 'seq'), may hold values from -0.1875 to 0.1875
- key_weight: bfloat16 [1024, 1024], P('dp', 'seq'), may hold values from -0.1875 to 0.1875
- value_weight: bfloat16 [1024, 1024], P('dp', 'seq'), may hold values from -0.1875 to 0.1875
- out_weight: bfloat16 [1024, 1024], P('dp', 'seq'), may hold values from -1.5 to 1.5
- norm2_gain: bfloat16 [1024], P('dp'), may hold values from 0.5 to 1.5
- gate_weight: bfloat16 [1024, 2816], P('dp', 'seq'), may hold values from -0.1875 to 0.1875
- up_weight: bfloat16 [1024, 2816], P('dp', 'seq'), may hold values from -0.1875 to 0.1875
- down_weight: bfloat16 [2816, 1024], P('dp', 'seq'), may hold values from -0.109375 to 0.109375
- output_cotangent: bfloat16 [16, 1024, 1024], P('dp', 'seq'), may hold values from -6 to 6
Outputs:
- output: bfloat16 [16, 1024, 1024], P('dp', 'seq')
- input_grad: float32 [16, 1024, 1024], P('dp', 'seq')
- first_values_grad: float32 [16, 1024, 1024], P('dp', 'seq')
- norm1_gain_grad: float32 [1024], P('dp')
- query_weight_grad: float32 [1024, 1024], P('dp', 'seq')
- key_weight_grad: float32 [1024, 1024], P('dp', 'seq')
- value_weight_grad: float32 [1024, 1024], P('dp', 'seq')
- out_weight_grad: float32 [1024, 1024], P('dp', 'seq')
- norm2_gain_grad: float32 [1024], P('dp')
- gate_weight_grad: float32 [1024, 2816], P('dp', 'seq')
- up_weight_grad: float32 [1024, 2816], P('dp', 'seq')
- down_weight_grad: float32 [2816, 1024], P('dp', 'seq')
The draws below stay inside these ranges and needn't reach their ends.
Inputs may be any that keep to these rules, and one draw needn't show every extreme that they name: `seq_counts`: sequence s is slot s mod 2 of group s // 2; a group's live sequences fill its first slots. Some group uses all 2 slots and some group uses one.
All inputs are finite; a program needn't handle non-finite values.
Results may differ from the reference program's by a relative error of at most 0.019.
Values may be sent and summed in bfloat16 or wider, within the bound.
No kernel may reach another device: no remote copies, remote signals or barrier semaphores. Data moves between devices by JAX's collectives and lax.ppermute only.
A program may use at most 256 MiB of HBM per device.

```python
import jax
import jax.numpy as jnp
from jax import lax

D = 1024
HEADS = 16
FF = 2816
SLOTS = 2
LEN = 1024
GROUPS = 8
SEQS = 16


def draw_seq_counts(key, part):
    key = jax.random.fold_in(key, 11)
    key_counts, key_order = jax.random.split(key)
    counts = jax.random.randint(key_counts, (GROUPS,), 1, SLOTS + 1)
    ordering = jax.random.permutation(key_order, GROUPS)
    counts = counts.at[ordering[0]].set(SLOTS)
    counts = counts.at[ordering[1]].set(1)
    return counts.astype(jnp.int32)


def steps_of(key, extent, shards, low, top_value):
    loudness, own = 1.0, jax.random.fold_in(key, 6)
    for dim, shards_of in shards:
        draws = jnp.exp(jax.random.uniform(jax.random.fold_in(own, dim), (shards_of,), jnp.float32, low / len(shards), top_value / len(shards)))
        loudness = loudness * jnp.repeat(draws, extent[dim] // shards_of).reshape([-1 if axis == dim else 1 for axis in range(len(extent))])
    return loudness


def bell_draw(stream_key, shape, scale, reach, shards=(), kind=jnp.bfloat16):
    level = steps_of(stream_key, shape, shards, -0.22, 0.18) if shards else 1.0
    values = jax.random.normal(stream_key, shape, jnp.float32) * scale * level
    return jnp.minimum(jnp.maximum(values, -reach), reach).astype(kind)


def setup_inputs(seed: int = 0) -> dict:
    splits = jax.random.split(jax.random.key(seed), 14)
    tokens = bell_draw(splits[0], (SEQS, LEN, D), 1.0, 6.0, ((0, 8), (1, 4)))
    first_values = bell_draw(splits[1], (SEQS, LEN, D), 1.0, 6.0, ((0, 8), (1, 4)))
    seq_counts = draw_seq_counts(jax.random.fold_in(splits[13], 71), 0)
    norm1_gain = jnp.clip(1.0 + 0.1 * jax.random.normal(splits[3], (D,), jnp.float32), 0.5, 1.5).astype(jnp.bfloat16)
    query_weight = bell_draw(splits[4], (D, D), D ** -0.5, 0.1875, ((0, 8), (1, 4)))
    key_weight = bell_draw(splits[5], (D, D), D ** -0.5, 0.1875, ((0, 8), (1, 4)))
    value_weight = bell_draw(splits[6], (D, D), D ** -0.5, 0.1875, ((0, 8), (1, 4)))
    out_weight = bell_draw(splits[7], (D, D), (D // 64) ** -0.5, 1.5, ((0, 8), (1, 4)))
    norm2_gain = jnp.clip(1.0 + 0.1 * jax.random.normal(splits[8], (D,), jnp.float32), 0.5, 1.5).astype(jnp.bfloat16)
    gate_weight = bell_draw(splits[9], (D, FF), D ** -0.5, 0.1875, ((0, 8), (1, 4)))
    up_weight = bell_draw(splits[10], (D, FF), D ** -0.5, 0.1875, ((0, 8), (1, 4)))
    down_weight = bell_draw(splits[11], (FF, D), FF ** -0.5, 0.109375, ((0, 8), (1, 4)))
    output_cotangent = bell_draw(splits[12], (SEQS, LEN, D), 1.0, 6.0, ((0, 8), (1, 4)))
    return dict(tokens=tokens, first_values=first_values, seq_counts=seq_counts, norm1_gain=norm1_gain, query_weight=query_weight, key_weight=key_weight, value_weight=value_weight, out_weight=out_weight, norm2_gain=norm2_gain, gate_weight=gate_weight, up_weight=up_weight, down_weight=down_weight, output_cotangent=output_cotangent)


EPSILON = 1e-06

@jax.custom_vjp
def low(v):
    return lax.optimization_barrier(v.astype(jnp.bfloat16)).astype(jnp.float32)

@jax.custom_vjp
def low_back(v):
    return v

def low_keep(v):
    return (low(v), None)

def low_pass(kept, grad):
    return (grad,)

def back_keep(v):
    return (v, None)

def back_low(kept, grad):
    return (low(grad),)
low.defvjp(low_keep, low_pass)
low_back.defvjp(back_keep, back_low)

def narrow_both(values):
    return low_back(low(values))

def scaled_norm(values, gain_vec):
    inverse = lax.rsqrt(lax.optimization_barrier(jnp.mean(values * values, axis=-1, keepdims=True)) + EPSILON)
    return values * inverse * gain_vec

def rotate(values, positions, head_count, direction):
    row_count, model_width = values.shape
    head_size = model_width // head_count
    half_size = head_size // 2
    frequency = 10000.0 ** (-(jnp.arange(half_size).astype(jnp.float32) * 2.0) / head_size)
    angles = positions.astype(jnp.float32)[:, None] * frequency[None, :]
    cosine = jnp.cos(angles)[:, None, :]
    sine_part = direction * jnp.sin(angles)[:, None, :]
    shaped = values.reshape(row_count, head_count, head_size)
    first_half = shaped[..., :half_size]
    second = shaped[..., half_size:]
    turned = jnp.concatenate([first_half * cosine - second * sine_part, second * cosine + first_half * sine_part], axis=-1)
    return turned.reshape(row_count, model_width)

def swiglu(gate_in, up_in):
    return jax.nn.silu(gate_in) * up_in

def product(left, right):
    return jnp.dot(left, right, precision=lax.Precision.HIGHEST)

def layer_one(values, first_vals, live_mask, weight_set):
    gain_one, w_query, w_key, w_value, w_out, gain_two, w_gate, w_up, w_down = weight_set
    length, model_width = values.shape
    head_size = model_width // HEADS
    positions = jnp.arange(length)
    h_first = low(scaled_norm(values, gain_one))
    query = low(rotate(low_back(product(h_first, w_query)), positions, HEADS, 1.0))
    key_rot = low(rotate(low_back(product(h_first, w_key)), positions, HEADS, 1.0))
    blended = low(0.5 * low_back(product(h_first, w_value)) + 0.5 * first_vals)
    query_heads = query.reshape(length, HEADS, head_size)
    key_heads = key_rot.reshape(length, HEADS, head_size)
    value_heads = blended.reshape(length, HEADS, head_size)
    raw_scores = jnp.einsum('qhd,khd->hqk', query_heads, key_heads, precision=lax.Precision.HIGHEST) * 0.125
    visible = positions[None, :] <= positions[:, None]
    scores = low_back(jnp.where(visible[None, :, :], raw_scores, -1e+30))
    log_total = jax.nn.logsumexp(scores, axis=-1, keepdims=True)
    probs = low(jnp.exp(scores - log_total))
    mixed = jnp.einsum('hqk,khd->qhd', probs, value_heads, precision=lax.Precision.HIGHEST)
    attended = narrow_both(mixed.reshape(length, model_width))
    middle = values + low_back(product(attended, w_out))
    h_second = low(scaled_norm(middle, gain_two))
    gate = low_back(product(h_second, w_gate))
    up_part = low_back(product(h_second, w_up))
    hidden = low(swiglu(gate, up_part))
    result = low_back(product(hidden, w_down))
    return live_mask * (middle + result)

def reference(tokens, first_values, seq_counts, norm1_gain, query_weight, key_weight, value_weight, out_weight, norm2_gain, gate_weight, up_weight, down_weight, output_cotangent):
    seq_total = tokens.shape[0]
    slot_index = jnp.arange(seq_total) % SLOTS
    group_index = jnp.arange(seq_total) // SLOTS
    live_rows = (slot_index < seq_counts[group_index]).astype(jnp.float32)[:, None, None]
    weight_list = (norm1_gain.astype(jnp.float32), query_weight.astype(jnp.float32), key_weight.astype(jnp.float32), value_weight.astype(jnp.float32), out_weight.astype(jnp.float32), norm2_gain.astype(jnp.float32), gate_weight.astype(jnp.float32), up_weight.astype(jnp.float32), down_weight.astype(jnp.float32))

    def forward(values, first_vals, weight_set):

        def scan_step(carried, scan_item):
            one_values, one_first, one_live = scan_item
            return (carried, jax.checkpoint(layer_one)(one_values, one_first, one_live, weight_set))
        _, outputs = lax.scan(scan_step, jnp.float32(0.0), (values, first_vals, live_rows))
        return outputs
    outputs, pullback = jax.vjp(forward, tokens.astype(jnp.float32), first_values.astype(jnp.float32), weight_list)
    grad_tokens, grad_first, grad_weights = pullback(output_cotangent.astype(jnp.float32))
    return (outputs.astype(jnp.bfloat16), grad_tokens, grad_first, grad_weights[0], grad_weights[1], grad_weights[2], grad_weights[3], grad_weights[4], grad_weights[5], grad_weights[6], grad_weights[7], grad_weights[8])
```

```python
import functools

import jax
import jax.numpy as jnp
from jax import lax
from jax.experimental import pallas as pl
from jax.experimental.pallas import tpu as pltpu
from jax.sharding import PartitionSpec as P

HEAD = 64
EPSILON = 1e-06
TILE = 256
BLOCKS = 8
F32 = jnp.float32
BF16 = jnp.bfloat16
VMEM_LIMIT = 56 * 1024 * 1024
MESH_Y, MESH_C = 2, 1
ZM, Z1, X1 = 6, 2, 1


def dot_nn(a, b):
    return lax.dot_general(a, b, (((1,), (0,)), ((), ())), preferred_element_type=F32)


def dot_nt(a, b):
    return lax.dot_general(a, b, (((1,), (1,)), ((), ())), preferred_element_type=F32)


def dot_tn(a, b):
    return lax.dot_general(a, b, (((0,), (0,)), ((), ())), preferred_element_type=F32)


def flip(value, axis, mask):
    pairs = [(i, i ^ mask) for i in range(lax.axis_size(axis))]
    return lax.ppermute(value, axis, pairs)


def pick(flag, when_one, when_zero):
    return jnp.where(flag == 1, when_one, when_zero)


def call(body, outs, ins, scratch, flops, moved, exps=0, grid=None, in_specs=None, out_specs=None):
    spaces = {"v": pltpu.VMEM, "s": pltpu.SMEM, "a": pl.ANY}
    if in_specs is None:
        in_specs = [pl.BlockSpec(memory_space=spaces[kind]) for kind, _ in ins]
        out_specs = [pl.BlockSpec(memory_space=pltpu.VMEM) for _ in outs]
    kwargs = {} if grid is None else {"grid": grid}
    return pl.pallas_call(
        body,
        out_shape=[jax.ShapeDtypeStruct(shape, kind) for shape, kind in outs],
        in_specs=in_specs,
        out_specs=out_specs,
        scratch_shapes=scratch,
        cost_estimate=pl.CostEstimate(flops=flops, bytes_accessed=moved, transcendentals=exps),
        compiler_params=pltpu.CompilerParams(vmem_limit_bytes=VMEM_LIMIT),
        **kwargs,
    )(*[value for _, value in ins])


def run_copies(copies):
    for copy in copies:
        copy.start()
    for copy in copies:
        copy.wait()


def turned(values, cosine, signed_sine):
    lane = lax.broadcasted_iota(jnp.int32, values.shape, 1)
    ahead = pltpu.roll(values, 128 - HEAD // 2, 1)
    behind = pltpu.roll(values, HEAD // 2, 1)
    partner = jnp.where(lane % HEAD < HEAD // 2, ahead, behind)
    return values * cosine + partner * signed_sine


def place_of(info, bx, b1, bm):
    z = info[3] ^ b1 ^ (3 * bm)
    return z * 2 + (info[4] ^ bx)


def qkv_body(info, x, fv, cosine, sine, a10, a11, a20, a21, h1, q, k, b, w, sem):
    cut = a10.shape[1]
    copies = []
    for by in range(2):
        for bx in range(2):
            for b1 in range(2):
                for bm in range(2):
                    d = place_of(info, bx, b1, bm)
                    i = len(copies)
                    first, second = (a10, a11)[by], (a20, a21)[bx]
                    copies.append(pltpu.make_async_copy(
                        first.at[bx * 4 + b1 * 2 + bm], w.at[by, d, pl.ds(0, cut)], sem.at[i]))
                    copies.append(pltpu.make_async_copy(
                        second.at[by * 4 + b1 * 2 + bm],
                        w.at[by, d, pl.ds(cut, w.shape[2] - cut)], sem.at[i + 1]))
    run_copies(copies)
    rows = 128
    width = w.shape[3]
    model = x.shape[1]
    gains = w[0, :, 3 * rows : 3 * rows + 16, 0:rows]
    gain = jnp.concatenate([gains[d, 0:1, :] for d in range(BLOCKS)], axis=1).astype(F32)

    def step(t, carry):
        at = pl.ds(pl.multiple_of(t * TILE, TILE), TILE)
        xt = x[at, :].astype(F32)
        inverse = lax.rsqrt(jnp.mean(xt * xt, axis=-1, keepdims=True) + EPSILON)
        h = (xt * inverse * gain).astype(BF16)
        h1[at, :] = h
        cos_t, sin_t = cosine[at, :], sine[at, :]
        for by in range(2):
            for n in range(3):
                weight = w[by, :, n * rows : (n + 1) * rows, :].reshape(model, width)
                acc = dot_nn(h, weight)
                cols = pl.ds(by * width, width)
                if n == 2:
                    column = pl.multiple_of(((info[0] ^ by) * 2 + info[1]) * width, width)
                    first = fv[at, pl.ds(column, width)].astype(F32)
                    b[at, cols] = (0.5 * acc + 0.5 * first).astype(BF16)
                else:
                    parts = [
                        turned(acc[:, j : j + 128], cos_t, sin_t) for j in range(0, width, 128)
                    ]
                    (q, k)[n][at, cols] = jnp.concatenate(parts, axis=1).astype(BF16)
        return carry

    lax.fori_loop(0, x.shape[0] // TILE, step, 0)


def split_heads(pair):
    lane = lax.broadcasted_iota(jnp.int32, pair.shape, 1)
    zero = jnp.zeros_like(pair)
    return jnp.concatenate(
        [jnp.where(lane < HEAD, pair, zero), jnp.where(lane < HEAD, zero, pair)], axis=0
    )


def join_heads(both):
    half = both.shape[0] // 2
    lane = lax.broadcasted_iota(jnp.int32, (half, both.shape[1]), 1)
    return jnp.where(lane < HEAD, both[:half], both[half:])


def hide_later(scores, fill):
    length, width = scores.shape
    key_at = lax.broadcasted_iota(jnp.int32, (TILE, width), 0)
    query_at = lax.broadcasted_iota(jnp.int32, (TILE, width), 1) % TILE
    last = jnp.where(key_at <= query_at, scores[length - TILE :], fill)
    if length == TILE:
        return last
    return jnp.concatenate([scores[: length - TILE], last], axis=0)


def attend_body(q, k, b, att, lse):
    for i in range(q.shape[0] // TILE):
        length = (i + 1) * TILE
        queries = split_heads(q[i * TILE : length, :])
        scores = hide_later(dot_nt(k[:length, :], queries) * 0.125, -1e30)
        top = jnp.max(scores, axis=0, keepdims=True)
        grown = jnp.exp(scores - top)
        total = jnp.sum(grown, axis=0, keepdims=True)
        logs = top + jnp.log(total)
        probs = (grown * (1.0 / total)).astype(BF16)
        att[i * TILE : length, :] = join_heads(dot_tn(probs, b[:length, :])).astype(BF16)
        lse[0, 0:1, i * TILE : length] = logs[:, :TILE]
        lse[0, 1:2, i * TILE : length] = logs[:, TILE:]


def attend_back_body(q, k, b, datt, lse, cosine, sine, dq, dk, dv, k_acc, v_acc):
    k_acc[...] = jnp.zeros_like(k_acc)
    v_acc[...] = jnp.zeros_like(v_acc)
    for i in range(q.shape[0] // TILE):
        length = (i + 1) * TILE
        at = slice(i * TILE, length)
        queries = split_heads(q[at, :])
        grads = split_heads(datt[at, :])
        keys = k[:length, :]
        logs = jnp.concatenate([lse[0, 0:1, at], lse[0, 1:2, at]], axis=1)
        scores = dot_nt(keys, queries) * 0.125
        probs = jnp.exp(hide_later(scores - logs, -1e30))
        grad_probs = dot_nt(b[:length, :], grads)
        delta = jnp.sum(probs * grad_probs, axis=0, keepdims=True)
        grad_scores = (probs * (grad_probs - delta)).astype(BF16)
        v_acc[:length, :] += dot_nn(probs.astype(BF16), grads)
        k_acc[:length, :] += dot_nn(grad_scores, queries)
        turned_back = turned(
            0.125 * join_heads(dot_tn(grad_scores, keys)), cosine[at, :], -sine[at, :]
        )
        dq[at, :] = turned_back.astype(BF16)
    for i in range(q.shape[0] // TILE):
        at = slice(i * TILE, (i + 1) * TILE)
        dk[at, :] = turned(0.125 * k_acc[at, :], cosine[at, :], -sine[at, :]).astype(BF16)
        dv[at, :] = (0.5 * v_acc[at, :]).astype(BF16)


def row_spot(info, hidden_block):
    even = (info[3] & 1) ^ info[1]
    t = hidden_block ^ info[0] ^ (info[3] >> 1) ^ even
    return t, t ^ even


def row_copies(info, hidden_block, od0, od1, odx, target, rows, first, sem, start):
    t, bm = row_spot(info, hidden_block)
    copies = []
    count = rows.stop - rows.start
    for by in range(2):
        for bx in range(2):
            row = first + (info[4] ^ bx) * count
            for own in range(2):
                core = info[1] ^ (1 - own)
                column = pl.multiple_of(((info[0] ^ by) * 2 + core) * 256, 256)
                if own:
                    source = (od0, od1)[by].at[bx * 4 + t * 2 + bm, pl.ds(rows.start, count)]
                else:
                    source = odx.at[by, bx, t, pl.ds(rows.start, count)]
                copies.append(pltpu.make_async_copy(
                    source, target.at[pl.ds(pl.multiple_of(row, 16), count), pl.ds(column, 256)],
                    sem.at[start + len(copies)]))
    return copies


def out_copies(info, od0, od1, odx, wo, sem):
    copies = []
    for block in range(2):
        copies += row_copies(
            info, block, od0, od1, odx, wo, slice(0, 128), block * 256, sem, len(copies))
    return copies


def out_body(info, att, od0, od1, odx, part, wo, sem):
    run_copies(out_copies(info, od0, od1, odx, wo, sem))

    def step(t, carry):
        at = pl.ds(pl.multiple_of(t * TILE, TILE), TILE)
        part[at, :] = dot_nn(att[at, :], wo[...]).astype(BF16)
        return carry

    lax.fori_loop(0, att.shape[0] // TILE, step, 0)


def out_back_body(info, gb, att, od0, od1, odx, datt, keep, send, wo, sem):
    run_copies(out_copies(info, od0, od1, odx, wo, sem))

    def step(t, carry):
        at = pl.ds(pl.multiple_of(t * TILE, TILE), TILE)
        datt[at, :] = dot_nt(gb[at, :], wo[...]).astype(BF16)
        return carry

    lax.fori_loop(0, att.shape[0] // TILE, step, 0)
    for by in range(2):
        for own in range(2):
            core = info[1] ^ (1 - own)
            column = pl.multiple_of(((info[0] ^ by) * 2 + core) * 256, 256)
            grad = dot_tn(att[...], gb[:, pl.ds(column, 256)]).astype(BF16)
            for block in range(2):
                t, _ = row_spot(info, block)
                for bx in range(2):
                    row = [grad[block * 256 + j * 128 : block * 256 + (j + 1) * 128] for j in (0, 1)]
                    (send, keep)[own][by, bx, t] = jnp.where((info[4] ^ bx) == 1, row[1], row[0])


def ffn_body(
    info, h2, gy, g0, g1, od0, od1, odx,
    gh2, gux0, gux1, dkeep, dsend, rkeep, rsend,
    wgu, wd, ggu, hid, gh2_acc, res_acc, sem,
):
    units = wd.shape[0]
    half = units // 2
    tiles = h2.shape[0] // TILE
    for block in (1, 0):
        copies = row_copies(info, block, od0, od1, odx, wd, slice(128, 128 + half), 0, sem, 0)
        for bx in range(2):
            for b1 in range(2):
                for bm in range(2):
                    d = place_of(info, bx, b1, bm)
                    for part in range(2):
                        copies.append(pltpu.make_async_copy(
                            (g0, g1)[bx].at[block * 4 + b1 * 2 + bm, :, pl.ds(part * 128, 128)],
                            wgu.at[pl.ds(part * units, units),
                                   pl.ds(pl.multiple_of(d * 128, 128), 128)],
                            sem.at[len(copies)]))
        run_copies(copies)

        def step(t, carry, block=block):
            at = pl.ds(pl.multiple_of(t * TILE, TILE), TILE)
            both = dot_nt(wgu[...], h2[at, :])
            gate, up = both[:units], both[units:]
            sig = 1.0 / (1.0 + jnp.exp(-gate))
            act = gate * sig
            hidden = (act * up).astype(BF16)
            hid[:, at] = hidden
            grad_hidden = dot_nt(wd[...], gy[at, :])
            grad_gate = (grad_hidden * up * (sig + act * (1.0 - sig))).astype(BF16)
            grad_up = (grad_hidden * act).astype(BF16)
            ggu[:units, at] = grad_gate
            ggu[units:, at] = grad_up
            grad_h = dot_tn(ggu[:, at], wgu[...])
            result = dot_tn(hidden, wd[...])
            if block == 1:
                gh2_acc[at, :] = grad_h
                res_acc[at, :] = result
            else:
                gh2[at, :] = (gh2_acc[at, :] + grad_h).astype(BF16)
                result = res_acc[at, :] + result

                @pl.when((t & 1) == info[1])
                def _():
                    rkeep[t >> 1] = result

                @pl.when((t & 1) != info[1])
                def _():
                    rsend[t >> 1] = result.astype(BF16)

            return carry

        lax.fori_loop(0, tiles, step, 0)

        for b1 in range(2):
            for bm in range(2):
                z = info[3] ^ b1 ^ (3 * bm)
                column = pl.multiple_of(z * 256, 256)
                grad = dot_nn(ggu[...], h2[:, pl.ds(column, 256)]).astype(BF16)
                lo, hi = grad[:, :128], grad[:, 128:]
                swap = info[4] == 1
                for bx, part in ((0, jnp.where(swap, hi, lo)), (1, jnp.where(swap, lo, hi))):
                    target = (gux0, gux1)[bx]
                    target[block, b1 * 2 + bm, :, 0:128] = part[:units]
                    target[block, b1 * 2 + bm, :, 128:256] = part[units:]
        t_spot, _ = row_spot(info, block)
        for by in range(2):
            for own in range(2):
                core = info[1] ^ (1 - own)
                column = pl.multiple_of(((info[0] ^ by) * 2 + core) * 256, 256)
                grad = dot_nn(hid[...], gy[:, pl.ds(column, 256)]).astype(BF16)
                for bx in range(2):
                    (dsend, dkeep)[own][by, bx, t_spot] = jnp.where(
                        (info[4] ^ bx) == 1, grad[half:], grad[:half])


def qkv_back_body(
    info, dq, dk, dv, h1, x, gain2, of0, of1, a10, a11, a20, a21,
    out0, out1, gkeep, gsend, w, acc, sem,
):
    cut = a10.shape[1]
    copies = []
    for by in range(2):
        for bx in range(2):
            for b1 in range(2):
                for bm in range(2):
                    d = place_of(info, bx, b1, bm)
                    i = len(copies)
                    first, second = (a10, a11)[by], (a20, a21)[bx]
                    copies.append(pltpu.make_async_copy(
                        first.at[bx * 4 + b1 * 2 + bm], w.at[by, d, pl.ds(0, cut)], sem.at[i]))
                    copies.append(pltpu.make_async_copy(
                        second.at[by * 4 + b1 * 2 + bm],
                        w.at[by, d, pl.ds(cut, w.shape[2] - cut)], sem.at[i + 1]))
    for copy in copies:
        copy.start()
    width = w.shape[3]
    model = x.shape[1]
    for by in (1, 0):
        cols = slice(by * width, (by + 1) * width)
        three = jnp.concatenate([dq[:, cols], dk[:, cols], dv[:, cols]], axis=1)
        for b1 in range(2):
            for bm in range(2):
                z = info[3] ^ b1 ^ (3 * bm)
                grad = dot_tn(h1[:, pl.ds(pl.multiple_of(z * 256, 256), 256)], three).astype(BF16)
                for bx in range(2):
                    part = jnp.where((info[4] ^ bx) == 1, grad[128:], grad[:128])
                    for n in range(3):
                        (out0, out1)[by][bx * 4 + b1 * 2 + bm, n * 128 : (n + 1) * 128, :] = (
                            part[:, n * width : (n + 1) * width])
    for copy in copies:
        copy.wait()
    acc[...] = jnp.zeros_like(acc)

    def step(t, carry):
        at = pl.ds(pl.multiple_of(t * TILE, TILE), TILE)
        grad_h = jnp.zeros((TILE, model), F32)
        for by in range(2):
            cols = slice(by * width, (by + 1) * width)
            for n, grad in enumerate((dq, dk, dv)):
                weight = w[by, :, n * 128 : (n + 1) * 128, :].reshape(model, width)
                grad_h = grad_h + dot_nt(grad[at, cols], weight)
        xt = x[at, :].astype(F32)
        inverse = lax.rsqrt(jnp.mean(xt * xt, axis=-1, keepdims=True) + EPSILON)
        acc[0:1, :] += jnp.sum(grad_h * xt * inverse, axis=0, keepdims=True)

        @pl.when((t & 1) == info[1])
        def _():
            gkeep[t >> 1] = grad_h

        @pl.when((t & 1) != info[1])
        def _():
            gsend[t >> 1] = grad_h.astype(BF16)

        return carry

    lax.fori_loop(0, x.shape[0] // TILE, step, 0)
    for b1 in range(2):
        for bm in range(2):
            for bx in range(2):
                d = place_of(info, bx, b1, bm)
                spot = pl.ds(pl.multiple_of(d * 128, 128), 128)
                row = jnp.concatenate([acc[0:1, spot], gain2[0:1, spot]], axis=1)
                full = jnp.broadcast_to(row, (16, 256)).astype(BF16)
                p = bx * 4 + b1 * 2 + bm
                out0[p, 384:400, :] = full
                out1[p, 384:400, :] = full
                out0[p, 400:528, :] = of0[p]
                out1[p, 400:528, :] = of1[p]


def gathered(shard, flips):
    held = shard[None]
    for axis, mask in flips[:-1]:
        held = jnp.concatenate([held, flip(held, axis, mask)], axis=0)
    return held, flip(held, *flips[-1])


def scattered(send, keep, flips):
    total = keep.astype(F32) + flip(send, *flips[0]).astype(F32)
    for axis, mask in flips[1:]:
        half = total.shape[0] // 2
        outgoing = total[half:].astype(BF16)
        total = total[:half] + flip(outgoing, axis, mask).astype(F32)
    return total[0]


def on_device(
    tokens, first_values, seq_counts, norm1_gain, query_weight, key_weight, value_weight,
    out_weight, norm2_gain, gate_weight, up_weight, down_weight, output_cotangent,
):
    slots, piece, model = tokens.shape
    length = piece * lax.axis_size("seq")
    wide = lax.axis_size("dp") // BLOCKS
    s = lax.axis_index("seq")
    place = lax.axis_index("dp")
    y, c = s // 2, s % 2
    d = place // wide
    z, x_at = d // 2, d % 2
    info = jnp.stack([y, c, d, z, x_at]).astype(jnp.int32)
    even = (z & 1) ^ c

    def pregather(shard):
        step = 1
        while step < wide:
            other = flip(shard, "dp", step)
            bit = (place // step) % 2
            shard = pick(
                bit, jnp.concatenate([other, shard]), jnp.concatenate([shard, other]))
            step *= 2
        return shard

    def postscatter(total):
        step = wide // 2
        while step >= 1:
            half = total.shape[0] // 2
            bit = (place // step) % 2
            lo, hi = total[:half], total[half:]
            total = pick(bit, hi, lo) + flip(pick(bit, lo, hi), "dp", step)
            step //= 2
        return total

    zm, z1, xf = (("dp", mask * wide) for mask in (ZM, Z1, X1))
    yf, cf = ("seq", MESH_Y), ("seq", MESH_C)
    y_last, x_last = (zm, z1, xf, yf), (zm, z1, yf, xf)

    def swap_slots(block):
        keep, send = pick(y, block[1], block[0]), pick(y, block[0], block[1])
        recv = flip(send, *yf)
        return pick(y, jnp.stack([recv, keep]), jnp.stack([keep, recv]))

    def join_cores(half):
        other = flip(half, *cf)
        return pick(c, jnp.stack([other, half], 1), jnp.stack([half, other], 1))

    x_full = join_cores(swap_slots(tokens)).reshape(length, model)

    gains = jnp.pad(
        jnp.concatenate([pregather(norm1_gain), pregather(norm2_gain)])[None], ((0, 15), (0, 0)))
    attn = jnp.concatenate(
        [pregather(query_weight), pregather(key_weight), pregather(value_weight), gains])
    cut = 208
    a10, a11 = gathered(attn[:cut], y_last)
    a20, a21 = gathered(attn[cut:], x_last)
    rows = jnp.concatenate([pregather(out_weight), pregather(down_weight)])
    od0, od1 = gathered(rows, y_last)
    ffn = jnp.concatenate([pregather(gate_weight).T, pregather(up_weight).T], axis=1)
    g0, g1 = gathered(ffn, x_last)

    def for_core(od):
        od = od.reshape(2, 2, 2, *od.shape[1:])
        spread = [[pick(even, od[:, t, t], od[:, t, 1 - t])] for t in range(2)]
        return jnp.concatenate([jnp.stack(part, 1) for part in spread], axis=1)

    odx = flip(jnp.stack([for_core(od0), for_core(od1)]), *cf)

    pair = jnp.stack([first_values, output_cotangent], axis=1)
    pair = join_cores(swap_slots(pair))
    fv_full = pair[:, :, 0].reshape(length, model)
    live = (y < seq_counts[0]).astype(BF16)
    gy_full = pair[:, :, 1].reshape(length, model) * live

    half = HEAD // 2
    frequency = 10000.0 ** (-(jnp.arange(half).astype(F32) * 2.0) / HEAD)
    angles = jnp.arange(length).astype(F32)[:, None] * frequency[None, :]
    cosine = jnp.tile(jnp.cos(angles), (1, 4))
    sine = jnp.tile(jnp.concatenate([-jnp.sin(angles), jnp.sin(angles)], axis=1), (1, 2))

    local = model // 2
    width = local // 2
    units = gate_weight.shape[1]
    rows_all = attn.shape[0]
    h1, q, k, b = call(
        qkv_body,
        [((length, model), BF16)] + [((length, local), BF16)] * 3,
        [("s", info), ("v", x_full), ("v", fv_full), ("v", cosine), ("v", sine)]
        + [("a", part) for part in (a10, a11, a20, a21)],
        [pltpu.VMEM((2, BLOCKS, rows_all, width), BF16), pltpu.SemaphoreType.DMA((32,))],
        6 * length * model * local, 14 << 20,
    )
    head_specs = [pl.BlockSpec((length, 128), lambda i: (0, i))] * 3
    lse_spec = pl.BlockSpec((1, 2, length), lambda i: (i, 0, 0))
    pairs = local // 128
    att, lse = call(
        attend_body,
        [((length, local), BF16), ((pairs, 2, length), F32)],
        [("v", q), ("v", k), ("v", b)], [],
        4 * length * length * local, 4 << 20, length * length * pairs * 2,
        grid=(pairs,), in_specs=head_specs, out_specs=[head_specs[0], lse_spec],
    )
    weights_od = [("a", od0), ("a", od1), ("a", odx)]
    (part,) = call(
        out_body, [((length, model), BF16)],
        [("s", info), ("v", att)] + weights_od,
        [pltpu.VMEM((local, model), BF16), pltpu.SemaphoreType.DMA((16,))],
        2 * length * model * local, 5 << 20,
    )
    x32 = x_full.astype(F32)
    middle = x32 + (part.astype(F32) + flip(part, *cf).astype(F32))
    gain_rows = jnp.zeros((BLOCKS, 128), BF16)
    spots = [(bx, b1, bm) for bx in range(2) for b1 in range(2) for bm in range(2)]
    ranks = jnp.stack([place_of(info, *spot) for spot in spots])
    order = jnp.zeros((BLOCKS,), jnp.int32).at[ranks].set(jnp.arange(BLOCKS))
    gain_by_p = jnp.concatenate(
        [a20[:4, 400 - cut - 16, 128:256], a21[:4, 400 - cut - 16, 128:256]])
    gain2 = jnp.take(gain_by_p, order, axis=0).reshape(1, model).astype(F32)
    del gain_rows
    inverse2 = lax.rsqrt(jnp.mean(middle * middle, axis=-1, keepdims=True) + EPSILON)
    h2 = (middle * inverse2 * gain2).astype(BF16)

    tile = (2, piece, model)
    gh2, gux0, gux1, dkeep, dsend, rkeep, rsend = call(
        ffn_body,
        [((length, model), BF16), ((2, 4, units, 256), BF16), ((2, 4, units, 256), BF16),
         ((2, 2, 2, units // 2, 256), BF16), ((2, 2, 2, units // 2, 256), BF16),
         (tile, F32), (tile, BF16)],
        [("s", info), ("v", h2), ("v", gy_full), ("a", g0), ("a", g1)] + weights_od,
        [pltpu.VMEM((2 * units, model), BF16), pltpu.VMEM((units, model), BF16),
         pltpu.VMEM((2 * units, length), BF16), pltpu.VMEM((units, length), BF16),
         pltpu.VMEM((length, model), F32), pltpu.VMEM((length, model), F32),
         pltpu.SemaphoreType.DMA((24,))],
        36 * length * model * units, 40 << 20, 2 * length * units,
    )

    def own_tokens(full):
        cut_up = full.reshape(2, 2, piece, full.shape[-1])
        return pick(c, cut_up[:, 1], cut_up[:, 0])

    def to_owner(halves):
        keep, send = pick(y, halves[1], halves[0]), pick(y, halves[0], halves[1])
        recv = flip(send.astype(BF16), *yf).astype(halves.dtype)
        return pick(y, jnp.stack([recv, keep]), jnp.stack([keep, recv]))

    middle_own = own_tokens(middle)
    output = to_owner(
        (live.astype(F32) * (middle_own + (rkeep + flip(rsend, *cf).astype(F32)))).astype(BF16))

    def whole_rows(keep, send):
        recv = flip(send, *cf)
        cells = []
        for b1 in range(2):
            for bm in range(2):
                mine = even if b1 != bm else 1 - even
                cells.append(pick(mine, keep[:, :, b1], recv[:, :, b1]))
        full = jnp.stack(cells, axis=2)
        return full.reshape(2, BLOCKS, *full.shape[3:])

    down_full = whole_rows(dkeep, dsend)

    gy32 = gy_full.astype(F32)
    grad_h2 = gh2.astype(F32) + flip(gh2, *cf).astype(F32)
    scaled = grad_h2 * gain2
    grad_gain2 = jnp.sum(grad_h2 * middle * inverse2, axis=0, keepdims=True)
    grad_middle = (
        gy32 + inverse2 * scaled
        - middle * (inverse2 * inverse2 * inverse2)
        * jnp.mean(scaled * middle, axis=-1, keepdims=True))
    grad_branch = grad_middle.astype(BF16)
    datt, okeep, osend = call(
        out_back_body,
        [((length, local), BF16), ((2, 2, 2, 128, 256), BF16), ((2, 2, 2, 128, 256), BF16)],
        [("s", info), ("v", grad_branch), ("v", att)] + weights_od,
        [pltpu.VMEM((local, model), BF16), pltpu.SemaphoreType.DMA((16,))],
        4 * length * model * local, 6 << 20,
    )
    out_full = whole_rows(okeep, osend)
    table_spec = pl.BlockSpec((length, 128), lambda i: (0, 0))
    dq, dk, dv = call(
        attend_back_body,
        [((length, local), BF16)] * 3,
        [("v", q), ("v", k), ("v", b), ("v", datt), ("v", lse), ("v", cosine), ("v", sine)],
        [pltpu.VMEM((length, 128), F32), pltpu.VMEM((length, 128), F32)],
        10 * length * length * local, 8 << 20, length * length * pairs * 2,
        grid=(pairs,),
        in_specs=head_specs + [head_specs[0], lse_spec, table_spec, table_spec],
        out_specs=head_specs,
    )
    dv_cut = dv.reshape(2, 2, piece, local)
    dv_keep, dv_send = pick(c, dv_cut[:, 1], dv_cut[:, 0]), pick(c, dv_cut[:, 0], dv_cut[:, 1])
    dv_recv = flip(dv_send, *cf)
    blocks = []
    for column_y in range(2):
        for column_c in range(2):
            by = y ^ column_y
            mine = pick(by, dv_keep[..., width:], dv_keep[..., :width])
            theirs = pick(by, dv_recv[..., width:], dv_recv[..., :width])
            blocks.append(pick(c ^ column_c, theirs, mine))
    grad_first = to_owner(jnp.concatenate(blocks, axis=-1)).astype(F32)

    out0, out1, gkeep, gsend = call(
        qkv_back_body,
        [((BLOCKS, 528, width), BF16), ((BLOCKS, 528, width), BF16), (tile, F32), (tile, BF16)],
        [("s", info), ("v", dq), ("v", dk), ("v", dv), ("v", h1), ("v", x_full),
         ("v", grad_gain2), ("v", out_full[0]), ("v", out_full[1])]
        + [("a", part) for part in (a10, a11, a20, a21)],
        [pltpu.VMEM((2, BLOCKS, rows_all, width), BF16), pltpu.VMEM((8, model), F32),
         pltpu.SemaphoreType.DMA((32,))],
        12 * length * model * local, 20 << 20,
    )

    grad_h1 = gkeep + flip(gsend, *cf).astype(F32)
    x_own = own_tokens(x_full).astype(F32)
    gain_by_p1 = jnp.concatenate([a20[:4, 400 - cut - 16, :128], a21[:4, 400 - cut - 16, :128]])
    gain1 = jnp.take(gain_by_p1, order, axis=0).reshape(1, 1, model).astype(F32)
    inverse1 = lax.rsqrt(jnp.mean(x_own * x_own, axis=-1, keepdims=True) + EPSILON)
    scaled1 = grad_h1 * gain1
    grad_input = to_owner(
        own_tokens(grad_middle) + inverse1 * scaled1
        - x_own * (inverse1 * inverse1 * inverse1)
        * jnp.mean(scaled1 * x_own, axis=-1, keepdims=True))

    gu_send = gux1.reshape(8, units, 256)
    gu_keep = gux0.reshape(8, units, 256)
    gu_total = scattered(gu_send, gu_keep, (xf, yf, z1, zm))
    down_total = scattered(down_full[1], down_full[0], (yf, xf, z1, zm))
    attn_total = scattered(out1, out0, (yf, xf, z1, zm))
    gain_total = attn_total[384]
    gain_other = flip(jnp.broadcast_to(gain_total[None, :128], (8, 128)), *cf)[0]
    return (
        output,
        grad_input,
        grad_first,
        postscatter(gain_total[:128] + gain_other),
        postscatter(attn_total[:128]),
        postscatter(attn_total[128:256]),
        postscatter(attn_total[256:384]),
        postscatter(attn_total[400:]),
        postscatter(gain_total[128:]),
        postscatter(gu_total[:, :128].T),
        postscatter(gu_total[:, 128:].T),
        postscatter(down_total),
    )


def solution(mesh):
    cut = P("dp", "seq")
    flat = P("dp")
    whole = P("dp", "seq", None)
    return jax.shard_map(
        on_device,
        mesh=mesh,
        in_specs=(whole, whole, flat, flat, cut, cut, cut, cut, flat, cut, cut, cut, whole),
        out_specs=(whole, whole, whole, flat, cut, cut, cut, cut, flat, cut, cut, cut),
        check_vma=False,
    )
```

```python
import functools

import jax
import jax.numpy as jnp
from jax import lax
from jax.experimental import pallas as pl
from jax.experimental.pallas import tpu as pltpu
from jax.sharding import PartitionSpec as P

HEAD = 64
EPSILON = 1e-06
TILE = 256
BLOCKS = 8
F32 = jnp.float32
BF16 = jnp.bfloat16
VMEM_LIMIT = 56 * 1024 * 1024
MESH_Y, MESH_C = 2, 1
ZM, Z1, X1 = 6, 2, 1


def dot_nn(a, b):
    return lax.dot_general(a, b, (((1,), (0,)), ((), ())), preferred_element_type=F32)


def dot_nt(a, b):
    return lax.dot_general(a, b, (((1,), (1,)), ((), ())), preferred_element_type=F32)


def dot_tn(a, b):
    return lax.dot_general(a, b, (((0,), (0,)), ((), ())), preferred_element_type=F32)


def flip(value, axis, mask):
    pairs = [(i, i ^ mask) for i in range(lax.axis_size(axis))]
    return lax.ppermute(value, axis, pairs)


def pick(flag, when_one, when_zero):
    return jnp.where(flag == 1, when_one, when_zero)


def call(body, outs, ins, scratch, flops, moved, exps=0, grid=None, in_specs=None, out_specs=None):
    spaces = {"v": pltpu.VMEM, "s": pltpu.SMEM, "a": pl.ANY}
    if in_specs is None:
        in_specs = [pl.BlockSpec(memory_space=spaces[kind]) for kind, _ in ins]
        out_specs = [pl.BlockSpec(memory_space=pltpu.VMEM) for _ in outs]
    kwargs = {} if grid is None else {"grid": grid}
    return pl.pallas_call(
        body,
        out_shape=[jax.ShapeDtypeStruct(shape, kind) for shape, kind in outs],
        in_specs=in_specs,
        out_specs=out_specs,
        scratch_shapes=scratch,
        cost_estimate=pl.CostEstimate(flops=flops, bytes_accessed=moved, transcendentals=exps),
        compiler_params=pltpu.CompilerParams(vmem_limit_bytes=VMEM_LIMIT),
        **kwargs,
    )(*[value for _, value in ins])


def run_copies(copies):
    for copy in copies:
        copy.start()
    for copy in copies:
        copy.wait()


def turned(values, cosine, signed_sine):
    lane = lax.broadcasted_iota(jnp.int32, values.shape, 1)
    ahead = pltpu.roll(values, 128 - HEAD // 2, 1)
    behind = pltpu.roll(values, HEAD // 2, 1)
    partner = jnp.where(lane % HEAD < HEAD // 2, ahead, behind)
    return values * cosine + partner * signed_sine


def place_of(info, bx, b1, bm):
    z = info[3] ^ b1 ^ (3 * bm)
    return z * 2 + (info[4] ^ bx)


def bits(count):
    return [tuple((i >> (count - 1 - j)) & 1 for j in range(count)) for i in range(1 << count)]


def attn_copies(info, a10, a11, a20, a21, w, sem):
    cut = a10.shape[1]
    rest = w.shape[2] - cut
    copies = []
    for by, bx, b1, bm in bits(4):
        d = place_of(info, bx, b1, bm)
        copies.append(pltpu.make_async_copy(
            (a10, a11)[by].at[bx * 4 + b1 * 2 + bm], w.at[by, d, pl.ds(0, cut)],
            sem.at[len(copies)]))
        copies.append(pltpu.make_async_copy(
            (a20, a21)[bx].at[by * 4 + b1 * 2 + bm, pl.ds(0, rest)],
            w.at[by, d, pl.ds(cut, rest)], sem.at[len(copies)]))
    return copies


def qkv_body(info, x, fv, cosine, sine, a10, a11, a20, a21, h1, q, k, b, w, sem):
    run_copies(attn_copies(info, a10, a11, a20, a21, w, sem))
    rows = 128
    width = w.shape[3]
    model = x.shape[1]
    gains = w[0, :, 3 * rows : 3 * rows + 16, 0:rows]
    gain = jnp.concatenate([gains[d, 0:1, :] for d in range(BLOCKS)], axis=1).astype(F32)

    def step(t, carry):
        at = pl.ds(pl.multiple_of(t * TILE, TILE), TILE)
        xt = x[at, :].astype(F32)
        inverse = lax.rsqrt(jnp.mean(xt * xt, axis=-1, keepdims=True) + EPSILON)
        h = (xt * inverse * gain).astype(BF16)
        h1[at, :] = h
        cos_t, sin_t = cosine[at, :], sine[at, :]
        for by in range(2):
            for n in range(3):
                weight = w[by, :, n * rows : (n + 1) * rows, :].reshape(model, width)
                acc = dot_nn(h, weight)
                cols = pl.ds(by * width, width)
                if n == 2:
                    column = pl.multiple_of(((info[0] ^ by) * 2 + info[1]) * width, width)
                    first = fv[at, pl.ds(column, width)].astype(F32)
                    b[at, cols] = (0.5 * acc + 0.5 * first).astype(BF16)
                else:
                    parts = [
                        turned(acc[:, j : j + 128], cos_t, sin_t) for j in range(0, width, 128)
                    ]
                    (q, k)[n][at, cols] = jnp.concatenate(parts, axis=1).astype(BF16)
        return carry

    lax.fori_loop(0, x.shape[0] // TILE, step, 0)


def split_heads(pair):
    lane = lax.broadcasted_iota(jnp.int32, pair.shape, 1)
    zero = jnp.zeros_like(pair)
    return jnp.concatenate(
        [jnp.where(lane < HEAD, pair, zero), jnp.where(lane < HEAD, zero, pair)], axis=0
    )


def join_heads(both):
    half = both.shape[0] // 2
    lane = lax.broadcasted_iota(jnp.int32, (half, both.shape[1]), 1)
    return jnp.where(lane < HEAD, both[:half], both[half:])


def hide_later(scores, fill):
    length, width = scores.shape
    key_at = lax.broadcasted_iota(jnp.int32, (TILE, width), 0)
    query_at = lax.broadcasted_iota(jnp.int32, (TILE, width), 1) % TILE
    last = jnp.where(key_at <= query_at, scores[length - TILE :], fill)
    if length == TILE:
        return last
    return jnp.concatenate([scores[: length - TILE], last], axis=0)


def attend_body(q, k, b, att, lse):
    for i in range(q.shape[0] // TILE):
        length = (i + 1) * TILE
        queries = split_heads(q[i * TILE : length, :])
        scores = hide_later(dot_nt(k[:length, :], queries) * 0.125, -1e30)
        top = jnp.max(scores, axis=0, keepdims=True)
        grown = jnp.exp(scores - top)
        total = jnp.sum(grown, axis=0, keepdims=True)
        logs = top + jnp.log(total)
        probs = (grown * (1.0 / total)).astype(BF16)
        att[i * TILE : length, :] = join_heads(dot_tn(probs, b[:length, :])).astype(BF16)
        lse[0, 0:1, i * TILE : length] = logs[:, :TILE]
        lse[0, 1:2, i * TILE : length] = logs[:, TILE:]


def attend_back_body(q, k, b, datt, lse, cosine, sine, dq, dk, dv, k_acc, v_acc):
    k_acc[...] = jnp.zeros_like(k_acc)
    v_acc[...] = jnp.zeros_like(v_acc)
    for i in range(q.shape[0] // TILE):
        length = (i + 1) * TILE
        at = slice(i * TILE, length)
        queries = split_heads(q[at, :])
        grads = split_heads(datt[at, :])
        keys = k[:length, :]
        logs = jnp.concatenate([lse[0, 0:1, at], lse[0, 1:2, at]], axis=1)
        scores = dot_nt(keys, queries) * 0.125
        probs = jnp.exp(hide_later(scores - logs, -1e30))
        grad_probs = dot_nt(b[:length, :], grads)
        delta = jnp.sum(probs * grad_probs, axis=0, keepdims=True)
        grad_scores = (probs * (grad_probs - delta)).astype(BF16)
        v_acc[:length, :] += dot_nn(probs.astype(BF16), grads)
        k_acc[:length, :] += dot_nn(grad_scores, queries)
        turned_back = turned(
            0.125 * join_heads(dot_tn(grad_scores, keys)), cosine[at, :], -sine[at, :]
        )
        dq[at, :] = turned_back.astype(BF16)
    for i in range(q.shape[0] // TILE):
        at = slice(i * TILE, (i + 1) * TILE)
        dk[at, :] = turned(0.125 * k_acc[at, :], cosine[at, :], -sine[at, :]).astype(BF16)
        dv[at, :] = (0.5 * v_acc[at, :]).astype(BF16)


def row_spot(info, hidden_block):
    even = (info[3] & 1) ^ info[1]
    t = hidden_block ^ info[0] ^ (info[3] >> 1) ^ even
    return t, t ^ even


def column_of(info, by, other):
    block = (info[0] ^ by) * 2 + (info[1] ^ other)
    return pl.multiple_of(block * 256, 256)


def out_copies(info, a20, a21, ox, wo, sem):
    first = a20.shape[1] - 128
    copies = []
    for block, by, bx in bits(3):
        t, bm = row_spot(info, block)
        row = pl.multiple_of(block * 256 + (info[4] ^ bx) * 128, 128)
        for other in range(2):
            if other:
                source = ox.at[bx, by, t]
            else:
                source = (a20, a21)[bx].at[by * 4 + t * 2 + bm, pl.ds(first, 128)]
            copies.append(pltpu.make_async_copy(
                source, wo.at[pl.ds(row, 128), pl.ds(column_of(info, by, other), 256)],
                sem.at[len(copies)]))
    return copies


def out_body(info, att, a20, a21, ox, part, wo, sem):
    run_copies(out_copies(info, a20, a21, ox, wo, sem))

    def step(t, carry):
        at = pl.ds(pl.multiple_of(t * TILE, TILE), TILE)
        part[at, :] = dot_nn(att[at, :], wo[...]).astype(BF16)
        return carry

    lax.fori_loop(0, att.shape[0] // TILE, step, 0)


def out_back_body(info, gb, att, a20, a21, ox, datt, grads, wo, sem):
    copies = out_copies(info, a20, a21, ox, wo, sem)
    for copy in copies:
        copy.start()
    for by, other in bits(2):
        grad = dot_tn(att[...], gb[:, pl.ds(column_of(info, by, other), 256)]).astype(BF16)
        for block in range(2):
            t, _ = row_spot(info, block)
            row = [grad[block * 256 + j * 128 : block * 256 + (j + 1) * 128] for j in (0, 1)]
            for bx in range(2):
                grads[by, bx, other, t] = jnp.where((info[4] ^ bx) == 1, row[1], row[0])
    for copy in copies:
        copy.wait()

    def step(t, carry):
        at = pl.ds(pl.multiple_of(t * TILE, TILE), TILE)
        datt[at, :] = dot_nt(gb[at, :], wo[...]).astype(BF16)
        return carry

    lax.fori_loop(0, att.shape[0] // TILE, step, 0)


def ffn_copies(info, p10, p11, p20, p21, wgu, wd, sem):
    units = wd.shape[0]
    own = units // 2
    part = own // 2
    cut = p10.shape[1]
    copies = []
    for by, bx, b1, bm in bits(4):
        lane = pl.multiple_of(place_of(info, bx, b1, bm) * 128, 128)
        first = (p10, p11)[by].at[bx * 4 + b1 * 2 + bm]
        second = (p20, p21)[bx].at[by * 4 + b1 * 2 + bm]
        for up in range(2):
            lanes = pl.ds(up * 128, 128)
            row = up * units + by * own
            copies.append(pltpu.make_async_copy(
                first.at[:, lanes], wgu.at[pl.ds(row, cut), pl.ds(lane, 128)],
                sem.at[len(copies)]))
            copies.append(pltpu.make_async_copy(
                second.at[pl.ds(0, own - cut), lanes],
                wgu.at[pl.ds(row + cut, own - cut), pl.ds(lane, 128)], sem.at[len(copies)]))
    for block, by, bx in bits(3):
        t, _ = row_spot(info, block)
        row = pl.multiple_of(block * own + (info[4] ^ bx) * part, 16)
        for other in range(2):
            source = (p20, p21)[bx].at[by * 4 + other * 2 + t, pl.ds(own - cut, part)]
            copies.append(pltpu.make_async_copy(
                source, wd.at[pl.ds(row, part), pl.ds(column_of(info, by, other), 256)],
                sem.at[len(copies)]))
    return copies


def ffn_body(last, *refs):
    info, h2, gy, p10, p11, p20, p21 = refs[:7]
    refs = refs[7:]
    if last:
        gh2_in, res_in, gh2, rkeep, rsend = refs[:5]
        refs = refs[5:]
    else:
        gh2, res = refs[:2]
        refs = refs[2:]
    y_send, y_keep, x_send, x_keep, wgu, wd, ggu, hid, sem = refs
    run_copies(ffn_copies(info, p10, p11, p20, p21, wgu, wd, sem))
    units = wd.shape[0]
    own = units // 2
    part = own // 2
    cut = p10.shape[1]

    def step(t, carry):
        at = pl.ds(pl.multiple_of(t * TILE, TILE), TILE)
        both = dot_nt(wgu[...], h2[at, :])
        gate, up = both[:units], both[units:]
        sig = 1.0 / (1.0 + jnp.exp(-gate))
        act = gate * sig
        hidden = (act * up).astype(BF16)
        hid[:, at] = hidden
        grad_hidden = dot_nt(wd[...], gy[at, :])
        ggu[:units, at] = (grad_hidden * up * (sig + act * (1.0 - sig))).astype(BF16)
        ggu[units:, at] = (grad_hidden * act).astype(BF16)
        grad_h = dot_tn(ggu[:, at], wgu[...])
        result = dot_tn(hidden, wd[...])
        if not last:
            gh2[at, :] = grad_h
            res[at, :] = result
        else:
            gh2[at, :] = (gh2_in[at, :] + grad_h).astype(BF16)
            result = res_in[at, :] + result

            @pl.when((t & 1) == info[1])
            def _():
                rkeep[t >> 1] = result

            @pl.when((t & 1) != info[1])
            def _():
                rsend[t >> 1] = result.astype(BF16)

        return carry

    lax.fori_loop(0, h2.shape[0] // TILE, step, 0)

    swap = info[4] == 1
    for b1, bm in bits(2):
        z = info[3] ^ b1 ^ (3 * bm)
        q = b1 * 2 + bm
        column = pl.multiple_of(z * 256, 256)
        grad = dot_nn(ggu[...], h2[:, pl.ds(column, 256)]).astype(BF16)
        lo, hi = grad[:, :128], grad[:, 128:]
        for bx, side in ((0, jnp.where(swap, hi, lo)), (1, jnp.where(swap, lo, hi))):
            for by, up in bits(2):
                lanes = slice(up * 128, up * 128 + 128)
                piece = side[up * units + by * own : up * units + (by + 1) * own]
                (y_keep, y_send)[by][bx * 4 + q, :, lanes] = piece[:cut]
                (x_keep, x_send)[bx][by * 4 + q, 0 : own - cut, lanes] = piece[cut:]
    for by, other in bits(2):
        grad = dot_nn(hid[...], gy[:, pl.ds(column_of(info, by, other), 256)]).astype(BF16)
        for block in range(2):
            t, _ = row_spot(info, block)
            first, second = (
                grad[block * own + j * part : block * own + (j + 1) * part] for j in (0, 1))
            for bx in range(2):
                (x_keep, x_send)[bx][by * 4 + other * 2 + t, own - cut :, :] = jnp.where(
                    (info[4] ^ bx) == 1, second, first)


def qkv_back_body(
    info, dq, dk, dv, h1, x, gain2, og, a10, a11, a20, a21,
    y_send, y_keep, x_send, x_keep, gkeep, gsend, w, acc, sem,
):
    copies = attn_copies(info, a10, a11, a20, a21, w, sem)
    for copy in copies:
        copy.start()
    width = w.shape[3]
    model = x.shape[1]
    cut = y_send.shape[1]
    for by in (1, 0):
        cols = slice(by * width, (by + 1) * width)
        three = jnp.concatenate([dq[:, cols], dk[:, cols], dv[:, cols]], axis=1)
        for b1, bm in bits(2):
            z = info[3] ^ b1 ^ (3 * bm)
            q = b1 * 2 + bm
            grad = dot_tn(h1[:, pl.ds(pl.multiple_of(z * 256, 256), 256)], three).astype(BF16)
            for bx in range(2):
                part = jnp.where((info[4] ^ bx) == 1, grad[128:], grad[:128])
                to_y = (y_keep, y_send)[by]
                to_x = (x_keep, x_send)[bx]
                to_y[bx * 4 + q, 0:128, :] = part[:, :width]
                to_y[bx * 4 + q, 128:256, :] = part[:, width : 2 * width]
                to_y[bx * 4 + q, 256:cut, :] = part[: cut - 256, 2 * width :]
                to_x[by * 4 + q, 0 : 384 - cut, :] = part[cut - 256 :, 2 * width :]
                to_x[by * 4 + q, 400 - cut :, :] = og[by, bx, b1, bm]
    for copy in copies:
        copy.wait()
    acc[...] = jnp.zeros_like(acc)

    def step(t, carry):
        at = pl.ds(pl.multiple_of(t * TILE, TILE), TILE)
        grad_h = jnp.zeros((TILE, model), F32)
        for by in range(2):
            cols = slice(by * width, (by + 1) * width)
            for n, grad in enumerate((dq, dk, dv)):
                weight = w[by, :, n * 128 : (n + 1) * 128, :].reshape(model, width)
                grad_h = grad_h + dot_nt(grad[at, cols], weight)
        xt = x[at, :].astype(F32)
        inverse = lax.rsqrt(jnp.mean(xt * xt, axis=-1, keepdims=True) + EPSILON)
        acc[0:1, :] += jnp.sum(grad_h * xt * inverse, axis=0, keepdims=True)

        @pl.when((t & 1) == info[1])
        def _():
            gkeep[t >> 1] = grad_h

        @pl.when((t & 1) != info[1])
        def _():
            gsend[t >> 1] = grad_h.astype(BF16)

        return carry

    lax.fori_loop(0, x.shape[0] // TILE, step, 0)
    for bx, b1, bm in bits(3):
        d = place_of(info, bx, b1, bm)
        spot = pl.ds(pl.multiple_of(d * 128, 128), 128)
        row = jnp.concatenate([acc[0:1, spot], gain2[0:1, spot]], axis=1)
        full = jnp.broadcast_to(row, (16, 256)).astype(BF16)
        for by in range(2):
            (x_keep, x_send)[bx][by * 4 + b1 * 2 + bm, 384 - cut : 400 - cut, :] = full


def in_step(*values):
    return lax.optimization_barrier(values)


def grow(held, recv):
    return jnp.concatenate([held, recv], axis=0)


def plus(keep, recv):
    return keep.astype(F32) + recv.astype(F32)


def on_device(
    tokens, first_values, seq_counts, norm1_gain, query_weight, key_weight, value_weight,
    out_weight, norm2_gain, gate_weight, up_weight, down_weight, output_cotangent,
):
    slots, piece, model = tokens.shape
    length = piece * lax.axis_size("seq")
    wide = lax.axis_size("dp") // BLOCKS
    s = lax.axis_index("seq")
    place = lax.axis_index("dp")
    y, c = s // 2, s % 2
    d = place // wide
    z, x_at = d // 2, d % 2
    info = jnp.stack([y, c, d, z, x_at]).astype(jnp.int32)
    even = (z & 1) ^ c

    def pregather(shard):
        step = 1
        while step < wide:
            other = flip(shard, "dp", step)
            bit = (place // step) % 2
            shard = pick(
                bit, jnp.concatenate([other, shard]), jnp.concatenate([shard, other]))
            step *= 2
        return shard

    def postscatter(total):
        step = wide // 2
        while step >= 1:
            half = total.shape[0] // 2
            bit = (place // step) % 2
            lo, hi = total[:half], total[half:]
            total = pick(bit, hi, lo) + flip(pick(bit, lo, hi), "dp", step)
            step //= 2
        return total

    def far(v):
        return flip(v, "dp", ZM * wide)

    def near(v):
        return flip(v, "dp", Z1 * wide)

    def over_x(v):
        return flip(v, "dp", X1 * wide)

    def over_y(v):
        return flip(v, "seq", MESH_Y)

    def over_core(v):
        return flip(v, "seq", MESH_C)

    def slot_parts(block):
        return pick(y, block[1], block[0]), pick(y, block[0], block[1])

    def both_slots(keep, recv):
        return pick(y, jnp.stack([recv, keep]), jnp.stack([keep, recv]))

    def both_cores(half, other):
        joined = pick(c, jnp.stack([other, half], 1), jnp.stack([half, other], 1))
        return joined.reshape(length, model)

    def for_partner(rows):
        return jnp.stack([pick(even, rows[:, t * 3], rows[:, t * 2 + 1 - t]) for t in range(2)], 1)

    def mine_of(rows):
        return jnp.stack([pick(even, rows[t * 2 + 1 - t], rows[t * 3]) for t in range(2)])

    def theirs_of(rows):
        return jnp.stack([pick(even, rows[t * 3], rows[t * 2 + 1 - t]) for t in range(2)])

    gains = jnp.pad(
        jnp.concatenate([pregather(norm1_gain), pregather(norm2_gain)])[None], ((0, 15), (0, 0)))
    attn = jnp.concatenate(
        [pregather(query_weight), pregather(key_weight), pregather(value_weight), gains,
         pregather(out_weight)])[None]
    down = pregather(down_weight)
    ffn = jnp.concatenate([pregather(gate_weight).T, pregather(up_weight).T], axis=1)
    units = ffn.shape[0]
    part = units // 4
    groups = [
        jnp.concatenate(
            [ffn[i * part : (i + 1) * part], ffn[(i + 2) * part : (i + 3) * part],
             down[i * part : (i + 1) * part]])[None]
        for i in range(2)
    ]
    own = 2 * part
    cut_a, cut_g = 240, 256

    t_keep, t_send = slot_parts(tokens)
    f_keep, f_send = slot_parts(first_values)
    c_keep, c_send = slot_parts(output_cotangent)
    attn, a_recv, t_keep, t_recv, f_keep, f_send, ga, gb, c_send, c_keep = in_step(
        attn, far(attn), t_keep, over_y(t_send), f_keep, f_send, *groups, c_send, c_keep)
    attn = grow(attn, a_recv)
    t_half = both_slots(t_keep, t_recv)
    attn, a_recv, t_half, t_other, f_keep, f_recv, ga, gb, c_send, c_keep = in_step(
        attn, near(attn), t_half, over_core(t_half), f_keep, over_y(f_send), ga, gb,
        c_send, c_keep)
    a1 = grow(attn[:, :cut_a], a_recv[:, :cut_a])
    a2 = grow(attn[:, cut_a:], a_recv[:, cut_a:])
    x_full = both_cores(t_half, t_other)
    f_half = both_slots(f_keep, f_recv)
    half = HEAD // 2
    frequency = 10000.0 ** (-(jnp.arange(half).astype(F32) * 2.0) / HEAD)
    angles = jnp.arange(length).astype(F32)[:, None] * frequency[None, :]
    cosine = jnp.tile(jnp.cos(angles), (1, 4))
    sine = jnp.tile(jnp.concatenate([-jnp.sin(angles), jnp.sin(angles)], axis=1), (1, 2))
    a1, a1_recv, a2, a2_recv, ga, ga_recv, gb, f_half, f_other, x_full, cosine, sine, c_send, c_keep = (
        in_step(a1, over_x(a1), a2, over_y(a2), ga, far(ga), gb, f_half, over_core(f_half), x_full,
                cosine, sine, c_send, c_keep))
    a10, a20 = grow(a1, a1_recv), grow(a2, a2_recv)
    ga = grow(ga, ga_recv)
    fv_full = both_cores(f_half, f_other)
    a10, a11, a20, a21, ga, ga_recv, gb, gb_recv, x_full, fv_full, c_send, c_keep = in_step(
        a10, over_y(a10), a20, over_x(a20), ga, near(ga), gb, far(gb), x_full, fv_full,
        c_send, c_keep)

    def core_rows(held):
        rows = held[:, own:]
        return jnp.concatenate([mine_of(rows), over_core(theirs_of(rows))])

    def halves(held, rows):
        top = held[:, :cut_g]
        return top, jnp.concatenate([held[:, cut_g:own], rows], axis=1)

    local = model // 2
    width = local // 2
    attn_rows = 3 * 128 + 16
    attn_parts = [("a", value) for value in (a10, a11, a20, a21)]
    h1, q, k, b = call(
        qkv_body,
        [((length, model), BF16)] + [((length, local), BF16)] * 3,
        [("s", info), ("v", x_full), ("v", fv_full), ("v", cosine), ("v", sine)] + attn_parts,
        [pltpu.VMEM((2, BLOCKS, attn_rows, width), BF16), pltpu.SemaphoreType.DMA((32,))],
        6 * length * model * local, 14 << 20,
    )
    gb = grow(gb, gb_recv)
    gb_recv = near(gb)
    ga = grow(ga, ga_recv)
    ga1, ga2 = halves(ga, core_rows(ga))
    o_rows = jnp.stack([a20, a21])[:, :, a20.shape[1] - 128 :].reshape(4, 4, 128, 256)
    o_send = for_partner(o_rows).reshape(2, 2, 2, 128, 256)
    h1, q, k, b, ga1, ga1_recv, ga2, ga2_recv, gb, gb_recv, ox, c_send, c_keep = in_step(
        h1, q, k, b, ga1, over_x(ga1), ga2, over_y(ga2), gb, gb_recv, over_core(o_send),
        c_send, c_keep)
    head_specs = [pl.BlockSpec((length, 128), lambda i: (0, i))] * 3
    lse_spec = pl.BlockSpec((1, 2, length), lambda i: (i, 0, 0))
    pairs = local // 128
    ga1, ga2 = grow(ga1, ga1_recv), grow(ga2, ga2_recv)
    gb = grow(gb, gb_recv)
    gb1, gb2 = halves(gb, core_rows(gb))
    att, lse = call(
        attend_body,
        [((length, local), BF16), ((pairs, 2, length), F32)],
        [("v", q), ("v", k), ("v", b)], [],
        4 * length * length * local, 4 << 20, length * length * pairs * 2,
        grid=(pairs,), in_specs=head_specs, out_specs=[head_specs[0], lse_spec],
    )
    att, lse, ga1, ga1_recv, ga2, ga2_recv, gb1, gb2, c_send, c_keep = in_step(
        att, lse, ga1, over_y(ga1), ga2, over_x(ga2), gb1, gb2, c_send, c_keep)
    out_parts = [("a", a20), ("a", a21), ("a", ox)]
    (partial,) = call(
        out_body, [((length, model), BF16)],
        [("s", info), ("v", att)] + out_parts,
        [pltpu.VMEM((local, model), BF16), pltpu.SemaphoreType.DMA((16,))],
        2 * length * model * local, 5 << 20,
    )
    x32 = x_full.astype(F32)
    middle = x32 + plus(partial, over_core(partial))
    ranks = jnp.stack([place_of(info, *spot) for spot in bits(3)])
    order = jnp.zeros((BLOCKS,), jnp.int32).at[ranks].set(jnp.arange(BLOCKS))
    gain_row = 384 - cut_a
    gain_by_p = jnp.concatenate([a20[:4, gain_row], a21[:4, gain_row]])
    gain_rows = jnp.take(gain_by_p, order, axis=0).astype(F32)
    gain1 = gain_rows[:, :128].reshape(1, 1, model)
    gain2 = gain_rows[:, 128:].reshape(1, model)
    inverse2 = lax.rsqrt(jnp.mean(middle * middle, axis=-1, keepdims=True) + EPSILON)
    h2 = (middle * inverse2 * gain2).astype(BF16)
    c_half = both_slots(c_keep, over_y(c_send))
    live = (y < seq_counts[0]).astype(BF16)
    gy_full = both_cores(c_half, over_core(c_half)) * live
    h2, middle, inverse2, gy_full, gb1, gb1_recv, gb2, gb2_recv = in_step(
        h2, middle, inverse2, gy_full, gb1, over_x(gb1), gb2, over_y(gb2))
    gb1, gb2 = grow(gb1, gb1_recv), grow(gb2, gb2_recv)
    tile = (2, piece, model)
    grad_outs = [((BLOCKS, cut_g, 256), BF16)] * 2 + [((BLOCKS, 3 * part - cut_g, 256), BF16)] * 2

    def ffn_call(last, parts, extra, outs):
        return call(
            functools.partial(ffn_body, last), outs + grad_outs,
            [("s", info), ("v", h2), ("v", gy_full)] + [("a", value) for value in parts] + extra,
            [pltpu.VMEM((2 * units, model), BF16), pltpu.VMEM((units, model), BF16),
             pltpu.VMEM((2 * units, length), BF16), pltpu.VMEM((units, length), BF16),
             pltpu.SemaphoreType.DMA((80,))],
            18 * length * model * units, 24 << 20, length * units,
        )

    gh2_a, res_a, ays, ayk, axs, axk = ffn_call(
        False, (ga1, ga1_recv, ga2, ga2_recv), [], [((length, model), F32)] * 2)
    gh2_a, res_a, ays, ayk, axs, axk, gb1, gb1_recv, gb2, gb2_recv = in_step(
        gh2_a, res_a, ays, ayk, axs, axk, gb1, over_y(gb1), gb2, over_x(gb2))
    gh2, rkeep, rsend, bys, byk, bxs, bxk = ffn_call(
        True, (gb1, gb1_recv, gb2, gb2_recv), [("v", gh2_a), ("v", res_a)],
        [((length, model), BF16), (tile, F32), (tile, BF16)])
    gh2, rkeep, rsend, bys, byk, bxs, bxk, ay, ax, ayk, axk = in_step(
        gh2, rkeep, rsend, bys, byk, bxs, bxk, over_y(ays), over_x(axs), ayk, axk)

    def own_tokens(full):
        cut_up = full.reshape(2, 2, piece, full.shape[-1])
        return pick(c, cut_up[:, 1], cut_up[:, 0])

    def to_owner(halves_of):
        keep, send = slot_parts(halves_of)
        return keep, send.astype(BF16)

    def fold(keep, recv):
        total = plus(keep, recv)
        return total[:4], total[4:].astype(BF16)

    gy32 = gy_full.astype(F32)
    grad_h2 = plus(gh2, over_core(gh2))
    scaled = grad_h2 * gain2
    grad_gain2 = jnp.sum(grad_h2 * middle * inverse2, axis=0, keepdims=True)
    grad_middle = (
        gy32 + inverse2 * scaled
        - middle * (inverse2 * inverse2 * inverse2)
        * jnp.mean(scaled * middle, axis=-1, keepdims=True))
    grad_branch = grad_middle.astype(BF16)
    datt, og = call(
        out_back_body,
        [((length, local), BF16), ((2, 2, 2, 2, 128, 256), BF16)],
        [("s", info), ("v", grad_branch), ("v", att)] + out_parts,
        [pltpu.VMEM((local, model), BF16), pltpu.SemaphoreType.DMA((16,))],
        4 * length * model * local, 6 << 20,
    )
    ayk, ays = fold(ayk, ay)
    axk, axs = fold(axk, ax)
    r_recv = over_core(rsend)
    datt, og, grad_middle, by, bx, byk, bxk, ayk, ays, axk, axs, r_recv, rkeep = in_step(
        datt, og, grad_middle, over_y(bys), over_x(bxs), byk, bxk, ayk, ays, axk, axs,
        r_recv, rkeep)
    o_keep, o_send = to_owner(
        (live.astype(F32) * (own_tokens(middle) + plus(rkeep, r_recv))).astype(BF16))
    table_spec = pl.BlockSpec((length, 128), lambda i: (0, 0))
    dq, dk, dv = call(
        attend_back_body,
        [((length, local), BF16)] * 3,
        [("v", q), ("v", k), ("v", b), ("v", datt), ("v", lse), ("v", cosine), ("v", sine)],
        [pltpu.VMEM((length, 128), F32), pltpu.VMEM((length, 128), F32)],
        10 * length * length * local, 8 << 20, length * length * pairs * 2,
        grid=(pairs,),
        in_specs=head_specs + [head_specs[0], lse_spec, table_spec, table_spec],
        out_specs=head_specs,
    )
    byk, bys = fold(byk, by)
    bxk, bxs = fold(bxk, bx)
    dq, dk, dv, ay, ax, ayk, axk, byk, bys, bxk, bxs, o_keep, o_recv = in_step(
        dq, dk, dv, over_x(ays), over_y(axs), ayk, axk, byk, bys, bxk, bxs, o_keep,
        over_y(o_send))
    output = both_slots(o_keep, o_recv)

    def row_total(y_keep, y_recv, x_keep, x_recv):
        total = jnp.concatenate([plus(y_keep, y_recv), plus(x_keep, x_recv)], axis=1)
        return total

    def spread(rows, recv):
        cells = []
        for b1, bm in bits(2):
            mine = even if b1 != bm else 1 - even
            cells.append(pick(mine, rows[b1], recv[b1]))
        return jnp.stack(cells)

    def ffn_fold(total):
        recv = over_core(total[2:, own:].astype(BF16)).astype(F32)
        full = jnp.concatenate([total[:, :own], spread(total[:2, own:], recv)], axis=1)
        return full[:2], full[2:].astype(BF16)

    az_keep, az_send = ffn_fold(row_total(ayk, ay, axk, ax))
    cut_r = 272
    ays2, ayk2, axs2, axk2, gkeep, gsend = call(
        qkv_back_body,
        [((BLOCKS, cut_r, width), BF16)] * 2 + [((BLOCKS, 528 - cut_r, width), BF16)] * 2
        + [(tile, F32), (tile, BF16)],
        [("s", info), ("v", dq), ("v", dk), ("v", dv), ("v", h1), ("v", x_full),
         ("v", grad_gain2), ("v", og)] + attn_parts,
        [pltpu.VMEM((2, BLOCKS, attn_rows, width), BF16), pltpu.VMEM((8, model), F32),
         pltpu.SemaphoreType.DMA((32,))],
        12 * length * model * local, 20 << 20,
    )
    dv_cut = dv.reshape(2, 2, piece, local)
    dv_keep, dv_send = pick(c, dv_cut[:, 1], dv_cut[:, 0]), pick(c, dv_cut[:, 0], dv_cut[:, 1])
    ays2, ayk2, axs2, axk2, gkeep, gsend, by, bx, byk, bxk, az_keep, az, dv_keep, dv_recv = in_step(
        ays2, ayk2, axs2, axk2, gkeep, gsend, over_x(bys), over_y(bxs), byk, bxk, az_keep,
        near(az_send), dv_keep, over_core(dv_send))
    bz_keep, bz_send = ffn_fold(row_total(byk, by, bxk, bx))
    az = plus(az_keep, az)
    az_keep, az_send = az[0], az[1].astype(BF16)
    grad_h1 = plus(gkeep, over_core(gsend))
    x_own = own_tokens(x_full).astype(F32)
    inverse1 = lax.rsqrt(jnp.mean(x_own * x_own, axis=-1, keepdims=True) + EPSILON)
    scaled1 = grad_h1 * gain1
    i_keep, i_send = to_owner(
        own_tokens(grad_middle) + inverse1 * scaled1
        - x_own * (inverse1 * inverse1 * inverse1)
        * jnp.mean(scaled1 * x_own, axis=-1, keepdims=True))
    blocks = []
    for column_y, column_c in bits(2):
        by_side = y ^ column_y
        mine = pick(by_side, dv_keep[..., width:], dv_keep[..., :width])
        theirs = pick(by_side, dv_recv[..., width:], dv_recv[..., :width])
        blocks.append(pick(c ^ column_c, theirs, mine))
    v_keep, v_send = to_owner(jnp.concatenate(blocks, axis=-1))
    ay, ax, ayk2, axk2, bz_keep, bz, az_keep, az, i_keep, i_send, v_keep, v_send = in_step(
        over_y(ays2), over_x(axs2), ayk2, axk2, bz_keep, near(bz_send), az_keep, far(az_send),
        i_keep, i_send, v_keep, v_send)
    total_a = plus(az_keep, az)
    bz = plus(bz_keep, bz)
    bz_keep, bz_send = bz[0], bz[1].astype(BF16)
    ayk, ays = fold(ayk2, ay)
    axk, axs = fold(axk2, ax)
    ay, ax, ayk, axk, bz_keep, bz, i_send, v_send = in_step(
        over_x(ays), over_y(axs), ayk, axk, bz_keep, far(bz_send), i_send, v_send)
    total_b = plus(bz_keep, bz)
    total = row_total(ayk, ay, axk, ax)
    message = jnp.concatenate([total[2:, 400:], total[:, 384:400].reshape(2, 32, 256)], axis=1)
    recv = over_core(message.astype(BF16)).astype(F32)
    sums = total[:, 384:400]
    sums = jnp.concatenate(
        [sums[..., :128] + recv[:, 128:].reshape(4, 16, 256)[..., :128], sums[..., 128:]], axis=-1)
    total = jnp.concatenate(
        [total[:, :384], sums, spread(total[:2, 400:], recv[:, :128])], axis=1)
    total_keep, total_send = total[:2], total[2:].astype(BF16)
    total_keep, recv, i_recv, v_send = in_step(
        total_keep, near(total_send), over_y(i_send), v_send)
    total = plus(total_keep, recv)
    total = plus(total[0], far(total[1].astype(BF16)))
    grad_input = both_slots(i_keep, i_recv.astype(F32))
    grad_first = both_slots(v_keep, over_y(v_send)).astype(F32)

    def weave(lanes):
        pieces = [total_a[:part, lanes], total_b[:part, lanes],
                  total_a[part:own, lanes], total_b[part:own, lanes]]
        return jnp.concatenate(pieces).T

    return (
        output,
        grad_input,
        grad_first,
        postscatter(total[384, :128]),
        postscatter(total[:128]),
        postscatter(total[128:256]),
        postscatter(total[256:384]),
        postscatter(total[400:]),
        postscatter(total[384, 128:]),
        postscatter(weave(slice(0, 128))),
        postscatter(weave(slice(128, 256))),
        postscatter(jnp.concatenate([total_a[own:], total_b[own:]])),
    )


def solution(mesh):
    cut = P("dp", "seq")
    flat = P("dp")
    whole = P("dp", "seq", None)
    return jax.shard_map(
        on_device,
        mesh=mesh,
        in_specs=(whole, whole, flat, flat, cut, cut, cut, cut, flat, cut, cut, cut, whole),
        out_specs=(whole, whole, whole, flat, cut, cut, cut, cut, flat, cut, cut, cut),
        check_vma=False,
    )
```

```python
import functools

import jax
import jax.numpy as jnp
from jax import lax
from jax.experimental import pallas as pl
from jax.experimental.pallas import tpu as pltpu
from jax.sharding import PartitionSpec as P

HEAD = 64
EPSILON = 1e-06
TILE = 256
BLOCKS = 8
F32 = jnp.float32
BF16 = jnp.bfloat16
MESH_Y, MESH_C = 2, 1
ZM, Z1, X1 = 6, 2, 1
SPLIT = 2


def dot_nn(a, b):
    return lax.dot_general(a, b, (((1,), (0,)), ((), ())), preferred_element_type=F32)


def dot_nt(a, b):
    return lax.dot_general(a, b, (((1,), (1,)), ((), ())), preferred_element_type=F32)


def dot_tn(a, b):
    return lax.dot_general(a, b, (((0,), (0,)), ((), ())), preferred_element_type=F32)


def flip(value, axis, mask):
    pairs = [(i, i ^ mask) for i in range(lax.axis_size(axis))]
    return lax.ppermute(value, axis, pairs)


def pick(flag, when_one, when_zero):
    return jnp.where(flag == 1, when_one, when_zero)


def call(
    body, outs, ins, scratch, flops, moved, exps=0, grid=None, in_specs=None, out_specs=None,
    vmem=56,
):
    spaces = {"v": pltpu.VMEM, "s": pltpu.SMEM, "a": pl.ANY}
    if in_specs is None:
        in_specs = [pl.BlockSpec(memory_space=spaces[kind]) for kind, _ in ins]
        out_specs = [pl.BlockSpec(memory_space=pltpu.VMEM) for _ in outs]
    kwargs = {} if grid is None else {"grid": grid}
    return pl.pallas_call(
        body,
        out_shape=[jax.ShapeDtypeStruct(shape, kind) for shape, kind in outs],
        in_specs=in_specs,
        out_specs=out_specs,
        scratch_shapes=scratch,
        cost_estimate=pl.CostEstimate(flops=flops, bytes_accessed=moved, transcendentals=exps),
        compiler_params=pltpu.CompilerParams(vmem_limit_bytes=vmem << 20),
        **kwargs,
    )(*[value for _, value in ins])


def run_copies(copies):
    for copy in copies:
        copy.start()
    for copy in copies:
        copy.wait()


def turned(values, cosine, signed_sine):
    lane = lax.broadcasted_iota(jnp.int32, values.shape, 1)
    ahead = pltpu.roll(values, 128 - HEAD // 2, 1)
    behind = pltpu.roll(values, HEAD // 2, 1)
    partner = jnp.where(lane % HEAD < HEAD // 2, ahead, behind)
    return values * cosine + partner * signed_sine


def bits(count):
    return [tuple((i >> (count - 1 - j)) & 1 for j in range(count)) for i in range(1 << count)]


def place_of(info, bx, q):
    z = info[3] ^ (q >> 1) ^ (3 * (q & 1))
    return z * 2 + (info[4] ^ bx)


def even_of(info):
    return (info[3] & 1) ^ info[1]


def block_of(info, t):
    return t ^ info[0] ^ (info[3] >> 1) ^ even_of(info)


def column_of(info, by, other):
    block = (info[0] ^ by) * 2 + (info[1] ^ other)
    return pl.multiple_of(block * 256, 256)


def source_of(parts, by, bx, q):
    own, over_x, over_y, corner_y, corner_x = parts
    if by == 0:
        return (own, over_x)[bx].at[q]
    if bx == 0:
        return over_y.at[q]
    split = corner_y.shape[0]
    return corner_y.at[q] if q < split else corner_x.at[q - split]


def put(outs, by, bx, q, rows, value):
    send_x, send_y, keep_x, keep_y, own = outs
    split = keep_x.shape[0]
    if by and bx:
        spot = (send_y, q) if q < split else (send_x, q - split)
    elif by:
        spot = (send_y, split + q) if q < split else (keep_y, q - split)
    elif bx:
        spot = (keep_x, q) if q < split else (send_x, 4 - split + q - split)
    else:
        spot = (own, q)
    spot[0][spot[1], rows, :] = value


def put_lanes(outs, by, bx, q, rows, lanes, value):
    class Cut:
        def __init__(self, ref):
            self.ref = ref
            self.shape = ref.shape

        def __setitem__(self, spot, content):
            self.ref[spot[0], spot[1], lanes] = content

    put(tuple(Cut(ref) for ref in outs), by, bx, q, rows, value)


def pack_body(*refs):
    out = refs[-1]
    at = 0
    for ref in refs[:-1]:
        if len(ref.shape) == 2:
            out[at] = ref[...]
            at += 1
        else:
            out[at : at + ref.shape[0]] = ref[...]
            at += ref.shape[0]


def piece_of(info, t, own, over_y, core):
    near = (t & 1) == info[1]
    mine = jnp.where(near, own[info[0]], core[0])
    other = jnp.where(near, over_y[...], core[1])
    return jnp.where((t >> 1) == info[0], mine, other)


def attn_copies(info, parts, w, sem):
    copies = []
    for by, bx in bits(2):
        for q in range(4):
            copies.append(pltpu.make_async_copy(
                source_of(parts, by, bx, q), w.at[by, place_of(info, bx, q)],
                sem.at[len(copies)]))
    return copies


def qkv_body(*refs):
    info, x_parts, fv_parts, cosine, sine = refs[0], refs[1:4], refs[4:7], refs[7], refs[8]
    parts = refs[9:14]
    x, h1, q, k, b, gains, w, sem = refs[14:]
    run_copies(attn_copies(info, parts, w, sem))
    rows = 128
    width = w.shape[3]
    model = x.shape[1]
    for j in range(2):
        pair = w[0, :, 3 * rows : 3 * rows + 16, j * rows : (j + 1) * rows]
        row = jnp.concatenate([pair[d, 0:1, :] for d in range(BLOCKS)], axis=1).astype(F32)
        gains[j : j + 1, :] = row
    gain = gains[0:1, :]

    def step(t, carry):
        at = pl.ds(pl.multiple_of(t * TILE, TILE), TILE)
        xb = piece_of(info, t, *x_parts)
        x[at, :] = xb
        first = piece_of(info, t, *fv_parts)
        xt = xb.astype(F32)
        inverse = lax.rsqrt(jnp.mean(xt * xt, axis=-1, keepdims=True) + EPSILON)
        h = (xt * inverse * gain).astype(BF16)
        h1[at, :] = h
        cos_t, sin_t = cosine[at, :], sine[at, :]
        quarters = [first[:, i * width : (i + 1) * width] for i in range(4)]
        for by in range(2):
            side = [jnp.where(info[1] == 1, quarters[2 * i + 1], quarters[2 * i]) for i in (0, 1)]
            blend = jnp.where((info[0] ^ by) == 1, side[1], side[0]).astype(F32)
            for n in range(3):
                weight = w[by, :, n * rows : (n + 1) * rows, :].reshape(model, width)
                acc = dot_nn(h, weight)
                cols = pl.ds(by * width, width)
                if n == 2:
                    b[at, cols] = (0.5 * acc + 0.5 * blend).astype(BF16)
                else:
                    halves = [
                        turned(acc[:, j : j + 128], cos_t, sin_t) for j in range(0, width, 128)
                    ]
                    both = jnp.concatenate(halves, axis=1).astype(BF16)
                    (q, k)[n][at, cols] = both * BF16(0.125) if n == 0 else both
        return carry

    lax.fori_loop(0, x.shape[0] // TILE, step, 0)


def split_heads(pair):
    lane = lax.broadcasted_iota(jnp.int32, pair.shape, 1)
    zero = jnp.zeros_like(pair)
    return jnp.concatenate(
        [jnp.where(lane < HEAD, pair, zero), jnp.where(lane < HEAD, zero, pair)], axis=0
    )


def join_heads(both):
    half = both.shape[0] // 2
    lane = lax.broadcasted_iota(jnp.int32, (half, both.shape[1]), 1)
    return jnp.where(lane < HEAD, both[:half], both[half:])


def hide_later(scores, fill):
    length, width = scores.shape
    key_at = lax.broadcasted_iota(jnp.int32, (TILE, width), 0)
    query_at = lax.broadcasted_iota(jnp.int32, (TILE, width), 1) % TILE
    last = jnp.where(key_at <= query_at, scores[length - TILE :], fill)
    if length == TILE:
        return last
    return jnp.concatenate([scores[: length - TILE], last], axis=0)


def attend_body(q, k, b, att, lse):
    for i in range(q.shape[0] // TILE):
        length = (i + 1) * TILE
        queries = split_heads(q[i * TILE : length, :])
        scores = hide_later(dot_nt(k[:length, :], queries), -1e30)
        top = jnp.max(scores, axis=0, keepdims=True)
        grown = jnp.exp(scores - top)
        total = jnp.sum(grown, axis=0, keepdims=True)
        logs = top + jnp.log(total)
        probs = (grown * (1.0 / total)).astype(BF16)
        att[i * TILE : length, :] = join_heads(dot_tn(probs, b[:length, :])).astype(BF16)
        lse[0, 0:1, i * TILE : length] = logs[:, :TILE]
        lse[0, 1:2, i * TILE : length] = logs[:, TILE:]


def attend_back_body(q, k, b, datt, lse, cosine, sine, dq, dk, dv, k_acc, v_acc):
    k_acc[...] = jnp.zeros_like(k_acc)
    v_acc[...] = jnp.zeros_like(v_acc)
    for i in range(q.shape[0] // TILE):
        length = (i + 1) * TILE
        at = slice(i * TILE, length)
        queries = split_heads(q[at, :])
        grads = split_heads(datt[at, :])
        keys = k[:length, :]
        logs = jnp.concatenate([lse[0, 0:1, at], lse[0, 1:2, at]], axis=1)
        probs = jnp.exp(hide_later(dot_nt(keys, queries) - logs, -1e30))
        grad_probs = dot_nt(b[:length, :], grads)
        delta = jnp.sum(probs * grad_probs, axis=0, keepdims=True)
        grad_scores = (probs * (grad_probs - delta)).astype(BF16)
        v_acc[:length, :] += dot_nn(probs.astype(BF16), grads)
        k_acc[:length, :] += dot_nn(grad_scores, queries)
        turned_back = turned(
            0.125 * join_heads(dot_tn(grad_scores, keys)), cosine[at, :], -sine[at, :]
        )
        dq[at, :] = turned_back.astype(BF16)
    for i in range(q.shape[0] // TILE):
        at = slice(i * TILE, (i + 1) * TILE)
        dk[at, :] = turned(k_acc[at, :], cosine[at, :], -sine[at, :]).astype(BF16)
        dv[at, :] = (0.5 * v_acc[at, :]).astype(BF16)


def out_copies(info, parts, wo, sem):
    first = parts[0].shape[1] - 128
    copies = []
    for by, bx, other, t in bits(4):
        row = pl.multiple_of(block_of(info, t) * 256 + (info[4] ^ bx) * 128, 128)
        copies.append(pltpu.make_async_copy(
            source_of(parts, by, bx, other * 2 + t).at[pl.ds(first, 128)],
            wo.at[pl.ds(row, 128), pl.ds(column_of(info, by, other), 256)],
            sem.at[len(copies)]))
    return copies


def out_body(*refs):
    info, att, parts, (part, wo, sem) = refs[0], refs[1], refs[2:7], refs[7:]
    run_copies(out_copies(info, parts, wo, sem))

    def step(t, carry):
        at = pl.ds(pl.multiple_of(t * TILE, TILE), TILE)
        part[at, :] = dot_nn(att[at, :], wo[...]).astype(BF16)
        return carry

    lax.fori_loop(0, att.shape[0] // TILE, step, 0)


def middle_of(x, part, recv, at):
    return x[at, :].astype(F32) + (part[at, :].astype(F32) + recv[at, :].astype(F32))


def out_back_body(*refs):
    info, gh2, gh2_recv, x, part, recv, gy, gains, att, down = refs[:10]
    parts = refs[10:15]
    datt, own_mid, gain_grad = refs[15:18]
    outs, (wo, gb, sem) = refs[18:23], refs[23:]
    down_rows = down.shape[3]
    copies = out_copies(info, parts, wo, sem)
    for copy in copies:
        copy.start()
    gain_grad[...] = jnp.zeros_like(gain_grad)

    def norm_step(t, carry):
        at = pl.ds(pl.multiple_of(t * TILE, TILE), TILE)
        middle = middle_of(x, part, recv, at)
        inverse = lax.rsqrt(jnp.mean(middle * middle, axis=-1, keepdims=True) + EPSILON)
        grad = gh2[at, :].astype(F32) + gh2_recv[at, :].astype(F32)
        scaled = grad * gains[1:2, :]
        share = inverse * inverse * inverse * jnp.mean(scaled * middle, axis=-1, keepdims=True)
        total = gy[at, :].astype(F32) + inverse * scaled - middle * share
        gb[at, :] = total.astype(BF16)
        gain_grad[0:1, :] += jnp.sum(grad * middle * inverse, axis=0, keepdims=True)

        @pl.when((t & 1) == info[1])
        def _():
            own_mid[t >> 1] = total

        return carry

    tiles = att.shape[0] // TILE
    lax.fori_loop(0, tiles, norm_step, 0)
    for copy in copies:
        copy.wait()

    def step(t, carry):
        at = pl.ds(pl.multiple_of(t * TILE, TILE), TILE)
        datt[at, :] = dot_nt(gb[at, :], wo[...]).astype(BF16)
        return carry

    lax.fori_loop(0, tiles, step, 0)
    for by, other in bits(2):
        grad = dot_tn(att[...], gb[:, pl.ds(column_of(info, by, other), 256)]).astype(BF16)
        for t in range(2):
            swap = block_of(info, t) == 1
            block = jnp.where(swap, grad[256:], grad[:256])
            for bx in range(2):
                q = other * 2 + t
                put(outs, by, bx, q, slice(0, down_rows), down[by, bx, q])
                put(outs, by, bx, q, slice(down_rows, down_rows + 128), jnp.where(
                    (info[4] ^ bx) == 1, block[128:], block[:128]))


def crossed(parts, by, bx, q):
    low, low_x, low_y, low_xy, high, high_x, high_y, high_xy = parts
    group = (low, low_x, low_y, low_xy) if q < 2 else (high, high_x, high_y, high_xy)
    return group[by * 2 + bx].at[q & 1]


def ffn_copies(info, first, parts, wgu, wd, sem):
    units = wd.shape[0]
    own = units // 2
    part = own // 2
    copies = []
    for by, bx in bits(2):
        for q in range(4):
            lane = pl.multiple_of(place_of(info, bx, q) * 128, 128)
            if first:
                source = parts[q].at[0] if by + bx == 0 else parts[4 + q].at[by * 2 + bx - 1]
            else:
                source = crossed(parts, by, bx, q)
            for up in range(2):
                copies.append(pltpu.make_async_copy(
                    source.at[pl.ds(0, own), pl.ds(up * 128, 128)],
                    wgu.at[pl.ds(up * units + by * own, own), pl.ds(lane, 128)],
                    sem.at[len(copies)]))
    for by, bx, other, t in bits(4):
        row = pl.multiple_of(block_of(info, t) * own + (info[4] ^ bx) * part, 16)
        q = other * 2 + t
        if first:
            source = source_of(parts[8:], by, bx, q).at[pl.ds(0, part)]
        else:
            source = crossed(parts, by, bx, q).at[pl.ds(own, part)]
        copies.append(pltpu.make_async_copy(
            source, wd.at[pl.ds(row, part), pl.ds(column_of(info, by, other), 256)],
            sem.at[len(copies)]))
    return copies


def ffn_body(first, *refs):
    info = refs[0]
    if first:
        x, part, recv, gains = refs[1:5]
        cot_parts, parts = refs[5:8], refs[8:21]
        h2, gy, gh2, res = refs[21:25]
        outs, refs = refs[25:30], refs[30:]
    else:
        h2, gy, gh2_in, res_in = refs[1:5]
        parts = refs[5:13]
        gh2, rkeep, rsend = refs[13:16]
        outs, down_grad, refs = refs[16:20], refs[20], refs[21:]
    hid, ggu, wgu, wd, sem = refs
    copies = ffn_copies(info, first, parts, wgu, wd, sem)
    for copy in copies:
        copy.start()
    units = wd.shape[0]
    tiles = h2.shape[0] // TILE
    if first:
        live = jnp.where(info[0] < info[5], 1.0, 0.0)

        def norm_step(t, carry):
            at = pl.ds(pl.multiple_of(t * TILE, TILE), TILE)
            middle = middle_of(x, part, recv, at)
            inverse = lax.rsqrt(jnp.mean(middle * middle, axis=-1, keepdims=True) + EPSILON)
            h2[at, :] = (middle * inverse * gains[1:2, :]).astype(BF16)
            gy[at, :] = (piece_of(info, t, *cot_parts).astype(F32) * live).astype(BF16)
            return carry

        lax.fori_loop(0, tiles, norm_step, 0)
    for copy in copies:
        copy.wait()

    def step(t, carry):
        at = pl.ds(pl.multiple_of(t * TILE, TILE), TILE)
        both = dot_nt(wgu[...], h2[at, :])
        gate, up = both[:units], both[units:]
        sig = 1.0 / (1.0 + jnp.exp(-gate))
        act = gate * sig
        hidden = (act * up).astype(BF16)
        hid[:, at] = hidden
        grad_hidden = dot_nt(wd[...], gy[at, :])
        ggu[:units, at] = (grad_hidden * up * (sig + act * (1.0 - sig))).astype(BF16)
        ggu[units:, at] = (grad_hidden * act).astype(BF16)
        grad_h = dot_tn(ggu[:, at], wgu[...])
        result = dot_tn(hidden, wd[...])
        if first:
            gh2[at, :] = grad_h.astype(BF16)
            res[at, :] = result.astype(BF16)
        else:
            gh2[at, :] = (gh2_in[at, :].astype(F32) + grad_h).astype(BF16)
            result = res_in[at, :].astype(F32) + result

            @pl.when((t & 1) == info[1])
            def _():
                rkeep[t >> 1] = result

            @pl.when((t & 1) != info[1])
            def _():
                rsend[t >> 1] = result.astype(BF16)

        return carry

    lax.fori_loop(0, tiles, step, 0)
    own = units // 2
    part = own // 2
    swap = info[4] == 1
    for q in (3, 2, 1, 0):
        z = info[3] ^ (q >> 1) ^ (3 * (q & 1))
        grad = dot_nn(ggu[...], h2[:, pl.ds(pl.multiple_of(z * 256, 256), 256)]).astype(BF16)
        lo, hi = grad[:, :128], grad[:, 128:]
        for bx, side in ((0, jnp.where(swap, hi, lo)), (1, jnp.where(swap, lo, hi))):
            for by, up in bits(2):
                lanes = slice(up * 128, up * 128 + 128)
                piece = side[up * units + by * own : up * units + (by + 1) * own]
                if first:
                    put_lanes(outs, by, bx, q, slice(0, own), lanes, piece)
                else:
                    outs[q][bx * 2 + by, :, lanes] = piece
    for by, other in bits(2):
        grad = dot_nn(hid[...], gy[:, pl.ds(column_of(info, by, other), 256)]).astype(BF16)
        for t in range(2):
            block = jnp.where(block_of(info, t) == 1, grad[own:], grad[:own])
            for bx in range(2):
                q = other * 2 + t
                piece = jnp.where((info[4] ^ bx) == 1, block[part:], block[:part])
                if first:
                    put(outs, by, bx, q, slice(own, own + part), piece)
                else:
                    down_grad[by, bx, q] = piece


def qkv_grad_body(by, *refs):
    info, dq, dk, dv, h1, gains, gain_grad = refs[:7]
    parts, refs = (refs[7:10], refs[10:]) if by else (refs[7:9], refs[9:])
    outs, (w, acc, sem) = refs[:3], refs[3:]
    copies = []
    for bx in range(2):
        for q in range(4):
            if by == 0 or bx == 0:
                source = parts[bx].at[q]
            else:
                split = parts[1].shape[0]
                source = parts[1].at[q] if q < split else parts[2].at[q - split]
            copies.append(pltpu.make_async_copy(
                source, w.at[place_of(info, bx, q)], sem.at[len(copies)]))
    for copy in copies:
        copy.start()
    width = w.shape[2]

    def spot(bx, q):
        if by:
            diagonal, send, keep = outs
            split = send.shape[0] // 2
            if q < split:
                return send, q if bx else split + q
            return (diagonal if bx else keep), q - split
        send, keep, own = outs
        split = keep.shape[0]
        if not bx:
            return own, q
        return (keep, q) if q < split else (send, q - split)

    waiting = True
    ones = jnp.ones((8, 3 * width), BF16)
    three = jnp.concatenate([dq[...], dk[...], dv[...]], axis=1)
    for q in (3, 2, 1, 0):
        z = info[3] ^ (q >> 1) ^ (3 * (q & 1))
        at = pl.ds(pl.multiple_of(z * 256, 256), 256)
        grad = dot_tn(h1[:, at], three)
        if waiting:
            for copy in copies:
                copy.wait()
            waiting = False
        weight = jnp.concatenate(
            [w[pl.ds(z * 2, 2), n * 128 : (n + 1) * 128, :].reshape(256, width)
             for n in range(3)], axis=1)
        shares = dot_nt(ones, (grad * weight.astype(F32)).astype(BF16))
        acc[:, at] = shares / gains[0:1, at]
        grad = grad.astype(BF16)
        for bx in range(2):
            part = jnp.where((info[4] ^ bx) == 1, grad[128:], grad[:128])
            ref, i = spot(bx, q)
            for n in range(3):
                ref[i, n * 128 : (n + 1) * 128, :] = part[:, n * width : (n + 1) * width]
    for bx in range(2):
        for q in range(4):
            at = pl.ds(pl.multiple_of(place_of(info, bx, q) * 128, 128), 128)
            row = jnp.concatenate([acc[0:1, at], gain_grad[0:1, at]], axis=1)
            ref, i = spot(bx, q)
            ref[i, 384:400, :] = jnp.broadcast_to(row, (16, 256)).astype(BF16)


def qkv_back_body(*refs):
    info, grads = refs[0], (refs[1:4], refs[4:7])
    parts = refs[7:12]
    gkeep, gsend, w, sem = refs[12:]
    run_copies(attn_copies(info, parts, w, sem))
    width = w.shape[3]
    model = gkeep.shape[2]

    def step(t, carry):
        at = pl.ds(pl.multiple_of(t * TILE, TILE), TILE)
        grad_h = jnp.zeros((TILE, model), F32)
        for by in range(2):
            for n in range(3):
                weight = w[by, :, n * 128 : (n + 1) * 128, :].reshape(model, width)
                grad_h = grad_h + dot_nt(grads[by][n][at, :], weight)

        @pl.when((t & 1) == info[1])
        def _():
            gkeep[t >> 1] = grad_h

        @pl.when((t & 1) != info[1])
        def _():
            gsend[t >> 1] = grad_h.astype(BF16)

        return carry

    lax.fori_loop(0, gkeep.shape[0] * 2, step, 0)


def input_body(info, gkeep, grecv, x, own_mid, gains, keep, send):
    for half in range(2):
        at = pl.ds(pl.multiple_of((half * 2 + info[1]) * TILE, TILE), TILE)
        xt = x[at, :].astype(F32)
        grad = gkeep[half] + grecv[half].astype(F32)
        inverse = lax.rsqrt(jnp.mean(xt * xt, axis=-1, keepdims=True) + EPSILON)
        scaled = grad * gains[0:1, :]
        share = inverse * inverse * inverse * jnp.mean(scaled * xt, axis=-1, keepdims=True)
        total = own_mid[half] + inverse * scaled - xt * share

        @pl.when(info[0] == half)
        def _():
            keep[...] = total

        @pl.when(info[0] != half)
        def _():
            send[...] = total.astype(BF16)


def gate(live, *names):
    for name, value in zip(names, lax.optimization_barrier([live[name] for name in names])):
        live[name] = value


def plus(*values):
    total = values[0].astype(F32)
    for value in values[1:]:
        total = total + value.astype(F32)
    return total


def on_device(
    tokens, first_values, seq_counts, norm1_gain, query_weight, key_weight, value_weight,
    out_weight, norm2_gain, gate_weight, up_weight, down_weight, output_cotangent,
):
    slots, piece, model = tokens.shape
    length = piece * lax.axis_size("seq")
    wide = lax.axis_size("dp") // BLOCKS
    s = lax.axis_index("seq")
    place = lax.axis_index("dp")
    y, c = s // 2, s % 2
    d = place // wide
    z, x_at = d // 2, d % 2
    info = jnp.stack([y, c, d, z, x_at, seq_counts[0]]).astype(jnp.int32)
    even = (z & 1) ^ c

    def pregather(shard):
        step = 1
        while step < wide:
            other = flip(shard, "dp", step)
            bit = (place // step) % 2
            shard = pick(
                bit, jnp.concatenate([other, shard]), jnp.concatenate([shard, other]))
            step *= 2
        return shard

    def postscatter(total):
        step = wide // 2
        while step >= 1:
            half = total.shape[0] // 2
            bit = (place // step) % 2
            lo, hi = total[:half], total[half:]
            total = pick(bit, hi, lo) + flip(pick(bit, lo, hi), "dp", step)
            step //= 2
        return total

    def far(v):
        return flip(v, "dp", ZM * wide)

    def near(v):
        return flip(v, "dp", Z1 * wide)

    def over_x(v):
        return flip(v, "dp", X1 * wide)

    def over_y(v):
        return flip(v, "seq", MESH_Y)

    def over_core(v):
        return flip(v, "seq", MESH_C)

    def other_slot(block):
        return pick(y, block[0], block[1])

    def mine_of(low, high):
        return jnp.stack([pick(even, low[1], low[0]), pick(even, high[0], high[1])])

    def theirs_of(low, high):
        return jnp.stack([pick(even, low[0], low[1]), pick(even, high[1], high[0])])

    def own_slot(block, recv):
        return jnp.stack([pick(y, block[1], block[0]), recv])

    def pack(*parts):
        rows = parts[0].shape[-2]
        (out,) = call(
            pack_body, [((4, rows, 256), BF16)], [("v", part) for part in parts], [],
            1000, 1 << 20, vmem=8)
        return out

    local = model // 2
    width = local // 2
    v = {}
    v["a0"] = jnp.concatenate(
        [pregather(query_weight), pregather(key_weight), pregather(value_weight),
         jnp.pad(jnp.concatenate([pregather(norm1_gain), pregather(norm2_gain)])[None],
                 ((0, 15), (0, 0)))])
    attn_rows = v["a0"].shape[0]
    down = pregather(down_weight)
    part = down.shape[0] // 2
    own = 2 * part
    units = 2 * own
    ffn = jnp.concatenate([pregather(gate_weight).T, pregather(up_weight).T], axis=1)
    v["b0"] = jnp.concatenate([ffn[part:own], ffn[own + part :]])[None]
    v["g0"] = jnp.concatenate([ffn[:part], ffn[own : own + part], down[:part]])
    v["r0"] = jnp.concatenate([down[part:], pregather(out_weight)])
    out_rows = v["r0"].shape[0] - part
    v["t_send"] = other_slot(tokens)
    v["f_send"] = other_slot(first_values)
    v["c_send"] = other_slot(output_cotangent)
    v["tokens"], v["firsts"], v["cots"] = tokens, first_values, output_cotangent

    gate(v, "a0", "t_send", "b0")
    v["ty"], v["af"], v["an"] = over_y(v["t_send"]), far(v["a0"]), near(v["a0"])
    v["bx"], v["bf0"] = over_x(v["b0"]), far(v["b0"])
    gate(v, "a0", "af", "an", "ty", "tokens", "b0", "bx", "bf0", "f_send", "c_send", "firsts", "cots", "r0", "g0")
    v["fy"], v["anf"], v["rf"] = over_y(v["f_send"]), near(v["af"]), far(v["r0"])
    v["tc"] = over_core(own_slot(v["tokens"], v["ty"]))
    v["bn0"] = near(v["b0"])
    gate(v, "a0", "af", "an", "anf", "fy", "tc", "firsts", "b0", "bx", "bf0", "bn0", "r0", "rf", "g0", "c_send", "cots")
    v["z"] = pack(v["a0"], v["af"], v["an"], v["anf"])
    v["zx"], v["zy"] = over_x(v["z"]), over_y(v["z"])
    v["rlow"] = jnp.stack([v["r0"], v["rf"]])
    v["rhigh"], v["gf"] = near(v["rlow"]), far(v["g0"])
    v["fc"] = over_core(own_slot(v["firsts"], v["fy"]))
    half = HEAD // 2
    frequency = 10000.0 ** (-(jnp.arange(half).astype(F32) * 2.0) / HEAD)
    angles = jnp.arange(length).astype(F32)[:, None] * frequency[None, :]
    v["cosine"] = jnp.tile(jnp.cos(angles), (1, 4))
    v["sine"] = jnp.tile(jnp.concatenate([-jnp.sin(angles), jnp.sin(angles)], axis=1), (1, 2))
    gate(v, "z", "zx", "zy", "rlow", "rhigh", "g0", "gf", "fc", "b0", "bx", "bf0", "bn0", "cosine", "sine", "c_send", "cots")
    v["zu"], v["zv"] = over_y(v["zx"][:SPLIT]), over_x(v["zy"][SPLIT:])
    v["rmine"] = mine_of(v["rlow"], v["rhigh"])
    v["rother"] = over_core(theirs_of(v["rlow"], v["rhigh"]))
    v["b10"] = over_y(jnp.concatenate([v["b0"], v["bx"]]))
    v["glow"] = jnp.stack([v["g0"], v["gf"]])
    v["ghigh"] = near(v["glow"])
    gate(v, "z", "zx", "zy", "zu", "zv", "rmine", "rother", "b0", "bx", "b10", "bf0", "bn0", "glow", "ghigh", "c_send", "cots")
    v["r"] = pack(v["rmine"], v["rother"])
    v["rx"], v["ry"] = over_x(v["r"]), over_y(v["r"])
    v["b3"] = jnp.concatenate([v["bx"], v["b10"]])
    v["bf3"], v["bn3"] = far(v["b3"]), near(v["b3"])
    glow, ghigh = v["glow"][:, own:], v["ghigh"][:, own:]
    v["gmine"], v["gother"] = mine_of(glow, ghigh), over_core(theirs_of(glow, ghigh))

    def weights(name):
        return [("a", v[name + end]) for end in ("", "x", "y", "u", "v")]

    def values(*names):
        return [("v", v[name]) for name in names]

    square = ((length, model), BF16)
    tall = ((length, local), BF16)
    tile = (2, piece, model)
    w_scratch = pltpu.VMEM((2, BLOCKS, attn_rows, width), BF16)
    sem16 = pltpu.SemaphoreType.DMA((16,))
    narrow = 2 * length * model * local
    v["x"], v["h1"], v["q"], v["k"], v["b"], v["gains"] = call(
        qkv_body, [square, square, tall, tall, tall, ((8, model), F32)],
        [("s", info)] + values("tokens", "ty", "tc", "firsts", "fy", "fc", "cosine", "sine") + weights("z"),
        [w_scratch, sem16], 3 * narrow, 14 << 20, vmem=26,
    )
    gate(v, "x", "h1", "q", "k", "b", "gains", "r", "rx", "ry", "b0", "b3", "bf0", "bn0", "bf3", "bn3", "glow", "ghigh", "gmine", "gother", "c_send", "cots")
    v["ru"], v["rv"] = over_y(v["rx"][:SPLIT]), over_x(v["ry"][SPLIT:])
    v["gl"] = jnp.concatenate([v["glow"][:, :own], v["gmine"]], axis=1)
    v["gh"] = jnp.concatenate([v["ghigh"][:, :own], v["gother"]], axis=1)
    v["glx"], v["ghy"] = over_x(v["gl"]), over_y(v["gh"])
    v["bnf3"] = near(v["bf3"])
    head_specs = [pl.BlockSpec((length, 128), lambda i: (0, i))] * 3
    lse_spec = pl.BlockSpec((1, 2, length), lambda i: (i, 0, 0))
    pairs = local // 128
    v["att"], v["lse"] = call(
        attend_body, [tall, ((pairs, 2, length), F32)], values("q", "k", "b"), [],
        4 * length * length * local, 4 << 20, length * length * pairs * 2, vmem=20,
        grid=(pairs,), in_specs=head_specs, out_specs=[head_specs[0], lse_spec],
    )
    v["cy"], v["bnf0"] = over_y(v["c_send"]), near(v["bf0"])
    (v["part"],) = call(
        out_body, [square], [("s", info)] + values("att") + weights("r"),
        [pltpu.VMEM((local, model), BF16), sem16], narrow, 5 << 20, vmem=12,
    )
    gate(v, "att", "lse", "r", "rx", "ry", "ru", "rv", "part", "cy", "cots", "gl", "glx", "gh", "ghy", "b0", "b3", "bf0", "bn0", "bf3", "bn3", "bnf0", "bnf3")
    v["precv"], v["cc"] = over_core(v["part"]), over_core(own_slot(v["cots"], v["cy"]))
    gate(v, "part", "precv", "cc", "gl", "glx", "gh", "ghy")

    def five(rows):
        return [((count, rows, 256), BF16)
                for count in (2 * (4 - SPLIT), 2 * SPLIT, SPLIT, 4 - SPLIT, 4)]

    v["gly"], v["glxy"] = over_y(v["gl"]), over_y(v["glx"])
    v["ghx"], v["ghxy"] = over_x(v["gh"]), over_x(v["ghy"])
    scratch = [pltpu.VMEM((units, length), BF16), pltpu.VMEM((2 * units, length), BF16),
               pltpu.VMEM((2 * units, model), BF16), pltpu.VMEM((units, model), BF16),
               pltpu.SemaphoreType.DMA((48,))]
    ffn_flops = 18 * length * model * units
    v["h2"], v["gy"], v["gh2b"], v["resb"], v["bsx"], v["bsy"], v["bkx"], v["bky"], v["bown"] = call(
        functools.partial(ffn_body, True), [square] * 4 + five(own + part),
        [("s", info)] + values("x", "part", "precv", "gains", "cots", "cy", "cc")
        + [("a", v[name]) for name in ("b0", "bf0", "bn0", "bnf0")]
        + [("a", v[name]) for name in ("b3", "bf3", "bn3", "bnf3")] + weights("r"),
        scratch, ffn_flops, 24 << 20, vmem=40,
    )
    gate(v, "h2", "gy", "gh2b", "resb", "bsx", "bsy", "bkx", "bky", "bown", "gl", "glx", "gly", "glxy", "gh", "ghx", "ghy", "ghxy")
    v["brx"], v["bry"] = over_x(v["bsx"]), over_y(v["bsy"])
    quads = [((4, own, 256), BF16)] * 4 + [((2, 2, 4, part, 256), BF16)]
    (v["gh2"], v["rkeep"], v["rsend"], v["n0"], v["n1"], v["n2"], v["n3"], v["dgrad"]) = call(
        functools.partial(ffn_body, False), [square, (tile, F32), (tile, BF16)] + quads,
        [("s", info)] + values("h2", "gy", "gh2b", "resb")
        + [("a", v[half + over]) for half in ("gl", "gh") for over in ("", "x", "y", "xy")],
        scratch, ffn_flops, 24 << 20, vmem=40,
    )
    gate(v, "gh2", "rkeep", "rsend", "n0", "n1", "n2", "n3", "dgrad", "brx", "bry", "bkx", "bky", "bown", "part", "precv")

    def fold(name):
        v[name + "fx"] = plus(v[name + "kx"], v[name + "ry"][:SPLIT]).astype(BF16)
        v[name + "fy"] = plus(v[name + "ky"], v[name + "rx"][: 4 - SPLIT]).astype(BF16)

    def total_of(name):
        low = plus(v[name + "own"][:SPLIT], v[name + "ry"][SPLIT:], v[name + "rx2"])
        high = plus(v[name + "own"][SPLIT:], v[name + "rx"][4 - SPLIT :], v[name + "ry2"])
        return jnp.concatenate([low, high])

    def rows_out(name, total, first):
        v[name + "t"] = total
        v[name + "m"] = over_core(total[2:, first:].astype(BF16))

    def quarter(name, first, q):
        total, recv = v[name + "t"], v[name + "m"]
        rows = total[q >> 1, first:]
        other = recv[q >> 1].astype(F32)
        mine = pick(even, other, rows) if q in (0, 3) else pick(even, rows, other)
        return mine if first == 0 else jnp.concatenate([total[q, :first], mine])

    def owner_send(halves_of):
        return pick(y, halves_of[0], halves_of[1])

    def owner_keep(halves_of):
        return pick(y, halves_of[1], halves_of[0])

    def both_slots(keep, recv):
        return pick(y, jnp.stack([recv, keep]), jnp.stack([keep, recv]))

    def own_tokens(full):
        cut_up = full.reshape(2, 2, piece, full.shape[-1])
        return pick(c, cut_up[:, 1], cut_up[:, 0])

    v["gh2r"] = over_core(v["gh2"])
    v["rrecv"] = over_core(v["rsend"])
    fold("b")
    v["brx2"], v["bry2"] = over_x(v["bfx"]), over_y(v["bfy"])
    v["nn3"] = near(v["n3"])
    (v["datt"], v["mid"], v["gain2"],
     v["ssx"], v["ssy"], v["skx"], v["sky"], v["sown"]) = call(
        out_back_body, [tall, (tile, F32), ((8, model), F32)] + five(part + out_rows),
        [("s", info)] + values("gh2", "gh2r", "x", "part", "precv", "gy", "gains", "att", "dgrad") + weights("r"),
        [pltpu.VMEM((local, model), BF16), pltpu.VMEM((length, model), BF16), sem16],
        2 * narrow, 20 << 20, vmem=34,
    )
    gate(v, "datt", "mid", "gain2", "ssx", "ssy", "skx", "sky", "sown", "bown", "brx", "bry", "brx2", "bry2", "n0", "n1", "n2", "nn3", "rkeep", "rrecv", "part", "precv")
    v["srx"], v["sry"] = over_x(v["ssx"]), over_y(v["ssy"])
    v["n1"] = plus(v["n1"], v["nn3"]).astype(BF16)
    v["nf1"], v["nn2"] = far(v["n1"][2:]), near(v["n2"])
    rows_out("b", total_of("b"), own)

    def attend_back(side):
        first = side * (pairs // 2)
        column = pl.BlockSpec((length, 128), lambda i: (0, i + first))
        table = pl.BlockSpec((length, 128), lambda i: (0, 0))
        sums = pl.BlockSpec((1, 2, length), lambda i: (i + first, 0, 0))
        target = pl.BlockSpec((length, 128), lambda i: (0, i))
        v[f"dq{side}"], v[f"dk{side}"], v[f"dv{side}"] = call(
            attend_back_body, [((length, width), BF16)] * 3,
            values("q", "k", "b", "datt", "lse", "cosine", "sine"),
            [pltpu.VMEM((length, 128), F32), pltpu.VMEM((length, 128), F32)],
            5 * length * length * local, 4 << 20, length * length * pairs, vmem=26,
            grid=(pairs // 2,), in_specs=[column] * 4 + [sums, table, table],
            out_specs=[target] * 3,
        )

    def attn_grads(side):
        counts = (4 - SPLIT, 2 * SPLIT, 4 - SPLIT) if side else (4 - SPLIT, SPLIT, 4)
        names = ("zy", "zu", "zv") if side else ("z", "zx")
        return call(
            functools.partial(qkv_grad_body, side),
            [((count, attn_rows, width), BF16) for count in counts],
            [("s", info), ("v", v[f"dq{side}"]), ("v", v[f"dk{side}"]), ("v", v[f"dv{side}"])]
            + values("h1", "gains", "gain2") + [("a", v[name]) for name in names],
            [pltpu.VMEM((BLOCKS, attn_rows, width), BF16), pltpu.VMEM((8, model), F32),
             pltpu.SemaphoreType.DMA((8,))], 3 * narrow // 2, 7 << 20, vmem=24,
        )

    attend_back(1)
    v["qdx"], v["qsy"], v["qky"] = attn_grads(1)
    gate(v, "dq1", "dk1", "dv1", "qdx", "qsy", "qky", "q", "k", "b", "datt", "srx", "sry", "skx", "sky", "sown", "n0", "n1", "nf1", "nn2", "bt", "bm", "rkeep", "rrecv", "part", "precv")
    v["qry"], v["qrd"] = over_y(v["qsy"]), over_x(v["qdx"])
    fold("s")
    v["srx2"] = over_x(v["sfx"])
    v["nf0"] = far(v["n1"][:2])
    v["bzn"] = near(jnp.stack([quarter("b", own, 2), quarter("b", own, 3)]).astype(BF16))
    attend_back(0)
    v["qsx"], v["qkx"], v["qown"] = attn_grads(0)
    live_now = jnp.where(y < seq_counts[0], 1.0, 0.0)
    middle_own = own_tokens(v["x"]).astype(F32) + plus(
        own_tokens(v["part"]), own_tokens(v["precv"]))
    result = (live_now * (middle_own + plus(v["rkeep"], v["rrecv"]))).astype(BF16)
    v["okeep"], v["osend"] = owner_keep(result), owner_send(result)
    gate(v, "dq0", "dk0", "dv0", "dq1", "dk1", "dv1", "qsx", "qkx", "qown", "qry", "qrd", "qky", "srx", "sry", "srx2", "sfy", "sown", "n0", "nf0", "nf1", "nn2", "bzn", "bt", "bm", "okeep", "osend")
    v["qrx"] = over_x(v["qsx"])
    v["sry2"] = over_y(v["sfy"])
    v["nt0"] = plus(v["n0"][:2], v["nf0"], v["nn2"][:2])
    v["nx"] = over_x(plus(v["n0"][2:], v["nf1"], v["nn2"][2:]).astype(BF16))
    v["bt0"] = plus(quarter("b", own, 0), v["bzn"][0])
    v["bzf"] = far(plus(quarter("b", own, 1), v["bzn"][1]).astype(BF16))
    v["orecv"] = over_y(v["osend"])
    v["gkeep"], v["gsend"] = call(
        qkv_back_body, [(tile, F32), (tile, BF16)],
        [("s", info)] + values("dq0", "dk0", "dv0", "dq1", "dk1", "dv1") + weights("z"), [w_scratch, sem16],
        3 * narrow, 14 << 20, vmem=18,
    )
    gate(v, "gkeep", "gsend", "qry", "qrd", "qky", "qrx", "qkx", "qown", "bt0", "bzf", "nt0", "nx", "srx", "sry", "srx2", "sry2", "sown", "dv0", "dv1", "okeep", "orecv")
    output = both_slots(v["okeep"], v["orecv"])
    total_b = plus(v["bt0"], v["bzf"])
    v["grecv"] = over_core(v["gsend"])
    v["qfx"] = plus(v["qkx"], v["qry"][:SPLIT]).astype(BF16)
    v["qfy"] = plus(v["qky"], v["qrd"]).astype(BF16)
    v["qrx2"], v["qry2"] = over_x(v["qfx"]), over_y(v["qfy"])
    rows_out("s", total_of("s"), 0)
    v["nt0"] = plus(v["nt0"], v["nx"])
    v["ny"] = over_y(v["nt0"][1].astype(BF16))
    v["ikeep"], v["isend"] = call(
        input_body, [((piece, model), F32), ((piece, model), BF16)],
        [("s", info)] + values("gkeep", "grecv", "x", "mid", "gains"), [], 1000, 8 << 20, vmem=16,
    )
    gate(v, "ikeep", "isend", "qrx", "qry", "qrx2", "qry2", "qown", "st", "sm", "nt0", "ny", "dv0", "dv1")
    total_a = plus(v["nt0"][0], v["ny"])
    low = plus(v["qown"][:SPLIT], v["qry"][SPLIT:], v["qrx2"])
    high = plus(v["qown"][SPLIT:], v["qrx"], v["qry2"])
    v["qt"] = jnp.concatenate([low, high])
    v["qz"], v["sz"] = near(v["qt"][3].astype(BF16)), near(quarter("s", 0, 3).astype(BF16))
    v["irecv"] = over_y(v["isend"])
    cuts = [v[f"dv{side}"].reshape(2, 2, piece, width) for side in range(2)]
    dv_keep = [pick(c, cut[:, 1], cut[:, 0]) for cut in cuts]
    dv_recv = over_core(
        jnp.concatenate([pick(c, cut[:, 0], cut[:, 1]) for cut in cuts], axis=-1))
    dv_recv = [dv_recv[..., :width], dv_recv[..., width:]]
    blocks = []
    for column_y, column_c in bits(2):
        side = y ^ column_y
        mine = pick(side, dv_keep[1], dv_keep[0])
        theirs = pick(side, dv_recv[1], dv_recv[0])
        blocks.append(pick(c ^ column_c, theirs, mine))
    grad_rows = jnp.concatenate(blocks, axis=-1)
    v["fkeep"], v["fsend"] = owner_keep(grad_rows), owner_send(grad_rows)
    gate(v, "qt", "qz", "st", "sm", "sz", "irecv", "ikeep", "fkeep", "fsend")
    v["qzf"] = far(plus(v["qt"][1], v["qz"]).astype(BF16))
    v["szf"] = far(plus(quarter("s", 0, 1), v["sz"]).astype(BF16))
    v["qzn"] = near(v["qt"][2].astype(BF16))
    v["szn"] = near(quarter("s", 0, 2).astype(BF16))
    v["frecv"] = over_y(v["fsend"])
    v["qt0"], v["st0"] = v["qt"][0], quarter("s", 0, 0)
    grad_input = both_slots(v["ikeep"], v["irecv"].astype(F32))
    gate(v, "qt0", "st0", "qzf", "szf", "qzn", "szn", "fkeep", "frecv")
    total = plus(v["qt0"], v["qzf"], v["qzn"])
    gain_total = total[384]
    gain_share = jnp.broadcast_to(gain_total[None, :128], (8, 128))
    gain_sum = gain_total[:128] + over_core(gain_share)[0] + (
        over_y(gain_share)[0] + flip(gain_share, "seq", MESH_Y | MESH_C)[0])
    total_s = plus(v["st0"], v["szf"], v["szn"])
    grad_first = both_slots(v["fkeep"], v["frecv"]).astype(F32)

    def weave(lanes):
        pieces = [total_a[:part, lanes], total_b[:part, lanes],
                  total_a[part:own, lanes], total_b[part:own, lanes]]
        return jnp.concatenate(pieces).T

    return (
        output,
        grad_input,
        grad_first,
        postscatter(gain_sum),
        postscatter(total[:128]),
        postscatter(total[128:256]),
        postscatter(total[256:384]),
        postscatter(total_s[part:]),
        postscatter(gain_total[128:]),
        postscatter(weave(slice(0, 128))),
        postscatter(weave(slice(128, 256))),
        postscatter(jnp.concatenate([total_s[:part], total_b[own:]])),
    )


def solution(mesh):
    cut = P("dp", "seq")
    flat = P("dp")
    whole = P("dp", "seq", None)
    return jax.shard_map(
        on_device,
        mesh=mesh,
        in_specs=(whole, whole, flat, flat, cut, cut, cut, cut, flat, cut, cut, cut, whole),
        out_specs=(whole, whole, whole, flat, cut, cut, cut, cut, flat, cut, cut, cut),
        check_vma=False,
    )
```

```python
import functools

import jax
import jax.numpy as jnp
import numpy as np
from jax import lax
from jax.experimental import pallas as pl
from jax.experimental.pallas import tpu as pltpu
from jax.sharding import PartitionSpec as P

HEAD = 64
EPSILON = 1e-06
TILE = 256
BLOCKS = 8
F32 = jnp.float32
BF16 = jnp.bfloat16
MESH_Y, MESH_C = 2, 1
ZM, Z1, X1 = 6, 2, 1
SPLIT = 2


def dot_nn(a, b):
    return lax.dot_general(a, b, (((1,), (0,)), ((), ())), preferred_element_type=F32)


def dot_nt(a, b):
    return lax.dot_general(a, b, (((1,), (1,)), ((), ())), preferred_element_type=F32)


def dot_tn(a, b):
    return lax.dot_general(a, b, (((0,), (0,)), ((), ())), preferred_element_type=F32)


def flip(value, axis, mask):
    pairs = [(i, i ^ mask) for i in range(lax.axis_size(axis))]
    return lax.ppermute(value, axis, pairs)


def pick(flag, when_one, when_zero):
    return jnp.where(flag == 1, when_one, when_zero)


def call(
    body, outs, ins, scratch, flops, moved, exps=0, grid=None, in_specs=None, out_specs=None,
    vmem=56,
):
    spaces = {"v": pltpu.VMEM, "s": pltpu.SMEM, "a": pl.ANY}
    if in_specs is None:
        in_specs = [pl.BlockSpec(memory_space=spaces[kind]) for kind, _ in ins]
        out_specs = [pl.BlockSpec(memory_space=pltpu.VMEM) for _ in outs]
    kwargs = {} if grid is None else {"grid": grid}
    return pl.pallas_call(
        body,
        out_shape=[jax.ShapeDtypeStruct(shape, kind) for shape, kind in outs],
        in_specs=in_specs,
        out_specs=out_specs,
        scratch_shapes=scratch,
        cost_estimate=pl.CostEstimate(flops=flops, bytes_accessed=moved, transcendentals=exps),
        compiler_params=pltpu.CompilerParams(vmem_limit_bytes=vmem << 20),
        **kwargs,
    )(*[value for _, value in ins])


def run_copies(copies):
    for copy in copies:
        copy.start()
    for copy in copies:
        copy.wait()


def turned(values, cosine, signed_sine):
    lane = lax.broadcasted_iota(jnp.int32, values.shape, 1)
    ahead = pltpu.roll(values, 128 - HEAD // 2, 1)
    behind = pltpu.roll(values, HEAD // 2, 1)
    partner = jnp.where(lane % HEAD < HEAD // 2, ahead, behind)
    return values * cosine + partner * signed_sine


def bits(count):
    return [tuple((i >> (count - 1 - j)) & 1 for j in range(count)) for i in range(1 << count)]


def place_of(info, bx, q):
    z = info[3] ^ (q >> 1) ^ (3 * (q & 1))
    return z * 2 + (info[4] ^ bx)


def even_of(info):
    return (info[3] & 1) ^ info[1]


def block_of(info, t):
    return t ^ info[0] ^ (info[3] >> 1) ^ even_of(info)


def column_of(info, by, other):
    block = (info[0] ^ by) * 2 + (info[1] ^ other)
    return pl.multiple_of(block * 256, 256)


def source_of(parts, by, bx, q):
    own, over_x, over_y, corner_y, corner_x = parts
    if by == 0:
        return (own, over_x)[bx].at[q]
    if bx == 0:
        return over_y.at[q]
    split = corner_y.shape[0]
    return corner_y.at[q] if q < split else corner_x.at[q - split]


def put(outs, by, bx, q, rows, value):
    send_x, send_y, keep_x, keep_y, own = outs
    split = keep_x.shape[0]
    if by and bx:
        spot = (send_y, q) if q < split else (send_x, q - split)
    elif by:
        spot = (send_y, split + q) if q < split else (keep_y, q - split)
    elif bx:
        spot = (keep_x, q) if q < split else (send_x, 4 - split + q - split)
    else:
        spot = (own, q)
    spot[0][spot[1], rows, :] = value


def put_lanes(outs, by, bx, q, rows, lanes, value):
    class Cut:
        def __init__(self, ref):
            self.ref = ref
            self.shape = ref.shape

        def __setitem__(self, spot, content):
            self.ref[spot[0], spot[1], lanes] = content

    put(tuple(Cut(ref) for ref in outs), by, bx, q, rows, value)


def turn_tables(length):
    half = HEAD // 2
    steps = np.arange(half, dtype=np.float32) * np.float32(2.0)
    frequency = np.power(np.float32(10000.0), -steps / np.float32(HEAD), dtype=np.float32)
    angles = (np.arange(length, dtype=np.float32)[:, None] * frequency[None, :]).astype(np.float64)
    cosine = np.tile(np.cos(angles), (1, 4))
    sine = np.tile(np.concatenate([-np.sin(angles), np.sin(angles)], axis=1), (1, 2))
    return jnp.asarray(cosine.astype(np.float32)), jnp.asarray(sine.astype(np.float32))


def pack_body(*refs):
    out = refs[-1]
    at = 0
    for ref in refs[:-1]:
        if len(ref.shape) == 2:
            out[at] = ref[...]
            at += 1
        else:
            out[at : at + ref.shape[0]] = ref[...]
            at += ref.shape[0]


def piece_of(info, t, own, over_y, core):
    near = (t & 1) == info[1]
    mine = jnp.where(near, own[info[0]], core[0])
    other = jnp.where(near, over_y[...], core[1])
    return jnp.where((t >> 1) == info[0], mine, other)


def attn_copies(info, parts, w, sem):
    copies = []
    for by, bx in bits(2):
        for q in range(4):
            copies.append(pltpu.make_async_copy(
                source_of(parts, by, bx, q), w.at[by, place_of(info, bx, q)],
                sem.at[len(copies)]))
    return copies


def qkv_body(*refs):
    info, x_parts, fv_parts, cosine, sine = refs[0], refs[1:4], refs[4:7], refs[7], refs[8]
    parts = refs[9:14]
    x, h1, q, k, b, gains, w, sem = refs[14:]
    run_copies(attn_copies(info, parts, w, sem))
    rows = 128
    width = w.shape[3]
    model = x.shape[1]
    for j in range(2):
        pair = w[0, :, 3 * rows : 3 * rows + 16, j * rows : (j + 1) * rows]
        row = jnp.concatenate([pair[d, 0:1, :] for d in range(BLOCKS)], axis=1).astype(F32)
        gains[j : j + 1, :] = row
    gain = gains[0:1, :]

    def step(t, carry):
        at = pl.ds(pl.multiple_of(t * TILE, TILE), TILE)
        xb = piece_of(info, t, *x_parts)
        x[at, :] = xb
        first = piece_of(info, t, *fv_parts)
        xt = xb.astype(F32)
        inverse = lax.rsqrt(jnp.mean(xt * xt, axis=-1, keepdims=True) + EPSILON)
        h = (xt * inverse * gain).astype(BF16)
        h1[at, :] = h
        cos_t, sin_t = cosine[at, :], sine[at, :]
        quarters = [first[:, i * width : (i + 1) * width] for i in range(4)]
        for by in range(2):
            side = [jnp.where(info[1] == 1, quarters[2 * i + 1], quarters[2 * i]) for i in (0, 1)]
            blend = jnp.where((info[0] ^ by) == 1, side[1], side[0]).astype(F32)
            for n in range(3):
                weight = w[by, :, n * rows : (n + 1) * rows, :].reshape(model, width)
                acc = dot_nn(h, weight)
                cols = pl.ds(by * width, width)
                if n == 2:
                    b[at, cols] = (0.5 * acc + 0.5 * blend).astype(BF16)
                else:
                    halves = [
                        turned(acc[:, j : j + 128], cos_t, sin_t) for j in range(0, width, 128)
                    ]
                    both = jnp.concatenate(halves, axis=1).astype(BF16)
                    (q, k)[n][at, cols] = both * BF16(0.125) if n == 0 else both
        return carry

    lax.fori_loop(0, x.shape[0] // TILE, step, 0, unroll=True)


def split_heads(pair):
    lane = lax.broadcasted_iota(jnp.int32, pair.shape, 1)
    zero = jnp.zeros_like(pair)
    return jnp.concatenate(
        [jnp.where(lane < HEAD, pair, zero), jnp.where(lane < HEAD, zero, pair)], axis=0
    )


def join_heads(both):
    half = both.shape[0] // 2
    lane = lax.broadcasted_iota(jnp.int32, (half, both.shape[1]), 1)
    return jnp.where(lane < HEAD, both[:half], both[half:])


def hide_later(scores, fill):
    length, width = scores.shape
    key_at = lax.broadcasted_iota(jnp.int32, (TILE, width), 0)
    query_at = lax.broadcasted_iota(jnp.int32, (TILE, width), 1) % TILE
    last = jnp.where(key_at <= query_at, scores[length - TILE :], fill)
    if length == TILE:
        return last
    return jnp.concatenate([scores[: length - TILE], last], axis=0)


def attend_body(q, k, b, att, lse):
    for i in range(q.shape[0] // TILE):
        length = (i + 1) * TILE
        queries = split_heads(q[i * TILE : length, :])
        scores = hide_later(dot_nt(k[:length, :], queries), -1e30)
        top = jnp.max(scores, axis=0, keepdims=True)
        grown = jnp.exp(scores - top)
        total = jnp.sum(grown, axis=0, keepdims=True)
        logs = top + jnp.log(total)
        probs = (grown * (1.0 / total)).astype(BF16)
        att[i * TILE : length, :] = join_heads(dot_tn(probs, b[:length, :])).astype(BF16)
        lse[0, 0:1, i * TILE : length] = logs[:, :TILE]
        lse[0, 1:2, i * TILE : length] = logs[:, TILE:]


def attend_back_body(q, k, b, datt, lse, cosine, sine, dq, dk, dv, k_acc, v_acc):
    k_acc[...] = jnp.zeros_like(k_acc)
    v_acc[...] = jnp.zeros_like(v_acc)
    for i in range(q.shape[0] // TILE):
        length = (i + 1) * TILE
        at = slice(i * TILE, length)
        queries = split_heads(q[at, :])
        grads = split_heads(datt[at, :])
        keys = k[:length, :]
        logs = jnp.concatenate([lse[0, 0:1, at], lse[0, 1:2, at]], axis=1)
        probs = jnp.exp(hide_later(dot_nt(keys, queries) - logs, -1e30))
        grad_probs = dot_nt(b[:length, :], grads)
        delta = jnp.sum(probs * grad_probs, axis=0, keepdims=True)
        grad_scores = (probs * (grad_probs - delta)).astype(BF16)
        v_acc[:length, :] += dot_nn(probs.astype(BF16), grads)
        k_acc[:length, :] += dot_nn(grad_scores, queries)
        turned_back = turned(
            0.125 * join_heads(dot_tn(grad_scores, keys)), cosine[at, :], -sine[at, :]
        )
        dq[at, :] = turned_back.astype(BF16)
    for i in range(q.shape[0] // TILE):
        at = slice(i * TILE, (i + 1) * TILE)
        dk[at, :] = turned(k_acc[at, :], cosine[at, :], -sine[at, :]).astype(BF16)
        dv[at, :] = (0.5 * v_acc[at, :]).astype(BF16)


def out_copies(info, parts, wo, sem):
    first = parts[0].shape[1] - 128
    copies = []
    for by, bx, other, t in bits(4):
        row = pl.multiple_of(block_of(info, t) * 256 + (info[4] ^ bx) * 128, 128)
        copies.append(pltpu.make_async_copy(
            source_of(parts, by, bx, other * 2 + t).at[pl.ds(first, 128)],
            wo.at[pl.ds(row, 128), pl.ds(column_of(info, by, other), 256)],
            sem.at[len(copies)]))
    return copies


def out_body(*refs):
    info, att, parts, (part, wo, sem) = refs[0], refs[1], refs[2:7], refs[7:]
    run_copies(out_copies(info, parts, wo, sem))

    def step(t, carry):
        at = pl.ds(pl.multiple_of(t * TILE, TILE), TILE)
        part[at, :] = dot_nn(att[at, :], wo[...]).astype(BF16)
        return carry

    lax.fori_loop(0, att.shape[0] // TILE, step, 0, unroll=True)


def middle_of(x, part, recv, at):
    return x[at, :].astype(F32) + (part[at, :].astype(F32) + recv[at, :].astype(F32))


def out_back_body(*refs):
    info, gh2, gh2_recv, x, part, recv, gy, gains, att, down = refs[:10]
    parts = refs[10:15]
    datt, own_mid, gain_grad = refs[15:18]
    outs, (wo, gb, sem) = refs[18:23], refs[23:]
    down_rows = down.shape[3]
    copies = out_copies(info, parts, wo, sem)
    for copy in copies:
        copy.start()
    gain_grad[...] = jnp.zeros_like(gain_grad)

    def norm_step(t, carry):
        at = pl.ds(pl.multiple_of(t * TILE, TILE), TILE)
        middle = middle_of(x, part, recv, at)
        inverse = lax.rsqrt(jnp.mean(middle * middle, axis=-1, keepdims=True) + EPSILON)
        grad = gh2[at, :].astype(F32) + gh2_recv[at, :].astype(F32)
        scaled = grad * gains[1:2, :]
        share = inverse * inverse * inverse * jnp.mean(scaled * middle, axis=-1, keepdims=True)
        total = gy[at, :].astype(F32) + inverse * scaled - middle * share
        gb[at, :] = total.astype(BF16)
        gain_grad[0:1, :] += jnp.sum(grad * middle * inverse, axis=0, keepdims=True)

        @pl.when((t & 1) == info[1])
        def _():
            own_mid[t >> 1] = total

        return carry

    tiles = att.shape[0] // TILE
    lax.fori_loop(0, tiles, norm_step, 0, unroll=True)
    for copy in copies:
        copy.wait()

    def step(t, carry):
        at = pl.ds(pl.multiple_of(t * TILE, TILE), TILE)
        datt[at, :] = dot_nt(gb[at, :], wo[...]).astype(BF16)
        return carry

    lax.fori_loop(0, tiles, step, 0, unroll=True)
    for by, other in bits(2):
        grad = dot_tn(att[...], gb[:, pl.ds(column_of(info, by, other), 256)]).astype(BF16)
        for t in range(2):
            swap = block_of(info, t) == 1
            block = jnp.where(swap, grad[256:], grad[:256])
            for bx in range(2):
                q = other * 2 + t
                put(outs, by, bx, q, slice(0, down_rows), down[by, bx, q])
                put(outs, by, bx, q, slice(down_rows, down_rows + 128), jnp.where(
                    (info[4] ^ bx) == 1, block[128:], block[:128]))


def crossed(parts, by, bx, q):
    low, low_x, low_y, low_xy, high, high_x, high_y, high_xy = parts
    group = (low, low_x, low_y, low_xy) if q < 2 else (high, high_x, high_y, high_xy)
    return group[by * 2 + bx].at[q & 1]


def ffn_copies(info, first, parts, wgu, wd, sem):
    units = wd.shape[0]
    own = units // 2
    part = own // 2
    copies = []
    for by, bx in bits(2):
        for q in range(4):
            lane = pl.multiple_of(place_of(info, bx, q) * 128, 128)
            if first:
                source = parts[q].at[0] if by + bx == 0 else parts[4 + q].at[by * 2 + bx - 1]
            else:
                source = crossed(parts, by, bx, q)
            for up in range(2):
                copies.append(pltpu.make_async_copy(
                    source.at[pl.ds(0, own), pl.ds(up * 128, 128)],
                    wgu.at[pl.ds(up * units + by * own, own), pl.ds(lane, 128)],
                    sem.at[len(copies)]))
    for by, bx, other, t in bits(4):
        row = pl.multiple_of(block_of(info, t) * own + (info[4] ^ bx) * part, 16)
        q = other * 2 + t
        if first:
            source = source_of(parts[8:], by, bx, q).at[pl.ds(0, part)]
        else:
            source = crossed(parts, by, bx, q).at[pl.ds(own, part)]
        copies.append(pltpu.make_async_copy(
            source, wd.at[pl.ds(row, part), pl.ds(column_of(info, by, other), 256)],
            sem.at[len(copies)]))
    return copies


def ffn_body(first, *refs):
    info = refs[0]
    if first:
        x, part, recv, gains = refs[1:5]
        cot_parts, parts = refs[5:8], refs[8:21]
        h2, gy, gh2, res = refs[21:25]
        outs, refs = refs[25:30], refs[30:]
    else:
        h2, gy, gh2_in, res_in = refs[1:5]
        parts = refs[5:13]
        gh2, rkeep, rsend = refs[13:16]
        outs, down_grad, refs = refs[16:20], refs[20], refs[21:]
    hid, ggu, wgu, wd, sem = refs
    copies = ffn_copies(info, first, parts, wgu, wd, sem)
    for copy in copies:
        copy.start()
    units = wd.shape[0]
    tiles = h2.shape[0] // TILE
    if first:
        live = jnp.where(info[0] < info[5], 1.0, 0.0)

        def norm_step(t, carry):
            at = pl.ds(pl.multiple_of(t * TILE, TILE), TILE)
            middle = middle_of(x, part, recv, at)
            inverse = lax.rsqrt(jnp.mean(middle * middle, axis=-1, keepdims=True) + EPSILON)
            h2[at, :] = (middle * inverse * gains[1:2, :]).astype(BF16)
            gy[at, :] = (piece_of(info, t, *cot_parts).astype(F32) * live).astype(BF16)
            return carry

        lax.fori_loop(0, tiles, norm_step, 0, unroll=True)
    for copy in copies:
        copy.wait()

    def step(t, carry):
        at = pl.ds(pl.multiple_of(t * TILE, TILE), TILE)
        both = dot_nt(wgu[...], h2[at, :])
        gate, up = both[:units], both[units:]
        sig = 1.0 / (1.0 + jnp.exp(-gate))
        act = gate * sig
        hidden = (act * up).astype(BF16)
        hid[:, at] = hidden
        grad_hidden = dot_nt(wd[...], gy[at, :])
        ggu[:units, at] = (grad_hidden * up * (sig + act * (1.0 - sig))).astype(BF16)
        ggu[units:, at] = (grad_hidden * act).astype(BF16)
        grad_h = dot_tn(ggu[:, at], wgu[...])
        result = dot_tn(hidden, wd[...])
        if first:
            gh2[at, :] = grad_h.astype(BF16)
            res[at, :] = result.astype(BF16)
        else:
            gh2[at, :] = (gh2_in[at, :].astype(F32) + grad_h).astype(BF16)
            result = res_in[at, :].astype(F32) + result

            @pl.when((t & 1) == info[1])
            def _():
                rkeep[t >> 1] = result

            @pl.when((t & 1) != info[1])
            def _():
                rsend[t >> 1] = result.astype(BF16)

        return carry

    lax.fori_loop(0, tiles, step, 0, unroll=True)
    own = units // 2
    part = own // 2
    swap = info[4] == 1
    for q in (3, 2, 1, 0):
        z = info[3] ^ (q >> 1) ^ (3 * (q & 1))
        grad = dot_nn(ggu[...], h2[:, pl.ds(pl.multiple_of(z * 256, 256), 256)]).astype(BF16)
        lo, hi = grad[:, :128], grad[:, 128:]
        for bx, side in ((0, jnp.where(swap, hi, lo)), (1, jnp.where(swap, lo, hi))):
            for by, up in bits(2):
                lanes = slice(up * 128, up * 128 + 128)
                piece = side[up * units + by * own : up * units + (by + 1) * own]
                if first:
                    put_lanes(outs, by, bx, q, slice(0, own), lanes, piece)
                else:
                    outs[q][bx * 2 + by, :, lanes] = piece
    for by, other in bits(2):
        grad = dot_nn(hid[...], gy[:, pl.ds(column_of(info, by, other), 256)]).astype(BF16)
        for t in range(2):
            block = jnp.where(block_of(info, t) == 1, grad[own:], grad[:own])
            for bx in range(2):
                q = other * 2 + t
                piece = jnp.where((info[4] ^ bx) == 1, block[part:], block[:part])
                if first:
                    put(outs, by, bx, q, slice(own, own + part), piece)
                else:
                    down_grad[by, bx, q] = piece


def qkv_grad_body(by, *refs):
    info, dq, dk, dv, h1, gains, gain_grad = refs[:7]
    parts, refs = (refs[7:10], refs[10:]) if by else (refs[7:9], refs[9:])
    outs, (w, acc, sem) = refs[:3], refs[3:]
    copies = []
    for bx in range(2):
        for q in range(4):
            if by == 0 or bx == 0:
                source = parts[bx].at[q]
            else:
                split = parts[1].shape[0]
                source = parts[1].at[q] if q < split else parts[2].at[q - split]
            copies.append(pltpu.make_async_copy(
                source, w.at[place_of(info, bx, q)], sem.at[len(copies)]))
    for copy in copies:
        copy.start()
    width = w.shape[2]

    def spot(bx, q):
        if by:
            diagonal, send, keep = outs
            split = send.shape[0] // 2
            if q < split:
                return send, q if bx else split + q
            return (diagonal if bx else keep), q - split
        send, keep, own = outs
        split = keep.shape[0]
        if not bx:
            return own, q
        return (keep, q) if q < split else (send, q - split)

    waiting = True
    ones = jnp.ones((8, 3 * width), BF16)
    three = jnp.concatenate([dq[...], dk[...], dv[...]], axis=1)
    for q in (3, 2, 1, 0):
        z = info[3] ^ (q >> 1) ^ (3 * (q & 1))
        at = pl.ds(pl.multiple_of(z * 256, 256), 256)
        grad = dot_tn(h1[:, at], three)
        if waiting:
            for copy in copies:
                copy.wait()
            waiting = False
        weight = jnp.concatenate(
            [w[pl.ds(z * 2, 2), n * 128 : (n + 1) * 128, :].reshape(256, width)
             for n in range(3)], axis=1)
        shares = dot_nt(ones, (grad * weight.astype(F32)).astype(BF16))
        acc[:, at] = shares / gains[0:1, at]
        grad = grad.astype(BF16)
        for bx in range(2):
            part = jnp.where((info[4] ^ bx) == 1, grad[128:], grad[:128])
            ref, i = spot(bx, q)
            for n in range(3):
                ref[i, n * 128 : (n + 1) * 128, :] = part[:, n * width : (n + 1) * width]
    for bx in range(2):
        for q in range(4):
            at = pl.ds(pl.multiple_of(place_of(info, bx, q) * 128, 128), 128)
            row = jnp.concatenate([acc[0:1, at], gain_grad[0:1, at]], axis=1)
            ref, i = spot(bx, q)
            ref[i, 384:400, :] = jnp.broadcast_to(row, (16, 256)).astype(BF16)


def qkv_back_body(*refs):
    info, grads = refs[0], (refs[1:4], refs[4:7])
    parts = refs[7:12]
    gkeep, gsend, w, sem = refs[12:]
    run_copies(attn_copies(info, parts, w, sem))
    width = w.shape[3]
    model = gkeep.shape[2]

    def step(t, carry):
        at = pl.ds(pl.multiple_of(t * TILE, TILE), TILE)
        grad_h = jnp.zeros((TILE, model), F32)
        for by in range(2):
            for n in range(3):
                weight = w[by, :, n * 128 : (n + 1) * 128, :].reshape(model, width)
                grad_h = grad_h + dot_nt(grads[by][n][at, :], weight)

        @pl.when((t & 1) == info[1])
        def _():
            gkeep[t >> 1] = grad_h

        @pl.when((t & 1) != info[1])
        def _():
            gsend[t >> 1] = grad_h.astype(BF16)

        return carry

    lax.fori_loop(0, gkeep.shape[0] * 2, step, 0, unroll=True)


def input_body(info, gkeep, grecv, x, own_mid, gains, keep, send):
    for half in range(2):
        at = pl.ds(pl.multiple_of((half * 2 + info[1]) * TILE, TILE), TILE)
        xt = x[at, :].astype(F32)
        grad = gkeep[half] + grecv[half].astype(F32)
        inverse = lax.rsqrt(jnp.mean(xt * xt, axis=-1, keepdims=True) + EPSILON)
        scaled = grad * gains[0:1, :]
        share = inverse * inverse * inverse * jnp.mean(scaled * xt, axis=-1, keepdims=True)
        total = own_mid[half] + inverse * scaled - xt * share

        @pl.when(info[0] == half)
        def _():
            keep[...] = total

        @pl.when(info[0] != half)
        def _():
            send[...] = total.astype(BF16)


def plus(*values):
    total = values[0].astype(F32)
    for value in values[1:]:
        total = total + value.astype(F32)
    return total


class Steps(dict):
    __getattr__ = dict.__getitem__
    __setattr__ = dict.__setitem__


def on_device(
    tokens, first_values, seq_counts, norm1_gain, query_weight, key_weight, value_weight,
    out_weight, norm2_gain, gate_weight, up_weight, down_weight, output_cotangent,
):
    slots, piece, model = tokens.shape
    length = piece * lax.axis_size("seq")
    wide = lax.axis_size("dp") // BLOCKS
    s = lax.axis_index("seq")
    place = lax.axis_index("dp")
    y, c = s // 2, s % 2
    d = place // wide
    z, x_at = d // 2, d % 2
    info = jnp.stack([y, c, d, z, x_at, seq_counts[0]]).astype(jnp.int32)
    even = (z & 1) ^ c

    def pregather(shard):
        step = 1
        while step < wide:
            other = flip(shard, "dp", step)
            bit = (place // step) % 2
            shard = pick(
                bit, jnp.concatenate([other, shard]), jnp.concatenate([shard, other]))
            step *= 2
        return shard

    def postscatter(total):
        step = wide // 2
        while step >= 1:
            half = total.shape[0] // 2
            bit = (place // step) % 2
            lo, hi = total[:half], total[half:]
            total = pick(bit, hi, lo) + flip(pick(bit, lo, hi), "dp", step)
            step //= 2
        return total

    def far(v):
        return flip(v, "dp", ZM * wide)

    def near(v):
        return flip(v, "dp", Z1 * wide)

    def over_x(v):
        return flip(v, "dp", X1 * wide)

    def over_y(v):
        return flip(v, "seq", MESH_Y)

    def over_core(v):
        return flip(v, "seq", MESH_C)

    def other_slot(block):
        return pick(y, block[0], block[1])

    def mine_of(low, high):
        return jnp.stack([pick(even, low[1], low[0]), pick(even, high[0], high[1])])

    def theirs_of(low, high):
        return jnp.stack([pick(even, low[0], low[1]), pick(even, high[1], high[0])])

    def own_slot(block, recv):
        return jnp.stack([pick(y, block[1], block[0]), recv])

    def pack(*parts):
        rows = parts[0].shape[-2]
        (out,) = call(
            pack_body, [((4, rows, 256), BF16)], [("v", part) for part in parts], [],
            1000, 1 << 20, vmem=8)
        return out

    local = model // 2
    width = local // 2
    v = Steps()
    v.cosine, v.sine = turn_tables(length)
    v.a0 = jnp.concatenate(
        [pregather(query_weight), pregather(key_weight), pregather(value_weight),
         jnp.pad(jnp.concatenate([pregather(norm1_gain), pregather(norm2_gain)])[None],
                 ((0, 15), (0, 0)))])
    attn_rows = v.a0.shape[0]
    down = pregather(down_weight)
    part_a = down.shape[0] * 192 // 352 // 16 * 16
    part_b = down.shape[0] - part_a
    whole = down.shape[0]
    ffn = jnp.concatenate([pregather(gate_weight).T, pregather(up_weight).T], axis=1)
    v.b0 = jnp.concatenate([ffn[part_a:whole], ffn[whole + part_a :]])[None]
    v.g0 = jnp.concatenate([ffn[:part_a], ffn[whole : whole + part_a], down[:part_a]])
    v.r0 = jnp.concatenate([down[part_a:], pregather(out_weight)])
    out_rows = v.r0.shape[0] - part_b
    v.t_send = other_slot(tokens)
    v.f_send = other_slot(first_values)
    v.c_send = other_slot(output_cotangent)
    v.tokens, v.firsts, v.cots = tokens, first_values, output_cotangent

    v.a0, v.t_send, v.b0 = lax.optimization_barrier(
        (v.a0, v.t_send, v.b0))
    v.ty, v.af, v.an = over_y(v.t_send), far(v.a0), near(v.a0)
    v.bx = over_x(v.b0)
    v.a0, v.af, v.an, v.ty, v.tokens, v.b0, v.bx, v.f_send, v.c_send, v.firsts, v.cots, v.r0, v.g0 = lax.optimization_barrier(
        (v.a0, v.af, v.an, v.ty, v.tokens, v.b0, v.bx, v.f_send, v.c_send, v.firsts, v.cots, v.r0, v.g0))
    v.fy, v.anf, v.rf = over_y(v.f_send), near(v.af), far(v.r0)
    v.bf0 = far(v.b0)
    v.tc = over_core(own_slot(v.tokens, v.ty))
    v.a0, v.af, v.an, v.anf, v.fy, v.tc, v.firsts, v.b0, v.bx, v.bf0, v.r0, v.rf, v.g0, v.c_send, v.cots = lax.optimization_barrier(
        (v.a0, v.af, v.an, v.anf, v.fy, v.tc, v.firsts, v.b0, v.bx, v.bf0, v.r0, v.rf, v.g0, v.c_send, v.cots))
    v.z = pack(v.a0, v.af, v.an, v.anf)
    v.zx, v.zy = over_x(v.z), over_y(v.z)
    v.rlow = jnp.stack([v.r0, v.rf])
    v.rhigh, v.gf = near(v.rlow), far(v.g0)
    v.fc = over_core(own_slot(v.firsts, v.fy))
    v.z, v.zx, v.zy, v.rlow, v.rhigh, v.g0, v.gf, v.fc, v.b0, v.bx, v.bf0, v.c_send, v.cots = lax.optimization_barrier(
        (v.z, v.zx, v.zy, v.rlow, v.rhigh, v.g0, v.gf, v.fc, v.b0, v.bx, v.bf0, v.c_send, v.cots))
    v.zu, v.zv = over_y(v.zx[:SPLIT]), over_x(v.zy[SPLIT:])
    v.rmine = mine_of(v.rlow, v.rhigh)
    v.rother = over_core(theirs_of(v.rlow, v.rhigh))
    v.b10 = over_y(jnp.concatenate([v.b0, v.bx]))
    v.glow = jnp.stack([v.g0, v.gf])
    v.ghigh = near(v.glow)
    v.z, v.zx, v.zy, v.zu, v.zv, v.rmine, v.rother, v.b0, v.bx, v.b10, v.bf0, v.glow, v.ghigh, v.c_send, v.cots = lax.optimization_barrier(
        (v.z, v.zx, v.zy, v.zu, v.zv, v.rmine, v.rother, v.b0, v.bx, v.b10, v.bf0, v.glow, v.ghigh, v.c_send, v.cots))
    v.r = pack(v.rmine, v.rother)
    v.rx, v.ry = over_x(v.r), over_y(v.r)
    v.b3 = jnp.concatenate([v.bx, v.b10])
    v.bf3, v.bn3 = far(v.b3), near(v.b3)
    glow, ghigh = v.glow[:, 2 * part_a :], v.ghigh[:, 2 * part_a :]
    v.gmine, v.gother = mine_of(glow, ghigh), over_core(theirs_of(glow, ghigh))

    def anywhere(*arrays):
        return [("a", array) for array in arrays]

    def values(*arrays):
        return [("v", array) for array in arrays]

    square = ((length, model), BF16)
    tall = ((length, local), BF16)
    tile = (2, piece, model)
    w_scratch = pltpu.VMEM((2, BLOCKS, attn_rows, width), BF16)
    sem16 = pltpu.SemaphoreType.DMA((16,))
    narrow = 2 * length * model * local
    v.x, v.h1, v.q, v.k, v.b, v.gains = call(
        qkv_body, [square, square, tall, tall, tall, ((8, model), F32)],
        [("s", info)] + values(v.tokens, v.ty, v.tc, v.firsts, v.fy, v.fc, v.cosine, v.sine) + anywhere(v.z, v.zx, v.zy, v.zu, v.zv),
        [w_scratch, sem16], 3 * narrow, 14 << 20, vmem=26,
    )
    v.x, v.h1, v.q, v.k, v.b, v.gains, v.r, v.rx, v.ry, v.b0, v.b3, v.bf0, v.bf3, v.bn3, v.glow, v.ghigh, v.gmine, v.gother, v.c_send, v.cots = lax.optimization_barrier(
        (v.x, v.h1, v.q, v.k, v.b, v.gains, v.r, v.rx, v.ry, v.b0, v.b3, v.bf0, v.bf3, v.bn3, v.glow, v.ghigh, v.gmine, v.gother, v.c_send, v.cots))
    v.ru, v.rv = over_y(v.rx[:SPLIT]), over_x(v.ry[SPLIT:])
    v.gl = jnp.concatenate([v.glow[:, : 2 * part_a], v.gmine], axis=1)
    v.gh = jnp.concatenate([v.ghigh[:, : 2 * part_a], v.gother], axis=1)
    v.glx, v.ghy = over_x(v.gl), over_y(v.gh)
    v.bnf3 = near(v.bf3)
    head_specs = [pl.BlockSpec((length, 128), lambda i: (0, i))] * 3
    lse_spec = pl.BlockSpec((1, 2, length), lambda i: (i, 0, 0))
    pairs = local // 128
    v.att, v.lse = call(
        attend_body, [tall, ((pairs, 2, length), F32)], values(v.q, v.k, v.b), [],
        4 * length * length * local, 4 << 20, length * length * pairs * 2, vmem=20,
        grid=(pairs,), in_specs=head_specs, out_specs=[head_specs[0], lse_spec],
    )
    v.att, v.lse, v.r, v.rx, v.ry, v.ru, v.rv, v.gl, v.glx, v.gh, v.ghy, v.bnf3, v.c_send, v.bf0, v.b0 = lax.optimization_barrier(
        (v.att, v.lse, v.r, v.rx, v.ry, v.ru, v.rv, v.gl, v.glx, v.gh, v.ghy, v.bnf3, v.c_send, v.bf0, v.b0))
    v.cy = over_y(v.c_send)
    v.bnf0, v.bn0 = near(v.bf0), near(v.b0)
    (v.part,) = call(
        out_body, [square], [("s", info)] + values(v.att) + anywhere(v.r, v.rx, v.ry, v.ru, v.rv),
        [pltpu.VMEM((local, model), BF16), sem16], narrow, 5 << 20, vmem=12,
    )
    v.att, v.lse, v.r, v.rx, v.ry, v.ru, v.rv, v.part, v.cy, v.cots, v.gl, v.glx, v.gh, v.ghy, v.b0, v.b3, v.bf0, v.bn0, v.bf3, v.bn3, v.bnf0, v.bnf3 = lax.optimization_barrier(
        (v.att, v.lse, v.r, v.rx, v.ry, v.ru, v.rv, v.part, v.cy, v.cots, v.gl, v.glx, v.gh, v.ghy, v.b0, v.b3, v.bf0, v.bn0, v.bf3, v.bn3, v.bnf0, v.bnf3))
    v.precv, v.cc = over_core(v.part), over_core(own_slot(v.cots, v.cy))
    v.part, v.precv, v.cc, v.gl, v.glx, v.gh, v.ghy = lax.optimization_barrier(
        (v.part, v.precv, v.cc, v.gl, v.glx, v.gh, v.ghy))

    def five(rows):
        return [((count, rows, 256), BF16)
                for count in (2 * (4 - SPLIT), 2 * SPLIT, SPLIT, 4 - SPLIT, 4)]

    v.gly, v.glxy = over_y(v.gl), over_y(v.glx)
    v.ghx, v.ghxy = over_x(v.gh), over_x(v.ghy)
    def ffn_scratch(units):
        return [pltpu.VMEM((units, length), BF16), pltpu.VMEM((2 * units, length), BF16),
                pltpu.VMEM((2 * units, model), BF16), pltpu.VMEM((units, model), BF16),
                pltpu.SemaphoreType.DMA((48,))]

    ffn_flops = 36 * length * model
    v.h2, v.gy, v.gh2b, v.resb, v.bsx, v.bsy, v.bkx, v.bky, v.bown = call(
        functools.partial(ffn_body, True), [square] * 4 + five(3 * part_b),
        [("s", info)] + values(v.x, v.part, v.precv, v.gains, v.cots, v.cy, v.cc)
        + anywhere(v.b0, v.bf0, v.bn0, v.bnf0, v.b3, v.bf3, v.bn3, v.bnf3) + anywhere(v.r, v.rx, v.ry, v.ru, v.rv),
        ffn_scratch(4 * part_b), ffn_flops * 2 * part_b, 24 << 20, vmem=40,
    )
    v.h2, v.gy, v.gh2b, v.resb, v.bsx, v.bsy, v.bkx, v.bky, v.bown, v.gl, v.glx, v.gly, v.glxy, v.gh, v.ghx, v.ghy, v.ghxy = lax.optimization_barrier(
        (v.h2, v.gy, v.gh2b, v.resb, v.bsx, v.bsy, v.bkx, v.bky, v.bown, v.gl, v.glx, v.gly, v.glxy, v.gh, v.ghx, v.ghy, v.ghxy))
    v.brx, v.bry = over_x(v.bsx), over_y(v.bsy)
    quads = [((4, 2 * part_a, 256), BF16)] * 4 + [((2, 2, 4, part_a, 256), BF16)]
    (v.gh2, v.rkeep, v.rsend, v.n0, v.n1, v.n2, v.n3, v.dgrad) = call(
        functools.partial(ffn_body, False), [square, (tile, F32), (tile, BF16)] + quads,
        [("s", info)] + values(v.h2, v.gy, v.gh2b, v.resb)
        + anywhere(v.gl, v.glx, v.gly, v.glxy, v.gh, v.ghx, v.ghy, v.ghxy),
        ffn_scratch(4 * part_a), ffn_flops * 2 * part_a, 24 << 20, vmem=40,
    )
    v.gh2, v.rkeep, v.rsend, v.n0, v.n1, v.n2, v.n3, v.dgrad, v.brx, v.bry, v.bkx, v.bky, v.bown, v.part, v.precv = lax.optimization_barrier(
        (v.gh2, v.rkeep, v.rsend, v.n0, v.n1, v.n2, v.n3, v.dgrad, v.brx, v.bry, v.bkx, v.bky, v.bown, v.part, v.precv))

    def fold(name):
        v[name + "fx"] = plus(v[name + "kx"], v[name + "ry"][:SPLIT]).astype(BF16)
        v[name + "fy"] = plus(v[name + "ky"], v[name + "rx"][: 4 - SPLIT]).astype(BF16)

    def total_of(name):
        low = plus(v[name + "own"][:SPLIT], v[name + "ry"][SPLIT:], v[name + "rx2"])
        high = plus(v[name + "own"][SPLIT:], v[name + "rx"][4 - SPLIT :], v[name + "ry2"])
        return jnp.concatenate([low, high])

    def rows_out(name, total, first):
        v[name + "t"] = total
        v[name + "m"] = over_core(total[2:, first:].astype(BF16))

    def quarter(name, first, q):
        total, recv = v[name + "t"], v[name + "m"]
        rows = total[q >> 1, first:]
        other = recv[q >> 1].astype(F32)
        mine = pick(even, other, rows) if q in (0, 3) else pick(even, rows, other)
        return mine if first == 0 else jnp.concatenate([total[q, :first], mine])

    def owner_send(halves_of):
        return pick(y, halves_of[0], halves_of[1])

    def owner_keep(halves_of):
        return pick(y, halves_of[1], halves_of[0])

    def both_slots(keep, recv):
        return pick(y, jnp.stack([recv, keep]), jnp.stack([keep, recv]))

    def own_tokens(full):
        cut_up = full.reshape(2, 2, piece, full.shape[-1])
        return pick(c, cut_up[:, 1], cut_up[:, 0])

    v.gh2r = over_core(v.gh2)
    v.rrecv = over_core(v.rsend)
    fold("b")
    v.brx2, v.bry2 = over_x(v.bfx), over_y(v.bfy)
    v.nn3 = near(v.n3)
    (v.datt, v.mid, v.gain2,
     v.ssx, v.ssy, v.skx, v.sky, v.sown) = call(
        out_back_body, [tall, (tile, F32), ((8, model), F32)] + five(part_a + out_rows),
        [("s", info)] + values(v.gh2, v.gh2r, v.x, v.part, v.precv, v.gy, v.gains, v.att, v.dgrad) + anywhere(v.r, v.rx, v.ry, v.ru, v.rv),
        [pltpu.VMEM((local, model), BF16), pltpu.VMEM((length, model), BF16), sem16],
        2 * narrow, 20 << 20, vmem=56,
    )
    v.datt, v.mid, v.gain2, v.ssx, v.ssy, v.skx, v.sky, v.sown, v.bown, v.brx, v.bry, v.brx2, v.bry2, v.n0, v.n1, v.n2, v.nn3, v.rkeep, v.rrecv, v.part, v.precv = lax.optimization_barrier(
        (v.datt, v.mid, v.gain2, v.ssx, v.ssy, v.skx, v.sky, v.sown, v.bown, v.brx, v.bry, v.brx2, v.bry2, v.n0, v.n1, v.n2, v.nn3, v.rkeep, v.rrecv, v.part, v.precv))
    v.srx, v.sry = over_x(v.ssx), over_y(v.ssy)
    v.n1 = plus(v.n1, v.nn3).astype(BF16)
    v.nf1, v.nn2 = far(v.n1[2:]), near(v.n2)
    rows_out("b", total_of("b"), 2 * part_b)

    live_now = jnp.where(y < seq_counts[0], 1.0, 0.0)
    middle_own = own_tokens(v.x).astype(F32) + plus(
        own_tokens(v.part), own_tokens(v.precv))
    result = (live_now * (middle_own + plus(v.rkeep, v.rrecv))).astype(BF16)
    v.okeep, v.osend = owner_keep(result), owner_send(result)
    def attend_back(side):
        first = side * (pairs // 2)
        column = pl.BlockSpec((length, 128), lambda i: (0, i + first))
        table = pl.BlockSpec((length, 128), lambda i: (0, 0))
        sums = pl.BlockSpec((1, 2, length), lambda i: (i + first, 0, 0))
        target = pl.BlockSpec((length, 128), lambda i: (0, i))
        return call(
            attend_back_body, [((length, width), BF16)] * 3,
            values(v.q, v.k, v.b, v.datt, v.lse, v.cosine, v.sine),
            [pltpu.VMEM((length, 128), F32), pltpu.VMEM((length, 128), F32)],
            5 * length * length * local, 4 << 20, length * length * pairs, vmem=26,
            grid=(pairs // 2,), in_specs=[column] * 4 + [sums, table, table],
            out_specs=[target] * 3,
        )

    def attn_grads(side):
        counts = (4 - SPLIT, 2 * SPLIT, 4 - SPLIT) if side else (4 - SPLIT, SPLIT, 4)
        arrays = (v.zy, v.zu, v.zv) if side else (v.z, v.zx)
        return call(
            functools.partial(qkv_grad_body, side),
            [((count, attn_rows, width), BF16) for count in counts],
            [("s", info)] + values(*(v.grads1 if side else v.grads0), v.h1, v.gains, v.gain2)
            + anywhere(*arrays),
            [pltpu.VMEM((BLOCKS, attn_rows, width), BF16), pltpu.VMEM((8, model), F32),
             pltpu.SemaphoreType.DMA((8,))], 3 * narrow // 2, 7 << 20, vmem=24,
        )

    v.grads1 = attend_back(1)
    v.qdx, v.qsy, v.qky = attn_grads(1)
    v.grads1, v.qdx, v.qsy, v.qky, v.q, v.k, v.b, v.datt, v.srx, v.sry, v.skx, v.sky, v.sown, v.n0, v.n1, v.nf1, v.nn2, v.bt, v.bm, v.okeep, v.osend = lax.optimization_barrier(
        (v.grads1, v.qdx, v.qsy, v.qky, v.q, v.k, v.b, v.datt, v.srx, v.sry, v.skx, v.sky, v.sown, v.n0, v.n1, v.nf1, v.nn2, v.bt, v.bm, v.okeep, v.osend))
    v.qry, v.qrd = over_y(v.qsy), over_x(v.qdx)
    fold("s")
    v.srx2 = over_x(v.sfx)
    v.nf0 = far(v.n1[:2])
    v.bzn = near(jnp.stack([quarter("b", 2 * part_b, 2), quarter("b", 2 * part_b, 3)]).astype(BF16))
    v.grads0 = attend_back(0)
    v.qsx, v.qkx, v.qown = attn_grads(0)
    v.grads0, v.grads1, v.qsx, v.qkx, v.qown, v.qry, v.qrd, v.qky, v.srx, v.sry, v.srx2, v.sfy, v.sown, v.n0, v.nf0, v.nf1, v.nn2, v.bzn, v.bt, v.bm, v.okeep, v.osend = lax.optimization_barrier(
        (v.grads0, v.grads1, v.qsx, v.qkx, v.qown, v.qry, v.qrd, v.qky, v.srx, v.sry, v.srx2, v.sfy, v.sown, v.n0, v.nf0, v.nf1, v.nn2, v.bzn, v.bt, v.bm, v.okeep, v.osend))
    v.qrx = over_x(v.qsx)
    v.sry2 = over_y(v.sfy)
    v.nt0 = plus(v.n0[:2], v.nf0, v.nn2[:2])
    v.nx = over_x(plus(v.n0[2:], v.nf1, v.nn2[2:]).astype(BF16))
    v.bt0 = plus(quarter("b", 2 * part_b, 0), v.bzn[0])
    v.bzf = far(plus(quarter("b", 2 * part_b, 1), v.bzn[1]).astype(BF16))
    v.orecv = over_y(v.osend)
    v.gkeep, v.gsend = call(
        qkv_back_body, [(tile, F32), (tile, BF16)],
        [("s", info)] + values(*v.grads0, *v.grads1) + anywhere(v.z, v.zx, v.zy, v.zu, v.zv), [w_scratch, sem16],
        3 * narrow, 14 << 20, vmem=18,
    )
    v.gkeep, v.gsend, v.qry, v.qrd, v.qky, v.qrx, v.qkx, v.qown, v.bt0, v.bzf, v.nt0, v.nx, v.srx, v.sry, v.srx2, v.sry2, v.sown, v.grads0, v.grads1, v.okeep, v.orecv = lax.optimization_barrier(
        (v.gkeep, v.gsend, v.qry, v.qrd, v.qky, v.qrx, v.qkx, v.qown, v.bt0, v.bzf, v.nt0, v.nx, v.srx, v.sry, v.srx2, v.sry2, v.sown, v.grads0, v.grads1, v.okeep, v.orecv))
    output = both_slots(v.okeep, v.orecv)
    total_b = plus(v.bt0, v.bzf)
    v.grecv = over_core(v.gsend)
    v.qfx = plus(v.qkx, v.qry[:SPLIT]).astype(BF16)
    v.qfy = plus(v.qky, v.qrd).astype(BF16)
    v.qrx2, v.qry2 = over_x(v.qfx), over_y(v.qfy)
    rows_out("s", total_of("s"), 0)
    v.nt0 = plus(v.nt0, v.nx)
    v.ny = over_y(v.nt0[1].astype(BF16))
    v.ikeep, v.isend = call(
        input_body, [((piece, model), F32), ((piece, model), BF16)],
        [("s", info)] + values(v.gkeep, v.grecv, v.x, v.mid, v.gains), [], 1000, 8 << 20, vmem=16,
    )
    v.ikeep, v.isend, v.qrx, v.qry, v.qrx2, v.qry2, v.qown, v.st, v.sm, v.nt0, v.ny, v.grads0, v.grads1 = lax.optimization_barrier(
        (v.ikeep, v.isend, v.qrx, v.qry, v.qrx2, v.qry2, v.qown, v.st, v.sm, v.nt0, v.ny, v.grads0, v.grads1))
    total_a = plus(v.nt0[0], v.ny)
    low = plus(v.qown[:SPLIT], v.qry[SPLIT:], v.qrx2)
    high = plus(v.qown[SPLIT:], v.qrx, v.qry2)
    v.qt = jnp.concatenate([low, high])
    v.qz, v.sz = near(v.qt[3].astype(BF16)), near(quarter("s", 0, 3).astype(BF16))
    v.irecv = over_y(v.isend)
    cuts = [grads[2].reshape(2, 2, piece, width) for grads in (v.grads0, v.grads1)]
    dv_keep = [pick(c, cut[:, 1], cut[:, 0]) for cut in cuts]
    dv_recv = over_core(
        jnp.concatenate([pick(c, cut[:, 0], cut[:, 1]) for cut in cuts], axis=-1))
    dv_recv = [dv_recv[..., :width], dv_recv[..., width:]]
    blocks = []
    for column_y, column_c in bits(2):
        side = y ^ column_y
        mine = pick(side, dv_keep[1], dv_keep[0])
        theirs = pick(side, dv_recv[1], dv_recv[0])
        blocks.append(pick(c ^ column_c, theirs, mine))
    grad_rows = jnp.concatenate(blocks, axis=-1)
    v.fkeep, v.fsend = owner_keep(grad_rows), owner_send(grad_rows)
    v.qt, v.qz, v.st, v.sm, v.sz, v.irecv, v.ikeep, v.fkeep, v.fsend = lax.optimization_barrier(
        (v.qt, v.qz, v.st, v.sm, v.sz, v.irecv, v.ikeep, v.fkeep, v.fsend))
    v.qzf = far(plus(v.qt[1], v.qz).astype(BF16))
    v.szf = far(plus(quarter("s", 0, 1), v.sz).astype(BF16))
    v.qzn = near(v.qt[2].astype(BF16))
    v.szn = near(quarter("s", 0, 2).astype(BF16))
    v.frecv = over_y(v.fsend)
    v.qt0, v.st0 = v.qt[0], quarter("s", 0, 0)
    grad_input = both_slots(v.ikeep, v.irecv.astype(F32))
    v.qt0, v.st0, v.qzf, v.szf, v.qzn, v.szn, v.fkeep, v.frecv = lax.optimization_barrier(
        (v.qt0, v.st0, v.qzf, v.szf, v.qzn, v.szn, v.fkeep, v.frecv))
    total = plus(v.qt0, v.qzf, v.qzn)
    gain_total = total[384]
    gain_share = jnp.broadcast_to(gain_total[None, :128], (8, 128))
    gain_sum = gain_total[:128] + over_core(gain_share)[0] + (
        over_y(gain_share)[0] + flip(gain_share, "seq", MESH_Y | MESH_C)[0])
    total_s = plus(v.st0, v.szf, v.szn)
    grad_first = both_slots(v.fkeep, v.frecv).astype(F32)

    def weave(lanes):
        pieces = [total_a[:part_a, lanes], total_b[:part_b, lanes],
                  total_a[part_a:, lanes], total_b[part_b : 2 * part_b, lanes]]
        return jnp.concatenate(pieces).T

    return (
        output,
        grad_input,
        grad_first,
        postscatter(gain_sum),
        postscatter(total[:128]),
        postscatter(total[128:256]),
        postscatter(total[256:384]),
        postscatter(total_s[part_a:]),
        postscatter(gain_total[128:]),
        postscatter(weave(slice(0, 128))),
        postscatter(weave(slice(128, 256))),
        postscatter(jnp.concatenate([total_s[:part_a], total_b[2 * part_b :]])),
    )


def solution(mesh):
    cut = P("dp", "seq")
    flat = P("dp")
    whole = P("dp", "seq", None)
    return jax.shard_map(
        on_device,
        mesh=mesh,
        in_specs=(whole, whole, flat, flat, cut, cut, cut, cut, flat, cut, cut, cut, whole),
        out_specs=(whole, whole, whole, flat, cut, cut, cut, cut, flat, cut, cut, cut),
        check_vma=False,
    )
```

```python
import functools

import jax
import jax.numpy as jnp
import numpy as np
from jax import lax
from jax.experimental import pallas as pl
from jax.experimental.pallas import tpu as pltpu
from jax.sharding import PartitionSpec as P

HEAD = 64
EPSILON = 1e-06
TILE = 256
BLOCKS = 8
F32 = jnp.float32
BF16 = jnp.bfloat16
MESH_Y, MESH_C = 2, 1
ZM, Z1, X1 = 6, 2, 1
SPLIT = 2


def dot_nn(a, b):
    return lax.dot_general(a, b, (((1,), (0,)), ((), ())), preferred_element_type=F32)


def dot_nt(a, b):
    return lax.dot_general(a, b, (((1,), (1,)), ((), ())), preferred_element_type=F32)


def dot_tn(a, b):
    return lax.dot_general(a, b, (((0,), (0,)), ((), ())), preferred_element_type=F32)


def flip(value, axis, mask):
    pairs = [(i, i ^ mask) for i in range(lax.axis_size(axis))]
    return lax.ppermute(value, axis, pairs)


def pick(flag, when_one, when_zero):
    return jnp.where(flag == 1, when_one, when_zero)


def call(
    body, outs, ins, scratch, flops, moved, exps=0, grid=None, in_specs=None, out_specs=None,
    vmem=56,
):
    spaces = {"v": pltpu.VMEM, "s": pltpu.SMEM, "a": pl.ANY}
    if in_specs is None:
        in_specs = [pl.BlockSpec(memory_space=spaces[kind]) for kind, _ in ins]
        out_specs = [pl.BlockSpec(memory_space=pltpu.VMEM) for _ in outs]
    kwargs = {} if grid is None else {"grid": grid}
    return pl.pallas_call(
        body,
        out_shape=[jax.ShapeDtypeStruct(shape, kind) for shape, kind in outs],
        in_specs=in_specs,
        out_specs=out_specs,
        scratch_shapes=scratch,
        cost_estimate=pl.CostEstimate(flops=flops, bytes_accessed=moved, transcendentals=exps),
        compiler_params=pltpu.CompilerParams(vmem_limit_bytes=vmem << 20),
        **kwargs,
    )(*[value for _, value in ins])


def run_copies(copies):
    for copy in copies:
        copy.start()
    for copy in copies:
        copy.wait()


def turned(values, cosine, signed_sine):
    lane = lax.broadcasted_iota(jnp.int32, values.shape, 1)
    ahead = pltpu.roll(values, 128 - HEAD // 2, 1)
    behind = pltpu.roll(values, HEAD // 2, 1)
    partner = jnp.where(lane % HEAD < HEAD // 2, ahead, behind)
    return values * cosine + partner * signed_sine


def bits(count):
    return [tuple((i >> (count - 1 - j)) & 1 for j in range(count)) for i in range(1 << count)]


def place_of(info, bx, q):
    z = info[3] ^ (q >> 1) ^ (3 * (q & 1))
    return z * 2 + (info[4] ^ bx)


def even_of(info):
    return (info[3] & 1) ^ info[1]


def block_of(info, t):
    return t ^ info[0] ^ (info[3] >> 1) ^ even_of(info)


def column_of(info, by, other):
    block = (info[0] ^ by) * 2 + (info[1] ^ other)
    return pl.multiple_of(block * 256, 256)


def source_of(parts, by, bx, q):
    own, over_x, over_y, corner_y, corner_x = parts
    if by == 0:
        return (own, over_x)[bx].at[q]
    if bx == 0:
        return over_y.at[q]
    split = corner_y.shape[0]
    return corner_y.at[q] if q < split else corner_x.at[q - split]


def put(outs, by, bx, q, rows, value):
    send_x, send_y, keep_x, keep_y, own = outs
    split = keep_x.shape[0]
    if by and bx:
        spot = (send_y, q) if q < split else (send_x, q - split)
    elif by:
        spot = (send_y, split + q) if q < split else (keep_y, q - split)
    elif bx:
        spot = (keep_x, q) if q < split else (send_x, 4 - split + q - split)
    else:
        spot = (own, q)
    spot[0][spot[1], rows, :] = value


def put_lanes(outs, by, bx, q, rows, lanes, value):
    class Cut:
        def __init__(self, ref):
            self.ref = ref
            self.shape = ref.shape

        def __setitem__(self, spot, content):
            self.ref[spot[0], spot[1], lanes] = content

    put(tuple(Cut(ref) for ref in outs), by, bx, q, rows, value)


def turn_tables(length):
    half = HEAD // 2
    steps = np.arange(half, dtype=np.float32) * np.float32(2.0)
    frequency = np.power(np.float32(10000.0), -steps / np.float32(HEAD), dtype=np.float32)
    angles = (np.arange(length, dtype=np.float32)[:, None] * frequency[None, :]).astype(np.float64)
    cosine = np.tile(np.cos(angles), (1, 4))
    sine = np.tile(np.concatenate([-np.sin(angles), np.sin(angles)], axis=1), (1, 2))
    return jnp.asarray(cosine.astype(np.float32)), jnp.asarray(sine.astype(np.float32))


def pack_body(*refs):
    out = refs[-1]
    at = 0
    for ref in refs[:-1]:
        if len(ref.shape) == 2:
            out[at] = ref[...]
            at += 1
        else:
            out[at : at + ref.shape[0]] = ref[...]
            at += ref.shape[0]


def piece_of(info, t, own, over_y, core):
    near = (t & 1) == info[1]
    mine = jnp.where(near, own[info[0]], core[0])
    other = jnp.where(near, over_y[...], core[1])
    return jnp.where((t >> 1) == info[0], mine, other)


def attn_copies(info, parts, w, sem):
    copies = []
    for by, bx in bits(2):
        for q in range(4):
            copies.append(pltpu.make_async_copy(
                source_of(parts, by, bx, q), w.at[by, place_of(info, bx, q)],
                sem.at[len(copies)]))
    return copies


def qkv_body(*refs):
    info, x_parts, fv_parts, cosine, sine = refs[0], refs[1:4], refs[4:7], refs[7], refs[8]
    parts = refs[9:14]
    x, h1, q, k, b, gains, w, sem = refs[14:]
    run_copies(attn_copies(info, parts, w, sem))
    rows = 128
    width = w.shape[3]
    model = x.shape[1]
    for j in range(2):
        pair = w[0, :, 3 * rows : 3 * rows + 16, j * rows : (j + 1) * rows]
        row = jnp.concatenate([pair[d, 0:1, :] for d in range(BLOCKS)], axis=1).astype(F32)
        gains[j : j + 1, :] = row
    gain = gains[0:1, :]

    def step(t, carry):
        at = pl.ds(pl.multiple_of(t * TILE, TILE), TILE)
        xb = piece_of(info, t, *x_parts)
        x[at, :] = xb
        first = piece_of(info, t, *fv_parts)
        xt = xb.astype(F32)
        inverse = lax.rsqrt(jnp.mean(xt * xt, axis=-1, keepdims=True) + EPSILON)
        h = (xt * inverse * gain).astype(BF16)
        h1[at, :] = h
        cos_t, sin_t = cosine[at, :], sine[at, :]
        quarters = [first[:, i * width : (i + 1) * width] for i in range(4)]
        for by in range(2):
            side = [jnp.where(info[1] == 1, quarters[2 * i + 1], quarters[2 * i]) for i in (0, 1)]
            blend = jnp.where((info[0] ^ by) == 1, side[1], side[0]).astype(F32)
            for n in range(3):
                weight = w[by, :, n * rows : (n + 1) * rows, :].reshape(model, width)
                acc = dot_nn(h, weight)
                cols = pl.ds(by * width, width)
                if n == 2:
                    b[at, cols] = (0.5 * acc + 0.5 * blend).astype(BF16)
                else:
                    halves = [
                        turned(acc[:, j : j + 128], cos_t, sin_t) for j in range(0, width, 128)
                    ]
                    both = jnp.concatenate(halves, axis=1).astype(BF16)
                    (q, k)[n][at, cols] = both * BF16(0.125) if n == 0 else both
        return carry

    lax.fori_loop(0, x.shape[0] // TILE, step, 0, unroll=True)


def split_heads(pair):
    lane = lax.broadcasted_iota(jnp.int32, pair.shape, 1)
    zero = jnp.zeros_like(pair)
    return jnp.concatenate(
        [jnp.where(lane < HEAD, pair, zero), jnp.where(lane < HEAD, zero, pair)], axis=0
    )


def join_heads(both):
    half = both.shape[0] // 2
    lane = lax.broadcasted_iota(jnp.int32, (half, both.shape[1]), 1)
    return jnp.where(lane < HEAD, both[:half], both[half:])


def hide_later(scores, fill):
    length, width = scores.shape
    key_at = lax.broadcasted_iota(jnp.int32, (TILE, width), 0)
    query_at = lax.broadcasted_iota(jnp.int32, (TILE, width), 1) % TILE
    last = jnp.where(key_at <= query_at, scores[length - TILE :], fill)
    if length == TILE:
        return last
    return jnp.concatenate([scores[: length - TILE], last], axis=0)


def attend_body(q, k, b, att, lse):
    for i in range(q.shape[0] // TILE):
        length = (i + 1) * TILE
        queries = split_heads(q[i * TILE : length, :])
        scores = hide_later(dot_nt(k[:length, :], queries), -1e30)
        top = jnp.max(scores, axis=0, keepdims=True)
        grown = jnp.exp(scores - top)
        total = jnp.sum(grown, axis=0, keepdims=True)
        logs = top + jnp.log(total)
        probs = (grown * (1.0 / total)).astype(BF16)
        att[i * TILE : length, :] = join_heads(dot_tn(probs, b[:length, :])).astype(BF16)
        lse[0, 0:1, i * TILE : length] = logs[:, :TILE]
        lse[0, 1:2, i * TILE : length] = logs[:, TILE:]


def attend_back_body(q, k, b, datt, lse, cosine, sine, dq, dk, dv, k_acc, v_acc):
    k_acc[...] = jnp.zeros_like(k_acc)
    v_acc[...] = jnp.zeros_like(v_acc)
    for i in range(q.shape[0] // TILE):
        length = (i + 1) * TILE
        at = slice(i * TILE, length)
        queries = split_heads(q[at, :])
        grads = split_heads(datt[at, :])
        keys = k[:length, :]
        logs = jnp.concatenate([lse[0, 0:1, at], lse[0, 1:2, at]], axis=1)
        probs = jnp.exp(hide_later(dot_nt(keys, queries) - logs, -1e30))
        grad_probs = dot_nt(b[:length, :], grads)
        delta = jnp.sum(probs * grad_probs, axis=0, keepdims=True)
        grad_scores = (probs * (grad_probs - delta)).astype(BF16)
        v_acc[:length, :] += dot_nn(probs.astype(BF16), grads)
        k_acc[:length, :] += dot_nn(grad_scores, queries)
        turned_back = turned(
            0.125 * join_heads(dot_tn(grad_scores, keys)), cosine[at, :], -sine[at, :]
        )
        dq[at, :] = turned_back.astype(BF16)
    for i in range(q.shape[0] // TILE):
        at = slice(i * TILE, (i + 1) * TILE)
        dk[at, :] = turned(k_acc[at, :], cosine[at, :], -sine[at, :]).astype(BF16)
        dv[at, :] = (0.5 * v_acc[at, :]).astype(BF16)


def out_copies(info, parts, wo, sem):
    first = parts[0].shape[1] - 128
    copies = []
    for by, bx, other, t in bits(4):
        row = pl.multiple_of(block_of(info, t) * 256 + (info[4] ^ bx) * 128, 128)
        copies.append(pltpu.make_async_copy(
            source_of(parts, by, bx, other * 2 + t).at[pl.ds(first, 128)],
            wo.at[pl.ds(row, 128), pl.ds(column_of(info, by, other), 256)],
            sem.at[len(copies)]))
    return copies


def out_body(*refs):
    info, att, parts, (part, wo, sem) = refs[0], refs[1], refs[2:7], refs[7:]
    run_copies(out_copies(info, parts, wo, sem))

    def step(t, carry):
        at = pl.ds(pl.multiple_of(t * TILE, TILE), TILE)
        part[at, :] = dot_nn(att[at, :], wo[...]).astype(BF16)
        return carry

    lax.fori_loop(0, att.shape[0] // TILE, step, 0, unroll=True)


def middle_of(x, part, recv, at):
    return x[at, :].astype(F32) + (part[at, :].astype(F32) + recv[at, :].astype(F32))


def out_back_body(*refs):
    info, gh2, gh2_recv, x, part, recv, gy, gains, att, down = refs[:10]
    parts = refs[10:15]
    datt, own_mid, gain_grad = refs[15:18]
    outs, (wo, gb, sem) = refs[18:23], refs[23:]
    down_rows = down.shape[3]
    copies = out_copies(info, parts, wo, sem)
    for copy in copies:
        copy.start()
    gain_grad[...] = jnp.zeros_like(gain_grad)

    def norm_step(t, carry):
        at = pl.ds(pl.multiple_of(t * TILE, TILE), TILE)
        middle = middle_of(x, part, recv, at)
        inverse = lax.rsqrt(jnp.mean(middle * middle, axis=-1, keepdims=True) + EPSILON)
        grad = gh2[at, :].astype(F32) + gh2_recv[at, :].astype(F32)
        scaled = grad * gains[1:2, :]
        share = inverse * inverse * inverse * jnp.mean(scaled * middle, axis=-1, keepdims=True)
        total = gy[at, :].astype(F32) + inverse * scaled - middle * share
        gb[at, :] = total.astype(BF16)
        gain_grad[0:1, :] += jnp.sum(grad * middle * inverse, axis=0, keepdims=True)

        @pl.when((t & 1) == info[1])
        def _():
            own_mid[t >> 1] = total

        return carry

    tiles = att.shape[0] // TILE
    lax.fori_loop(0, tiles, norm_step, 0, unroll=True)
    for copy in copies:
        copy.wait()

    def step(t, carry):
        at = pl.ds(pl.multiple_of(t * TILE, TILE), TILE)
        datt[at, :] = dot_nt(gb[at, :], wo[...]).astype(BF16)
        return carry

    lax.fori_loop(0, tiles, step, 0, unroll=True)
    for by, other in bits(2):
        grad = dot_tn(att[...], gb[:, pl.ds(column_of(info, by, other), 256)]).astype(BF16)
        for t in range(2):
            swap = block_of(info, t) == 1
            block = jnp.where(swap, grad[256:], grad[:256])
            for bx in range(2):
                q = other * 2 + t
                put(outs, by, bx, q, slice(0, down_rows), down[by, bx, q])
                put(outs, by, bx, q, slice(down_rows, down_rows + 128), jnp.where(
                    (info[4] ^ bx) == 1, block[128:], block[:128]))


def crossed(parts, by, bx, q):
    low, low_x, low_y, low_xy, high, high_x, high_y, high_xy = parts
    group = (low, low_x, low_y, low_xy) if q < 2 else (high, high_x, high_y, high_xy)
    return group[by * 2 + bx].at[q & 1]


def ffn_copies(info, first, parts, wgu, wd, sem):
    units = wd.shape[0]
    own = units // 2
    part = own // 2
    copies = []
    for by, bx in bits(2):
        for q in range(4):
            lane = pl.multiple_of(place_of(info, bx, q) * 128, 128)
            if first:
                source = parts[q].at[0] if by + bx == 0 else parts[4 + q].at[by * 2 + bx - 1]
            else:
                source = crossed(parts, by, bx, q)
            for up in range(2):
                copies.append(pltpu.make_async_copy(
                    source.at[pl.ds(0, own), pl.ds(up * 128, 128)],
                    wgu.at[pl.ds(up * units + by * own, own), pl.ds(lane, 128)],
                    sem.at[len(copies)]))
    for by, bx, other, t in bits(4):
        row = pl.multiple_of(block_of(info, t) * own + (info[4] ^ bx) * part, 16)
        q = other * 2 + t
        if first:
            source = source_of(parts[8:], by, bx, q).at[pl.ds(0, part)]
        else:
            source = crossed(parts, by, bx, q).at[pl.ds(own, part)]
        copies.append(pltpu.make_async_copy(
            source, wd.at[pl.ds(row, part), pl.ds(column_of(info, by, other), 256)],
            sem.at[len(copies)]))
    return copies


def ffn_body(first, *refs):
    info = refs[0]
    if first:
        x, part, recv, gains = refs[1:5]
        cot_parts, parts = refs[5:8], refs[8:21]
        h2, gy, gh2, res = refs[21:25]
        outs, refs = refs[25:30], refs[30:]
    else:
        h2, gy, gh2_in, res_in = refs[1:5]
        parts = refs[5:13]
        gh2, rkeep, rsend = refs[13:16]
        outs, down_grad, refs = refs[16:20], refs[20], refs[21:]
    hid, ggu, wgu, wd, sem = refs
    copies = ffn_copies(info, first, parts, wgu, wd, sem)
    for copy in copies:
        copy.start()
    units = wd.shape[0]
    tiles = h2.shape[0] // TILE
    if first:
        live = jnp.where(info[0] < info[5], 1.0, 0.0)

        def norm_step(t, carry):
            at = pl.ds(pl.multiple_of(t * TILE, TILE), TILE)
            middle = middle_of(x, part, recv, at)
            inverse = lax.rsqrt(jnp.mean(middle * middle, axis=-1, keepdims=True) + EPSILON)
            h2[at, :] = (middle * inverse * gains[1:2, :]).astype(BF16)
            gy[at, :] = (piece_of(info, t, *cot_parts).astype(F32) * live).astype(BF16)
            return carry

        lax.fori_loop(0, tiles, norm_step, 0, unroll=True)
    for copy in copies:
        copy.wait()

    def step(t, carry):
        at = pl.ds(pl.multiple_of(t * TILE, TILE), TILE)
        both = dot_nt(wgu[...], h2[at, :])
        gate, up = both[:units], both[units:]
        sig = 1.0 / (1.0 + jnp.exp(-gate))
        act = gate * sig
        hidden = (act * up).astype(BF16)
        hid[:, at] = hidden
        grad_hidden = dot_nt(wd[...], gy[at, :])
        ggu[:units, at] = (grad_hidden * up * (sig + act * (1.0 - sig))).astype(BF16)
        ggu[units:, at] = (grad_hidden * act).astype(BF16)
        grad_h = dot_tn(ggu[:, at], wgu[...])
        result = dot_tn(hidden, wd[...])
        if first:
            gh2[at, :] = grad_h.astype(BF16)
            res[at, :] = result.astype(BF16)
        else:
            gh2[at, :] = (gh2_in[at, :].astype(F32) + grad_h).astype(BF16)
            result = res_in[at, :].astype(F32) + result

            @pl.when((t & 1) == info[1])
            def _():
                rkeep[t >> 1] = result

            @pl.when((t & 1) != info[1])
            def _():
                rsend[t >> 1] = result.astype(BF16)

        return carry

    lax.fori_loop(0, tiles, step, 0, unroll=True)
    own = units // 2
    part = own // 2
    swap = info[4] == 1
    for q in (3, 2, 1, 0):
        z = info[3] ^ (q >> 1) ^ (3 * (q & 1))
        grad = dot_nn(ggu[...], h2[:, pl.ds(pl.multiple_of(z * 256, 256), 256)]).astype(BF16)
        lo, hi = grad[:, :128], grad[:, 128:]
        for bx, side in ((0, jnp.where(swap, hi, lo)), (1, jnp.where(swap, lo, hi))):
            for by, up in bits(2):
                lanes = slice(up * 128, up * 128 + 128)
                piece = side[up * units + by * own : up * units + (by + 1) * own]
                if first:
                    put_lanes(outs, by, bx, q, slice(0, own), lanes, piece)
                else:
                    outs[q][by * 2 + bx, :, lanes] = piece
    for by, other in bits(2):
        grad = dot_nn(hid[...], gy[:, pl.ds(column_of(info, by, other), 256)]).astype(BF16)
        for t in range(2):
            block = jnp.where(block_of(info, t) == 1, grad[own:], grad[:own])
            for bx in range(2):
                q = other * 2 + t
                piece = jnp.where((info[4] ^ bx) == 1, block[part:], block[:part])
                if first:
                    put(outs, by, bx, q, slice(own, own + part), piece)
                else:
                    down_grad[by, bx, q] = piece


def qkv_grad_body(by, *refs):
    info, dq, dk, dv, h1, gains, gain_grad = refs[:7]
    parts, refs = (refs[7:10], refs[10:]) if by else (refs[7:9], refs[9:])
    outs, (w, acc, sem) = refs[:3], refs[3:]
    copies = []
    for bx in range(2):
        for q in range(4):
            if by == 0 or bx == 0:
                source = parts[bx].at[q]
            else:
                split = parts[1].shape[0]
                source = parts[1].at[q] if q < split else parts[2].at[q - split]
            copies.append(pltpu.make_async_copy(
                source, w.at[place_of(info, bx, q)], sem.at[len(copies)]))
    for copy in copies:
        copy.start()
    width = w.shape[2]

    def spot(bx, q):
        if by:
            diagonal, send, keep = outs
            split = send.shape[0] // 2
            if q < split:
                return send, q if bx else split + q
            return (diagonal if bx else keep), q - split
        send, keep, own = outs
        split = keep.shape[0]
        if not bx:
            return own, q
        return (keep, q) if q < split else (send, q - split)

    waiting = True
    ones = jnp.ones((8, 3 * width), BF16)
    three = jnp.concatenate([dq[...], dk[...], dv[...]], axis=1)
    for q in (3, 2, 1, 0):
        z = info[3] ^ (q >> 1) ^ (3 * (q & 1))
        at = pl.ds(pl.multiple_of(z * 256, 256), 256)
        grad = dot_tn(h1[:, at], three)
        if waiting:
            for copy in copies:
                copy.wait()
            waiting = False
        weight = jnp.concatenate(
            [w[pl.ds(z * 2, 2), n * 128 : (n + 1) * 128, :].reshape(256, width)
             for n in range(3)], axis=1)
        shares = dot_nt(ones, (grad * weight.astype(F32)).astype(BF16))
        acc[:, at] = shares / gains[0:1, at]
        grad = grad.astype(BF16)
        for bx in range(2):
            part = jnp.where((info[4] ^ bx) == 1, grad[128:], grad[:128])
            ref, i = spot(bx, q)
            for n in range(3):
                ref[i, n * 128 : (n + 1) * 128, :] = part[:, n * width : (n + 1) * width]
    for bx in range(2):
        for q in range(4):
            at = pl.ds(pl.multiple_of(place_of(info, bx, q) * 128, 128), 128)
            row = jnp.concatenate([acc[0:1, at], gain_grad[0:1, at]], axis=1)
            ref, i = spot(bx, q)
            ref[i, 384:400, :] = jnp.broadcast_to(row, (16, 256)).astype(BF16)


def qkv_back_body(*refs):
    info, grads = refs[0], (refs[1:4], refs[4:7])
    parts = refs[7:12]
    gkeep, gsend, w, sem = refs[12:]
    run_copies(attn_copies(info, parts, w, sem))
    width = w.shape[3]
    model = gkeep.shape[2]

    def step(t, carry):
        at = pl.ds(pl.multiple_of(t * TILE, TILE), TILE)
        grad_h = jnp.zeros((TILE, model), F32)
        for by in range(2):
            for n in range(3):
                weight = w[by, :, n * 128 : (n + 1) * 128, :].reshape(model, width)
                grad_h = grad_h + dot_nt(grads[by][n][at, :], weight)

        @pl.when((t & 1) == info[1])
        def _():
            gkeep[t >> 1] = grad_h

        @pl.when((t & 1) != info[1])
        def _():
            gsend[t >> 1] = grad_h.astype(BF16)

        return carry

    lax.fori_loop(0, gkeep.shape[0] * 2, step, 0, unroll=True)


def input_body(info, gkeep, grecv, x, own_mid, gains, keep, send):
    for half in range(2):
        at = pl.ds(pl.multiple_of((half * 2 + info[1]) * TILE, TILE), TILE)
        xt = x[at, :].astype(F32)
        grad = gkeep[half] + grecv[half].astype(F32)
        inverse = lax.rsqrt(jnp.mean(xt * xt, axis=-1, keepdims=True) + EPSILON)
        scaled = grad * gains[0:1, :]
        share = inverse * inverse * inverse * jnp.mean(scaled * xt, axis=-1, keepdims=True)
        total = own_mid[half] + inverse * scaled - xt * share

        @pl.when(info[0] == half)
        def _():
            keep[...] = total

        @pl.when(info[0] != half)
        def _():
            send[...] = total.astype(BF16)


def plus(*values):
    total = values[0].astype(F32)
    for value in values[1:]:
        total = total + value.astype(F32)
    return total


class Steps(dict):
    __getattr__ = dict.__getitem__
    __setattr__ = dict.__setitem__


def on_device(
    tokens, first_values, seq_counts, norm1_gain, query_weight, key_weight, value_weight,
    out_weight, norm2_gain, gate_weight, up_weight, down_weight, output_cotangent,
):
    slots, piece, model = tokens.shape
    length = piece * lax.axis_size("seq")
    wide = lax.axis_size("dp") // BLOCKS
    s = lax.axis_index("seq")
    place = lax.axis_index("dp")
    y, c = s // 2, s % 2
    d = place // wide
    z, x_at = d // 2, d % 2
    info = jnp.stack([y, c, d, z, x_at, seq_counts[0]]).astype(jnp.int32)
    even = (z & 1) ^ c

    def pregather(shard):
        step = 1
        while step < wide:
            other = flip(shard, "dp", step)
            bit = (place // step) % 2
            shard = pick(
                bit, jnp.concatenate([other, shard]), jnp.concatenate([shard, other]))
            step *= 2
        return shard

    def postscatter(total):
        step = wide // 2
        while step >= 1:
            half = total.shape[0] // 2
            bit = (place // step) % 2
            lo, hi = total[:half], total[half:]
            total = pick(bit, hi, lo) + flip(pick(bit, lo, hi), "dp", step)
            step //= 2
        return total

    def far(v):
        return flip(v, "dp", ZM * wide)

    def near(v):
        return flip(v, "dp", Z1 * wide)

    def over_x(v):
        return flip(v, "dp", X1 * wide)

    def over_y(v):
        return flip(v, "seq", MESH_Y)

    def over_core(v):
        return flip(v, "seq", MESH_C)

    def other_slot(block):
        return pick(y, block[0], block[1])

    def mine_of(low, high):
        return jnp.stack([pick(even, low[1], low[0]), pick(even, high[0], high[1])])

    def theirs_of(low, high):
        return jnp.stack([pick(even, low[0], low[1]), pick(even, high[1], high[0])])

    def own_slot(block, recv):
        return jnp.stack([pick(y, block[1], block[0]), recv])

    def pack(*parts):
        rows = parts[0].shape[-2]
        (out,) = call(
            pack_body, [((4, rows, 256), BF16)], [("v", part) for part in parts], [],
            1000, 1 << 20, vmem=8)
        return out

    local = model // 2
    width = local // 2
    v = Steps()
    v.cosine, v.sine = turn_tables(length)
    v.a0 = jnp.concatenate(
        [pregather(query_weight), pregather(key_weight), pregather(value_weight),
         jnp.pad(jnp.concatenate([pregather(norm1_gain), pregather(norm2_gain)])[None],
                 ((0, 15), (0, 0)))])
    attn_rows = v.a0.shape[0]
    down = pregather(down_weight)
    part_a = down.shape[0] * 192 // 352 // 16 * 16
    part_b = down.shape[0] - part_a
    whole = down.shape[0]
    ffn = jnp.concatenate([pregather(gate_weight).T, pregather(up_weight).T], axis=1)
    v.b0 = jnp.concatenate([ffn[part_a:whole], ffn[whole + part_a :]])[None]
    v.g0 = jnp.concatenate([ffn[:part_a], ffn[whole : whole + part_a], down[:part_a]])
    v.r0 = jnp.concatenate([down[part_a:], pregather(out_weight)])
    out_rows = v.r0.shape[0] - part_b
    v.t_send = other_slot(tokens)
    v.f_send = other_slot(first_values)
    v.c_send = other_slot(output_cotangent)
    v.tokens, v.firsts, v.cots = tokens, first_values, output_cotangent

    v.a0, v.t_send, v.b0 = lax.optimization_barrier(
        (v.a0, v.t_send, v.b0))
    v.ty, v.af, v.an = over_y(v.t_send), far(v.a0), near(v.a0)
    v.bx = over_x(v.b0)
    v.a0, v.af, v.an, v.ty, v.tokens, v.b0, v.bx, v.f_send, v.c_send, v.firsts, v.cots, v.r0, v.g0 = lax.optimization_barrier(
        (v.a0, v.af, v.an, v.ty, v.tokens, v.b0, v.bx, v.f_send, v.c_send, v.firsts, v.cots, v.r0, v.g0))
    v.fy, v.anf, v.rf = over_y(v.f_send), near(v.af), far(v.r0)
    v.bf0 = far(v.b0)
    v.tc = over_core(own_slot(v.tokens, v.ty))
    v.a0, v.af, v.an, v.anf, v.fy, v.tc, v.firsts, v.b0, v.bx, v.bf0, v.r0, v.rf, v.g0, v.c_send, v.cots = lax.optimization_barrier(
        (v.a0, v.af, v.an, v.anf, v.fy, v.tc, v.firsts, v.b0, v.bx, v.bf0, v.r0, v.rf, v.g0, v.c_send, v.cots))
    v.z = pack(v.a0, v.af, v.an, v.anf)
    v.zx, v.zy = over_x(v.z), over_y(v.z)
    v.rlow = jnp.stack([v.r0, v.rf])
    v.rhigh, v.gf = near(v.rlow), far(v.g0)
    v.fc = over_core(own_slot(v.firsts, v.fy))
    v.z, v.zx, v.zy, v.rlow, v.rhigh, v.g0, v.gf, v.fc, v.b0, v.bx, v.bf0, v.c_send, v.cots = lax.optimization_barrier(
        (v.z, v.zx, v.zy, v.rlow, v.rhigh, v.g0, v.gf, v.fc, v.b0, v.bx, v.bf0, v.c_send, v.cots))
    v.zu, v.zv = over_y(v.zx[:SPLIT]), over_x(v.zy[SPLIT:])
    v.rmine = mine_of(v.rlow, v.rhigh)
    v.rother = over_core(theirs_of(v.rlow, v.rhigh))
    v.b10 = over_y(jnp.concatenate([v.b0, v.bx]))
    v.glow = jnp.stack([v.g0, v.gf])
    v.ghigh = near(v.glow)
    v.z, v.zx, v.zy, v.zu, v.zv, v.rmine, v.rother, v.b0, v.bx, v.b10, v.bf0, v.glow, v.ghigh, v.c_send, v.cots = lax.optimization_barrier(
        (v.z, v.zx, v.zy, v.zu, v.zv, v.rmine, v.rother, v.b0, v.bx, v.b10, v.bf0, v.glow, v.ghigh, v.c_send, v.cots))
    v.r = pack(v.rmine, v.rother)
    v.rx, v.ry = over_x(v.r), over_y(v.r)
    v.b3 = jnp.concatenate([v.bx, v.b10])
    v.bf3, v.bn3 = far(v.b3), near(v.b3)
    glow, ghigh = v.glow[:, 2 * part_a :], v.ghigh[:, 2 * part_a :]
    v.gmine, v.gother = mine_of(glow, ghigh), over_core(theirs_of(glow, ghigh))

    def anywhere(*arrays):
        return [("a", array) for array in arrays]

    def values(*arrays):
        return [("v", array) for array in arrays]

    square = ((length, model), BF16)
    tall = ((length, local), BF16)
    tile = (2, piece, model)
    w_scratch = pltpu.VMEM((2, BLOCKS, attn_rows, width), BF16)
    sem16 = pltpu.SemaphoreType.DMA((16,))
    narrow = 2 * length * model * local
    v.x, v.h1, v.q, v.k, v.b, v.gains = call(
        qkv_body, [square, square, tall, tall, tall, ((8, model), F32)],
        [("s", info)] + values(v.tokens, v.ty, v.tc, v.firsts, v.fy, v.fc, v.cosine, v.sine) + anywhere(v.z, v.zx, v.zy, v.zu, v.zv),
        [w_scratch, sem16], 3 * narrow, 14 << 20, vmem=26,
    )
    v.x, v.h1, v.q, v.k, v.b, v.gains, v.r, v.rx, v.ry, v.b0, v.b3, v.bf0, v.bf3, v.bn3, v.glow, v.ghigh, v.gmine, v.gother, v.c_send, v.cots = lax.optimization_barrier(
        (v.x, v.h1, v.q, v.k, v.b, v.gains, v.r, v.rx, v.ry, v.b0, v.b3, v.bf0, v.bf3, v.bn3, v.glow, v.ghigh, v.gmine, v.gother, v.c_send, v.cots))
    v.ru, v.rv = over_y(v.rx[:SPLIT]), over_x(v.ry[SPLIT:])
    v.gl = jnp.concatenate([v.glow[:, : 2 * part_a], v.gmine], axis=1)
    v.gh = jnp.concatenate([v.ghigh[:, : 2 * part_a], v.gother], axis=1)
    v.glx, v.ghy = over_x(v.gl), over_y(v.gh)
    v.bnf3 = near(v.bf3)
    head_specs = [pl.BlockSpec((length, 128), lambda i: (0, i))] * 3
    lse_spec = pl.BlockSpec((1, 2, length), lambda i: (i, 0, 0))
    pairs = local // 128
    v.att, v.lse = call(
        attend_body, [tall, ((pairs, 2, length), F32)], values(v.q, v.k, v.b), [],
        4 * length * length * local, 4 << 20, length * length * pairs * 2, vmem=20,
        grid=(pairs,), in_specs=head_specs, out_specs=[head_specs[0], lse_spec],
    )
    v.att, v.lse, v.r, v.rx, v.ry, v.ru, v.rv, v.gl, v.glx, v.gh, v.ghy, v.bnf3, v.c_send, v.bf0, v.b0 = lax.optimization_barrier(
        (v.att, v.lse, v.r, v.rx, v.ry, v.ru, v.rv, v.gl, v.glx, v.gh, v.ghy, v.bnf3, v.c_send, v.bf0, v.b0))
    v.cy = over_y(v.c_send)
    v.bnf0, v.bn0 = near(v.bf0), near(v.b0)
    (v.part,) = call(
        out_body, [square], [("s", info)] + values(v.att) + anywhere(v.r, v.rx, v.ry, v.ru, v.rv),
        [pltpu.VMEM((local, model), BF16), sem16], narrow, 5 << 20, vmem=12,
    )
    v.att, v.lse, v.r, v.rx, v.ry, v.ru, v.rv, v.part, v.cy, v.cots, v.gl, v.glx, v.gh, v.ghy, v.b0, v.b3, v.bf0, v.bn0, v.bf3, v.bn3, v.bnf0, v.bnf3 = lax.optimization_barrier(
        (v.att, v.lse, v.r, v.rx, v.ry, v.ru, v.rv, v.part, v.cy, v.cots, v.gl, v.glx, v.gh, v.ghy, v.b0, v.b3, v.bf0, v.bn0, v.bf3, v.bn3, v.bnf0, v.bnf3))
    v.precv, v.cc = over_core(v.part), over_core(own_slot(v.cots, v.cy))
    v.part, v.precv, v.cc, v.gl, v.glx, v.gh, v.ghy = lax.optimization_barrier(
        (v.part, v.precv, v.cc, v.gl, v.glx, v.gh, v.ghy))

    def five(rows):
        return [((count, rows, 256), BF16)
                for count in (2 * (4 - SPLIT), 2 * SPLIT, SPLIT, 4 - SPLIT, 4)]

    v.gly, v.glxy = over_y(v.gl), over_y(v.glx)
    v.ghx, v.ghxy = over_x(v.gh), over_x(v.ghy)
    def ffn_scratch(units):
        return [pltpu.VMEM((units, length), BF16), pltpu.VMEM((2 * units, length), BF16),
                pltpu.VMEM((2 * units, model), BF16), pltpu.VMEM((units, model), BF16),
                pltpu.SemaphoreType.DMA((48,))]

    ffn_flops = 36 * length * model
    v.h2, v.gy, v.gh2b, v.resb, v.bsx, v.bsy, v.bkx, v.bky, v.bown = call(
        functools.partial(ffn_body, True), [square] * 4 + five(3 * part_b),
        [("s", info)] + values(v.x, v.part, v.precv, v.gains, v.cots, v.cy, v.cc)
        + anywhere(v.b0, v.bf0, v.bn0, v.bnf0, v.b3, v.bf3, v.bn3, v.bnf3) + anywhere(v.r, v.rx, v.ry, v.ru, v.rv),
        ffn_scratch(4 * part_b), ffn_flops * 2 * part_b, 24 << 20, vmem=40,
    )
    v.h2, v.gy, v.gh2b, v.resb, v.bsx, v.bsy, v.bkx, v.bky, v.bown, v.gl, v.glx, v.gly, v.glxy, v.gh, v.ghx, v.ghy, v.ghxy = lax.optimization_barrier(
        (v.h2, v.gy, v.gh2b, v.resb, v.bsx, v.bsy, v.bkx, v.bky, v.bown, v.gl, v.glx, v.gly, v.glxy, v.gh, v.ghx, v.ghy, v.ghxy))
    v.brx, v.bry = over_x(v.bsx), over_y(v.bsy)
    quads = [((4, 2 * part_a, 256), BF16)] * 4 + [((2, 2, 4, part_a, 256), BF16)]
    (v.gh2, v.rkeep, v.rsend, v.n0, v.n1, v.n2, v.n3, v.dgrad) = call(
        functools.partial(ffn_body, False), [square, (tile, F32), (tile, BF16)] + quads,
        [("s", info)] + values(v.h2, v.gy, v.gh2b, v.resb)
        + anywhere(v.gl, v.glx, v.gly, v.glxy, v.gh, v.ghx, v.ghy, v.ghxy),
        ffn_scratch(4 * part_a), ffn_flops * 2 * part_a, 24 << 20, vmem=40,
    )
    v.gh2, v.rkeep, v.rsend, v.n0, v.n1, v.n2, v.n3, v.dgrad, v.brx, v.bry, v.bkx, v.bky, v.bown, v.part, v.precv = lax.optimization_barrier(
        (v.gh2, v.rkeep, v.rsend, v.n0, v.n1, v.n2, v.n3, v.dgrad, v.brx, v.bry, v.bkx, v.bky, v.bown, v.part, v.precv))

    def fold(name):
        v[name + "fx"] = plus(v[name + "kx"], v[name + "ry"][:SPLIT]).astype(BF16)
        v[name + "fy"] = plus(v[name + "ky"], v[name + "rx"][: 4 - SPLIT]).astype(BF16)

    def total_of(name):
        low = plus(v[name + "own"][:SPLIT], v[name + "ry"][SPLIT:], v[name + "rx2"])
        high = plus(v[name + "own"][SPLIT:], v[name + "rx"][4 - SPLIT :], v[name + "ry2"])
        return jnp.concatenate([low, high])

    def rows_out(name, total, first):
        v[name + "t"] = total
        v[name + "m"] = over_core(total[2:, first:].astype(BF16))

    def quarter(name, first, q):
        total, recv = v[name + "t"], v[name + "m"]
        rows = total[q >> 1, first:]
        other = recv[q >> 1].astype(F32)
        mine = pick(even, other, rows) if q in (0, 3) else pick(even, rows, other)
        return mine if first == 0 else jnp.concatenate([total[q, :first], mine])

    def owner_send(halves_of):
        return pick(y, halves_of[0], halves_of[1])

    def owner_keep(halves_of):
        return pick(y, halves_of[1], halves_of[0])

    def both_slots(keep, recv):
        return pick(y, jnp.stack([recv, keep]), jnp.stack([keep, recv]))

    def own_tokens(full):
        cut_up = full.reshape(2, 2, piece, full.shape[-1])
        return pick(c, cut_up[:, 1], cut_up[:, 0])

    v.gh2r = over_core(v.gh2)
    v.rrecv = over_core(v.rsend)
    fold("b")
    v.brx2, v.bry2 = over_x(v.bfx), over_y(v.bfy)
    v.nn3 = near(v.n3)
    (v.datt, v.mid, v.gain2,
     v.ssx, v.ssy, v.skx, v.sky, v.sown) = call(
        out_back_body, [tall, (tile, F32), ((8, model), F32)] + five(part_a + out_rows),
        [("s", info)] + values(v.gh2, v.gh2r, v.x, v.part, v.precv, v.gy, v.gains, v.att, v.dgrad) + anywhere(v.r, v.rx, v.ry, v.ru, v.rv),
        [pltpu.VMEM((local, model), BF16), pltpu.VMEM((length, model), BF16), sem16],
        2 * narrow, 20 << 20, vmem=56,
    )
    v.datt, v.mid, v.gain2, v.ssx, v.ssy, v.skx, v.sky, v.sown, v.bown, v.brx, v.bry, v.brx2, v.bry2, v.n0, v.n1, v.n2, v.nn3, v.rkeep, v.rrecv, v.part, v.precv = lax.optimization_barrier(
        (v.datt, v.mid, v.gain2, v.ssx, v.ssy, v.skx, v.sky, v.sown, v.bown, v.brx, v.bry, v.brx2, v.bry2, v.n0, v.n1, v.n2, v.nn3, v.rkeep, v.rrecv, v.part, v.precv))
    v.srx, v.sry = over_x(v.ssx), over_y(v.ssy)
    v.n1 = plus(v.n1, v.nn3).astype(BF16)
    v.nf1, v.nn2 = far(v.n1[2:]), near(v.n2)
    rows_out("b", total_of("b"), 2 * part_b)

    live_now = jnp.where(y < seq_counts[0], 1.0, 0.0)
    middle_own = own_tokens(v.x).astype(F32) + plus(
        own_tokens(v.part), own_tokens(v.precv))
    result = (live_now * (middle_own + plus(v.rkeep, v.rrecv))).astype(BF16)
    v.okeep, v.orecv = owner_keep(result), over_y(owner_send(result))
    def attend_back(side):
        first = side * (pairs // 2)
        column = pl.BlockSpec((length, 128), lambda i: (0, i + first))
        table = pl.BlockSpec((length, 128), lambda i: (0, 0))
        sums = pl.BlockSpec((1, 2, length), lambda i: (i + first, 0, 0))
        target = pl.BlockSpec((length, 128), lambda i: (0, i))
        return call(
            attend_back_body, [((length, width), BF16)] * 3,
            values(v.q, v.k, v.b, v.datt, v.lse, v.cosine, v.sine),
            [pltpu.VMEM((length, 128), F32), pltpu.VMEM((length, 128), F32)],
            5 * length * length * local, 4 << 20, length * length * pairs, vmem=26,
            grid=(pairs // 2,), in_specs=[column] * 4 + [sums, table, table],
            out_specs=[target] * 3,
        )

    def attn_grads(side):
        counts = (4 - SPLIT, 2 * SPLIT, 4 - SPLIT) if side else (4 - SPLIT, SPLIT, 4)
        arrays = (v.zy, v.zu, v.zv) if side else (v.z, v.zx)
        return call(
            functools.partial(qkv_grad_body, side),
            [((count, attn_rows, width), BF16) for count in counts],
            [("s", info)] + values(*(v.grads1 if side else v.grads0), v.h1, v.gains, v.gain2)
            + anywhere(*arrays),
            [pltpu.VMEM((BLOCKS, attn_rows, width), BF16), pltpu.VMEM((8, model), F32),
             pltpu.SemaphoreType.DMA((8,))], 3 * narrow // 2, 7 << 20, vmem=24,
        )

    v.grads1 = attend_back(1)
    v.qdx, v.qsy, v.qky = attn_grads(1)
    v.grads1, v.qdx, v.qsy, v.qky, v.q, v.k, v.b, v.datt, v.srx, v.sry, v.skx, v.sky, v.sown, v.n0, v.n1, v.nf1, v.nn2, v.bt, v.bm, v.okeep, v.orecv = lax.optimization_barrier(
        (v.grads1, v.qdx, v.qsy, v.qky, v.q, v.k, v.b, v.datt, v.srx, v.sry, v.skx, v.sky, v.sown, v.n0, v.n1, v.nf1, v.nn2, v.bt, v.bm, v.okeep, v.orecv))
    v.qry, v.qrd = over_y(v.qsy), over_x(v.qdx)
    fold("s")
    v.srx2 = over_x(v.sfx)
    v.nf0 = far(v.n1[:2])
    v.bzn = near(jnp.stack([quarter("b", 2 * part_b, 2), quarter("b", 2 * part_b, 3)]).astype(BF16))
    v.grads0 = attend_back(0)
    v.qsx, v.qkx, v.qown = attn_grads(0)
    v.grads0, v.grads1, v.qsx, v.qkx, v.qown, v.qry, v.qrd, v.qky, v.srx, v.sry, v.srx2, v.sfy, v.sown, v.n0, v.nf0, v.nf1, v.nn2, v.bzn, v.bt, v.bm, v.okeep, v.orecv = lax.optimization_barrier(
        (v.grads0, v.grads1, v.qsx, v.qkx, v.qown, v.qry, v.qrd, v.qky, v.srx, v.sry, v.srx2, v.sfy, v.sown, v.n0, v.nf0, v.nf1, v.nn2, v.bzn, v.bt, v.bm, v.okeep, v.orecv))
    v.qrx = over_x(v.qsx)
    v.sry2 = over_y(v.sfy)
    v.nt0 = plus(v.n0[:2], v.nf0, v.nn2[:2])
    v.nx = over_y(plus(v.n0[2:], v.nf1, v.nn2[2:]).astype(BF16))
    v.bt0 = plus(quarter("b", 2 * part_b, 0), v.bzn[0])
    v.bzf = far(plus(quarter("b", 2 * part_b, 1), v.bzn[1]).astype(BF16))
    v.gkeep, v.gsend = call(
        qkv_back_body, [(tile, F32), (tile, BF16)],
        [("s", info)] + values(*v.grads0, *v.grads1) + anywhere(v.z, v.zx, v.zy, v.zu, v.zv), [w_scratch, sem16],
        3 * narrow, 14 << 20, vmem=18,
    )
    v.gkeep, v.gsend, v.qry, v.qrd, v.qky, v.qrx, v.qkx, v.qown, v.bt0, v.bzf, v.nt0, v.nx, v.srx, v.sry, v.srx2, v.sry2, v.sown, v.grads0, v.grads1, v.okeep, v.orecv = lax.optimization_barrier(
        (v.gkeep, v.gsend, v.qry, v.qrd, v.qky, v.qrx, v.qkx, v.qown, v.bt0, v.bzf, v.nt0, v.nx, v.srx, v.sry, v.srx2, v.sry2, v.sown, v.grads0, v.grads1, v.okeep, v.orecv))
    output = both_slots(v.okeep, v.orecv)
    total_b = plus(v.bt0, v.bzf)
    v.grecv = over_core(v.gsend)
    v.qfx = plus(v.qkx, v.qry[:SPLIT]).astype(BF16)
    v.qfy = plus(v.qky, v.qrd).astype(BF16)
    v.qrx2, v.qry2 = over_x(v.qfx), over_y(v.qfy)
    rows_out("s", total_of("s"), 0)
    v.nt0 = plus(v.nt0, v.nx)
    v.ny = over_x(v.nt0[1].astype(BF16))
    v.ikeep, v.isend = call(
        input_body, [((piece, model), F32), ((piece, model), BF16)],
        [("s", info)] + values(v.gkeep, v.grecv, v.x, v.mid, v.gains), [], 1000, 8 << 20, vmem=16,
    )
    v.ikeep, v.isend, v.qrx, v.qry, v.qrx2, v.qry2, v.qown, v.st, v.sm, v.nt0, v.ny, v.grads0, v.grads1 = lax.optimization_barrier(
        (v.ikeep, v.isend, v.qrx, v.qry, v.qrx2, v.qry2, v.qown, v.st, v.sm, v.nt0, v.ny, v.grads0, v.grads1))
    total_a = plus(v.nt0[0], v.ny)
    low = plus(v.qown[:SPLIT], v.qry[SPLIT:], v.qrx2)
    high = plus(v.qown[SPLIT:], v.qrx, v.qry2)
    v.qt = jnp.concatenate([low, high])
    v.qz, v.sz = near(v.qt[3].astype(BF16)), near(quarter("s", 0, 3).astype(BF16))
    v.irecv = over_y(v.isend)
    cuts = [grads[2].reshape(2, 2, piece, width) for grads in (v.grads0, v.grads1)]
    dv_keep = [pick(c, cut[:, 1], cut[:, 0]) for cut in cuts]
    dv_recv = over_core(
        jnp.concatenate([pick(c, cut[:, 0], cut[:, 1]) for cut in cuts], axis=-1))
    dv_recv = [dv_recv[..., :width], dv_recv[..., width:]]
    blocks = []
    for column_y, column_c in bits(2):
        side = y ^ column_y
        mine = pick(side, dv_keep[1], dv_keep[0])
        theirs = pick(side, dv_recv[1], dv_recv[0])
        blocks.append(pick(c ^ column_c, theirs, mine))
    grad_rows = jnp.concatenate(blocks, axis=-1)
    v.fkeep, v.fsend = owner_keep(grad_rows), owner_send(grad_rows)
    v.qt, v.qz, v.st, v.sm, v.sz, v.irecv, v.ikeep, v.fkeep, v.fsend = lax.optimization_barrier(
        (v.qt, v.qz, v.st, v.sm, v.sz, v.irecv, v.ikeep, v.fkeep, v.fsend))
    v.qzf = far(plus(v.qt[1], v.qz).astype(BF16))
    v.szf = far(plus(quarter("s", 0, 1), v.sz).astype(BF16))
    v.qzn = near(v.qt[2].astype(BF16))
    v.szn = near(quarter("s", 0, 2).astype(BF16))
    v.frecv = over_y(v.fsend)
    v.qt0, v.st0 = v.qt[0], quarter("s", 0, 0)
    grad_input = both_slots(v.ikeep, v.irecv.astype(F32))
    v.qt0, v.st0, v.qzf, v.szf, v.qzn, v.szn, v.fkeep, v.frecv = lax.optimization_barrier(
        (v.qt0, v.st0, v.qzf, v.szf, v.qzn, v.szn, v.fkeep, v.frecv))
    total = plus(v.qt0, v.qzf, v.qzn)
    gain_total = total[384]
    gain_share = jnp.broadcast_to(gain_total[None, :128], (8, 128))
    gain_sum = gain_total[:128] + over_core(gain_share)[0] + (
        over_y(gain_share)[0] + flip(gain_share, "seq", MESH_Y | MESH_C)[0])
    total_s = plus(v.st0, v.szf, v.szn)
    grad_first = both_slots(v.fkeep, v.frecv).astype(F32)

    def weave(lanes):
        pieces = [total_a[:part_a, lanes], total_b[:part_b, lanes],
                  total_a[part_a:, lanes], total_b[part_b : 2 * part_b, lanes]]
        return jnp.concatenate(pieces).T

    return (
        output,
        grad_input,
        grad_first,
        postscatter(gain_sum),
        postscatter(total[:128]),
        postscatter(total[128:256]),
        postscatter(total[256:384]),
        postscatter(total_s[part_a:]),
        postscatter(gain_total[128:]),
        postscatter(weave(slice(0, 128))),
        postscatter(weave(slice(128, 256))),
        postscatter(jnp.concatenate([total_s[:part_a], total_b[2 * part_b :]])),
    )


def solution(mesh):
    cut = P("dp", "seq")
    flat = P("dp")
    whole = P("dp", "seq", None)
    return jax.shard_map(
        on_device,
        mesh=mesh,
        in_specs=(whole, whole, flat, flat, cut, cut, cut, cut, flat, cut, cut, cut, whole),
        out_specs=(whole, whole, whole, flat, cut, cut, cut, cut, flat, cut, cut, cut),
        check_vma=False,
    )
```

```python
import functools

import jax
import jax.numpy as jnp
import numpy as np
from jax import lax
from jax.experimental import pallas as pl
from jax.experimental.pallas import tpu as pltpu
from jax.sharding import PartitionSpec as P

HEAD = 64
EPSILON = 1e-06
TILE = 256
BLOCKS = 8
F32 = jnp.float32
BF16 = jnp.bfloat16
MESH_Y, MESH_C = 2, 1
ZM, Z1, X1 = 6, 2, 1
SPLIT = 2


def dot_nn(a, b):
    return lax.dot_general(a, b, (((1,), (0,)), ((), ())), preferred_element_type=F32)


def dot_nt(a, b):
    return lax.dot_general(a, b, (((1,), (1,)), ((), ())), preferred_element_type=F32)


def dot_tn(a, b):
    return lax.dot_general(a, b, (((0,), (0,)), ((), ())), preferred_element_type=F32)


def flip(value, axis, mask):
    pairs = [(i, i ^ mask) for i in range(lax.axis_size(axis))]
    return lax.ppermute(value, axis, pairs)


def pick(flag, when_one, when_zero):
    return jnp.where(flag == 1, when_one, when_zero)


def call(
    body, outs, ins, scratch, flops, moved, exps=0, grid=None, in_specs=None, out_specs=None,
    vmem=56,
):
    spaces = {"v": pltpu.VMEM, "s": pltpu.SMEM, "a": pl.ANY}
    if in_specs is None:
        in_specs = [pl.BlockSpec(memory_space=spaces[kind]) for kind, _ in ins]
        out_specs = [pl.BlockSpec(memory_space=pltpu.VMEM) for _ in outs]
    kwargs = {} if grid is None else {"grid": grid}
    return pl.pallas_call(
        body,
        out_shape=[jax.ShapeDtypeStruct(shape, kind) for shape, kind in outs],
        in_specs=in_specs,
        out_specs=out_specs,
        scratch_shapes=scratch,
        cost_estimate=pl.CostEstimate(flops=flops, bytes_accessed=moved, transcendentals=exps),
        compiler_params=pltpu.CompilerParams(vmem_limit_bytes=vmem << 20),
        **kwargs,
    )(*[value for _, value in ins])


def run_copies(copies):
    for copy in copies:
        copy.start()
    for copy in copies:
        copy.wait()


def turned(values, cosine, signed_sine):
    lane = lax.broadcasted_iota(jnp.int32, values.shape, 1)
    ahead = pltpu.roll(values, 128 - HEAD // 2, 1)
    behind = pltpu.roll(values, HEAD // 2, 1)
    partner = jnp.where(lane % HEAD < HEAD // 2, ahead, behind)
    return values * cosine + partner * signed_sine


def bits(count):
    return [tuple((i >> (count - 1 - j)) & 1 for j in range(count)) for i in range(1 << count)]


def place_of(info, bx, q):
    z = info[3] ^ (q >> 1) ^ (3 * (q & 1))
    return z * 2 + (info[4] ^ bx)


def even_of(info):
    return (info[3] & 1) ^ info[1]


def block_of(info, t):
    return t ^ info[0] ^ (info[3] >> 1) ^ even_of(info)


def column_of(info, by, other):
    block = (info[0] ^ by) * 2 + (info[1] ^ other)
    return pl.multiple_of(block * 256, 256)


def source_of(parts, by, bx, q):
    own, over_x, over_y, corner_y, corner_x = parts
    if by == 0:
        return (own, over_x)[bx].at[q]
    if bx == 0:
        return over_y.at[q]
    split = corner_y.shape[0]
    return corner_y.at[q] if q < split else corner_x.at[q - split]


def put(outs, by, bx, q, rows, value):
    send_x, send_y, keep_x, keep_y, own = outs
    split = keep_x.shape[0]
    if by and bx:
        spot = (send_y, q) if q < split else (send_x, q - split)
    elif by:
        spot = (send_y, split + q) if q < split else (keep_y, q - split)
    elif bx:
        spot = (keep_x, q) if q < split else (send_x, 4 - split + q - split)
    else:
        spot = (own, q)
    spot[0][spot[1], rows, :] = value


def put_lanes(outs, by, bx, q, rows, lanes, value):
    class Cut:
        def __init__(self, ref):
            self.ref = ref
            self.shape = ref.shape

        def __setitem__(self, spot, content):
            self.ref[spot[0], spot[1], lanes] = content

    put(tuple(Cut(ref) for ref in outs), by, bx, q, rows, value)


def turn_tables(length):
    half = HEAD // 2
    steps = np.arange(half, dtype=np.float32) * np.float32(2.0)
    frequency = np.power(np.float32(10000.0), -steps / np.float32(HEAD), dtype=np.float32)
    angles = (np.arange(length, dtype=np.float32)[:, None] * frequency[None, :]).astype(np.float64)
    cosine = np.tile(np.cos(angles), (1, 4))
    sine = np.tile(np.concatenate([-np.sin(angles), np.sin(angles)], axis=1), (1, 2))
    return jnp.asarray(cosine.astype(np.float32)), jnp.asarray(sine.astype(np.float32))


def pack_body(*refs):
    out = refs[-1]
    at = 0
    for ref in refs[:-1]:
        if len(ref.shape) == 2:
            out[at] = ref[...]
            at += 1
        else:
            out[at : at + ref.shape[0]] = ref[...]
            at += ref.shape[0]


def piece_of(info, t, own, over_y, core):
    near = (t & 1) == info[1]
    mine = jnp.where(near, own[info[0]], core[0])
    other = jnp.where(near, over_y[...], core[1])
    return jnp.where((t >> 1) == info[0], mine, other)


def attn_copies(info, parts, w, sem):
    copies = []
    for by, bx in bits(2):
        for q in range(4):
            copies.append(pltpu.make_async_copy(
                source_of(parts, by, bx, q), w.at[by, place_of(info, bx, q)],
                sem.at[len(copies)]))
    return copies


def qkv_body(*refs):
    info, x_parts, fv_parts, cosine, sine = refs[0], refs[1:4], refs[4:7], refs[7], refs[8]
    parts = refs[9:14]
    x, h1, q, k, b, gains, w, sem = refs[14:]
    run_copies(attn_copies(info, parts, w, sem))
    rows = 128
    width = w.shape[3]
    model = x.shape[1]
    for j in range(2):
        pair = w[0, :, 3 * rows : 3 * rows + 16, j * rows : (j + 1) * rows]
        row = jnp.concatenate([pair[d, 0:1, :] for d in range(BLOCKS)], axis=1).astype(F32)
        gains[j : j + 1, :] = row
    gain = gains[0:1, :]

    def step(t, carry):
        at = pl.ds(pl.multiple_of(t * TILE, TILE), TILE)
        xb = piece_of(info, t, *x_parts)
        x[at, :] = xb
        first = piece_of(info, t, *fv_parts)
        xt = xb.astype(F32)
        inverse = lax.rsqrt(jnp.mean(xt * xt, axis=-1, keepdims=True) + EPSILON)
        h = (xt * inverse * gain).astype(BF16)
        h1[at, :] = h
        cos_t, sin_t = cosine[at, :], sine[at, :]
        quarters = [first[:, i * width : (i + 1) * width] for i in range(4)]
        for by in range(2):
            side = [jnp.where(info[1] == 1, quarters[2 * i + 1], quarters[2 * i]) for i in (0, 1)]
            blend = jnp.where((info[0] ^ by) == 1, side[1], side[0]).astype(F32)
            for n in range(3):
                weight = w[by, :, n * rows : (n + 1) * rows, :].reshape(model, width)
                acc = dot_nn(h, weight)
                cols = pl.ds(by * width, width)
                if n == 2:
                    b[at, cols] = (0.5 * acc + 0.5 * blend).astype(BF16)
                else:
                    halves = [
                        turned(acc[:, j : j + 128], cos_t, sin_t) for j in range(0, width, 128)
                    ]
                    both = jnp.concatenate(halves, axis=1).astype(BF16)
                    (q, k)[n][at, cols] = both * BF16(0.125) if n == 0 else both
        return carry

    lax.fori_loop(0, x.shape[0] // TILE, step, 0, unroll=True)


def split_heads(pair):
    lane = lax.broadcasted_iota(jnp.int32, pair.shape, 1)
    zero = jnp.zeros_like(pair)
    return jnp.concatenate(
        [jnp.where(lane < HEAD, pair, zero), jnp.where(lane < HEAD, zero, pair)], axis=0
    )


def join_heads(both):
    half = both.shape[0] // 2
    lane = lax.broadcasted_iota(jnp.int32, (half, both.shape[1]), 1)
    return jnp.where(lane < HEAD, both[:half], both[half:])


def hide_later(scores, fill):
    length, width = scores.shape
    key_at = lax.broadcasted_iota(jnp.int32, (TILE, width), 0)
    query_at = lax.broadcasted_iota(jnp.int32, (TILE, width), 1) % TILE
    last = jnp.where(key_at <= query_at, scores[length - TILE :], fill)
    if length == TILE:
        return last
    return jnp.concatenate([scores[: length - TILE], last], axis=0)


def attend_body(q, k, b, att, lse):
    for i in range(q.shape[0] // TILE):
        length = (i + 1) * TILE
        queries = split_heads(q[i * TILE : length, :])
        scores = hide_later(dot_nt(k[:length, :], queries), -1e30)
        top = jnp.max(scores, axis=0, keepdims=True)
        grown = jnp.exp(scores - top)
        total = jnp.sum(grown, axis=0, keepdims=True)
        logs = top + jnp.log(total)
        probs = (grown * (1.0 / total)).astype(BF16)
        att[i * TILE : length, :] = join_heads(dot_tn(probs, b[:length, :])).astype(BF16)
        lse[0, 0:1, i * TILE : length] = logs[:, :TILE]
        lse[0, 1:2, i * TILE : length] = logs[:, TILE:]


def attend_back_body(q, k, b, datt, lse, cosine, sine, dq, dk, dv, k_acc, v_acc):
    k_acc[...] = jnp.zeros_like(k_acc)
    v_acc[...] = jnp.zeros_like(v_acc)
    for i in range(q.shape[0] // TILE):
        length = (i + 1) * TILE
        at = slice(i * TILE, length)
        queries = split_heads(q[at, :])
        grads = split_heads(datt[at, :])
        keys = k[:length, :]
        logs = jnp.concatenate([lse[0, 0:1, at], lse[0, 1:2, at]], axis=1)
        probs = jnp.exp(hide_later(dot_nt(keys, queries) - logs, -1e30))
        grad_probs = dot_nt(b[:length, :], grads)
        delta = jnp.sum(probs * grad_probs, axis=0, keepdims=True)
        grad_scores = (probs * (grad_probs - delta)).astype(BF16)
        v_acc[:length, :] += dot_nn(probs.astype(BF16), grads)
        k_acc[:length, :] += dot_nn(grad_scores, queries)
        turned_back = turned(
            0.125 * join_heads(dot_tn(grad_scores, keys)), cosine[at, :], -sine[at, :]
        )
        dq[at, :] = turned_back.astype(BF16)
    for i in range(q.shape[0] // TILE):
        at = slice(i * TILE, (i + 1) * TILE)
        dk[at, :] = turned(k_acc[at, :], cosine[at, :], -sine[at, :]).astype(BF16)
        dv[at, :] = (0.5 * v_acc[at, :]).astype(BF16)


def out_copies(info, parts, wo, sem):
    first = parts[0].shape[1] - 128
    copies = []
    for by, bx, other, t in bits(4):
        row = pl.multiple_of(block_of(info, t) * 256 + (info[4] ^ bx) * 128, 128)
        copies.append(pltpu.make_async_copy(
            source_of(parts, by, bx, other * 2 + t).at[pl.ds(first, 128)],
            wo.at[pl.ds(row, 128), pl.ds(column_of(info, by, other), 256)],
            sem.at[len(copies)]))
    return copies


def out_body(*refs):
    info, att, parts, (part, wo, sem) = refs[0], refs[1], refs[2:7], refs[7:]
    run_copies(out_copies(info, parts, wo, sem))

    def step(t, carry):
        at = pl.ds(pl.multiple_of(t * TILE, TILE), TILE)
        part[at, :] = dot_nn(att[at, :], wo[...]).astype(BF16)
        return carry

    lax.fori_loop(0, att.shape[0] // TILE, step, 0, unroll=True)


def middle_of(x, part, recv, at):
    return x[at, :].astype(F32) + (part[at, :].astype(F32) + recv[at, :].astype(F32))


def out_back_body(*refs):
    info, gh2, gh2_recv, x, part, recv, gy, gains, att, down = refs[:10]
    parts = refs[10:15]
    datt, own_mid, gain_grad = refs[15:18]
    outs, (wo, gb, sem) = refs[18:23], refs[23:]
    down_rows = down.shape[3]
    copies = out_copies(info, parts, wo, sem)
    for copy in copies:
        copy.start()
    gain_grad[...] = jnp.zeros_like(gain_grad)

    def norm_step(t, carry):
        at = pl.ds(pl.multiple_of(t * TILE, TILE), TILE)
        middle = middle_of(x, part, recv, at)
        inverse = lax.rsqrt(jnp.mean(middle * middle, axis=-1, keepdims=True) + EPSILON)
        grad = gh2[at, :].astype(F32) + gh2_recv[at, :].astype(F32)
        scaled = grad * gains[1:2, :]
        share = inverse * inverse * inverse * jnp.mean(scaled * middle, axis=-1, keepdims=True)
        total = gy[at, :].astype(F32) + inverse * scaled - middle * share
        gb[at, :] = total.astype(BF16)
        gain_grad[0:1, :] += jnp.sum(grad * middle * inverse, axis=0, keepdims=True)

        @pl.when((t & 1) == info[1])
        def _():
            own_mid[t >> 1] = total

        return carry

    tiles = att.shape[0] // TILE
    lax.fori_loop(0, tiles, norm_step, 0, unroll=True)
    for copy in copies:
        copy.wait()

    def step(t, carry):
        at = pl.ds(pl.multiple_of(t * TILE, TILE), TILE)
        datt[at, :] = dot_nt(gb[at, :], wo[...]).astype(BF16)
        return carry

    lax.fori_loop(0, tiles, step, 0, unroll=True)
    for by, other in bits(2):
        grad = dot_tn(att[...], gb[:, pl.ds(column_of(info, by, other), 256)]).astype(BF16)
        for t in range(2):
            swap = block_of(info, t) == 1
            block = jnp.where(swap, grad[256:], grad[:256])
            for bx in range(2):
                q = other * 2 + t
                put(outs, by, bx, q, slice(0, down_rows), down[by, bx, q])
                put(outs, by, bx, q, slice(down_rows, down_rows + 128), jnp.where(
                    (info[4] ^ bx) == 1, block[128:], block[:128]))


def crossed(parts, by, bx, q):
    low, low_x, low_y, low_xy, high, high_x, high_y, high_xy = parts
    group = (low, low_x, low_y, low_xy) if q < 2 else (high, high_x, high_y, high_xy)
    return group[by * 2 + bx].at[q & 1]


def ffn_copies(info, first, parts, wgu, wd, sem):
    units = wd.shape[0]
    own = units // 2
    part = own // 2
    copies = []
    for by, bx in bits(2):
        for q in range(4):
            lane = pl.multiple_of(place_of(info, bx, q) * 128, 128)
            if first:
                source = parts[q].at[0] if by + bx == 0 else parts[4 + q].at[by * 2 + bx - 1]
            else:
                source = crossed(parts, by, bx, q)
            for up in range(2):
                copies.append(pltpu.make_async_copy(
                    source.at[pl.ds(0, own), pl.ds(up * 128, 128)],
                    wgu.at[pl.ds(up * units + by * own, own), pl.ds(lane, 128)],
                    sem.at[len(copies)]))
    for by, bx, other, t in bits(4):
        row = pl.multiple_of(block_of(info, t) * own + (info[4] ^ bx) * part, 16)
        q = other * 2 + t
        if first:
            source = source_of(parts[8:], by, bx, q).at[pl.ds(0, part)]
        else:
            source = crossed(parts, by, bx, q).at[pl.ds(own, part)]
        copies.append(pltpu.make_async_copy(
            source, wd.at[pl.ds(row, part), pl.ds(column_of(info, by, other), 256)],
            sem.at[len(copies)]))
    return copies


def ffn_body(first, *refs):
    info = refs[0]
    if first:
        x, part, recv, gains = refs[1:5]
        cot_parts, parts = refs[5:8], refs[8:21]
        h2, gy, gh2, res = refs[21:25]
        outs, refs = refs[25:30], refs[30:]
    else:
        h2, gy, gh2_in, res_in = refs[1:5]
        parts = refs[5:13]
        gh2, rkeep, rsend = refs[13:16]
        outs, down_grad, refs = refs[16:20], refs[20], refs[21:]
    hid, ggu, wgu, wd, sem = refs
    copies = ffn_copies(info, first, parts, wgu, wd, sem)
    for copy in copies:
        copy.start()
    units = wd.shape[0]
    tiles = h2.shape[0] // TILE
    if first:
        live = jnp.where(info[0] < info[5], 1.0, 0.0)

        def norm_step(t, carry):
            at = pl.ds(pl.multiple_of(t * TILE, TILE), TILE)
            middle = middle_of(x, part, recv, at)
            inverse = lax.rsqrt(jnp.mean(middle * middle, axis=-1, keepdims=True) + EPSILON)
            h2[at, :] = (middle * inverse * gains[1:2, :]).astype(BF16)
            gy[at, :] = (piece_of(info, t, *cot_parts).astype(F32) * live).astype(BF16)
            return carry

        lax.fori_loop(0, tiles, norm_step, 0, unroll=True)
    for copy in copies:
        copy.wait()

    def step(t, carry):
        at = pl.ds(pl.multiple_of(t * TILE, TILE), TILE)
        both = dot_nt(wgu[...], h2[at, :])
        gate, up = both[:units], both[units:]
        sig = 1.0 / (1.0 + jnp.exp(-gate))
        act = gate * sig
        hidden = (act * up).astype(BF16)
        hid[:, at] = hidden
        grad_hidden = dot_nt(wd[...], gy[at, :])
        ggu[:units, at] = (grad_hidden * up * (sig + act * (1.0 - sig))).astype(BF16)
        ggu[units:, at] = (grad_hidden * act).astype(BF16)
        grad_h = dot_tn(ggu[:, at], wgu[...])
        result = dot_tn(hidden, wd[...])
        if first:
            gh2[at, :] = grad_h.astype(BF16)
            res[at, :] = result.astype(BF16)
        else:
            gh2[at, :] = (gh2_in[at, :].astype(F32) + grad_h).astype(BF16)
            result = res_in[at, :].astype(F32) + result

            @pl.when((t & 1) == info[1])
            def _():
                rkeep[t >> 1] = result

            @pl.when((t & 1) != info[1])
            def _():
                rsend[t >> 1] = result.astype(BF16)

        return carry

    lax.fori_loop(0, tiles, step, 0, unroll=True)
    own = units // 2
    part = own // 2
    swap = info[4] == 1
    for q in (3, 2, 1, 0):
        z = info[3] ^ (q >> 1) ^ (3 * (q & 1))
        grad = dot_nn(ggu[...], h2[:, pl.ds(pl.multiple_of(z * 256, 256), 256)]).astype(BF16)
        lo, hi = grad[:, :128], grad[:, 128:]
        for bx, side in ((0, jnp.where(swap, hi, lo)), (1, jnp.where(swap, lo, hi))):
            for by, up in bits(2):
                lanes = slice(up * 128, up * 128 + 128)
                piece = side[up * units + by * own : up * units + (by + 1) * own]
                if first:
                    put_lanes(outs, by, bx, q, slice(0, own), lanes, piece)
                else:
                    outs[q][by * 2 + bx, :, lanes] = piece
    for by, other in bits(2):
        grad = dot_nn(hid[...], gy[:, pl.ds(column_of(info, by, other), 256)]).astype(BF16)
        for t in range(2):
            block = jnp.where(block_of(info, t) == 1, grad[own:], grad[:own])
            for bx in range(2):
                q = other * 2 + t
                piece = jnp.where((info[4] ^ bx) == 1, block[part:], block[:part])
                if first:
                    put(outs, by, bx, q, slice(own, own + part), piece)
                else:
                    down_grad[by, bx, q] = piece


def qkv_grad_body(by, *refs):
    info, dq, dk, dv, h1, gains, gain_grad = refs[:7]
    parts, refs = (refs[7:10], refs[10:]) if by else (refs[7:9], refs[9:])
    outs, (w, acc, sem) = refs[:3], refs[3:]
    copies = []
    for bx in range(2):
        for q in range(4):
            if by == 0 or bx == 0:
                source = parts[bx].at[q]
            else:
                split = parts[1].shape[0]
                source = parts[1].at[q] if q < split else parts[2].at[q - split]
            copies.append(pltpu.make_async_copy(
                source, w.at[place_of(info, bx, q)], sem.at[len(copies)]))
    for copy in copies:
        copy.start()
    width = w.shape[2]

    def spot(bx, q):
        if by:
            diagonal, send, keep = outs
            split = send.shape[0] // 2
            if q < split:
                return send, q if bx else split + q
            return (diagonal if bx else keep), q - split
        send, keep, own = outs
        split = keep.shape[0]
        if not bx:
            return own, q
        return (keep, q) if q < split else (send, q - split)

    waiting = True
    ones = jnp.ones((8, 3 * width), BF16)
    three = jnp.concatenate([dq[...], dk[...], dv[...]], axis=1)
    for q in (3, 2, 1, 0):
        z = info[3] ^ (q >> 1) ^ (3 * (q & 1))
        at = pl.ds(pl.multiple_of(z * 256, 256), 256)
        grad = dot_tn(h1[:, at], three)
        if waiting:
            for copy in copies:
                copy.wait()
            waiting = False
        weight = jnp.concatenate(
            [w[pl.ds(z * 2, 2), n * 128 : (n + 1) * 128, :].reshape(256, width)
             for n in range(3)], axis=1)
        shares = dot_nt(ones, (grad * weight.astype(F32)).astype(BF16))
        acc[:, at] = shares / gains[0:1, at]
        grad = grad.astype(BF16)
        for bx in range(2):
            part = jnp.where((info[4] ^ bx) == 1, grad[128:], grad[:128])
            ref, i = spot(bx, q)
            for n in range(3):
                ref[i, n * 128 : (n + 1) * 128, :] = part[:, n * width : (n + 1) * width]
    for bx in range(2):
        for q in range(4):
            at = pl.ds(pl.multiple_of(place_of(info, bx, q) * 128, 128), 128)
            row = jnp.concatenate([acc[0:1, at], gain_grad[0:1, at]], axis=1)
            ref, i = spot(bx, q)
            ref[i, 384:400, :] = jnp.broadcast_to(row, (16, 256)).astype(BF16)


def qkv_back_body(*refs):
    info, grads = refs[0], (refs[1:4], refs[4:7])
    parts = refs[7:12]
    gkeep, gsend, w, sem = refs[12:]
    run_copies(attn_copies(info, parts, w, sem))
    width = w.shape[3]
    model = gkeep.shape[2]

    def step(t, carry):
        at = pl.ds(pl.multiple_of(t * TILE, TILE), TILE)
        grad_h = jnp.zeros((TILE, model), F32)
        for by in range(2):
            for n in range(3):
                weight = w[by, :, n * 128 : (n + 1) * 128, :].reshape(model, width)
                grad_h = grad_h + dot_nt(grads[by][n][at, :], weight)

        @pl.when((t & 1) == info[1])
        def _():
            gkeep[t >> 1] = grad_h

        @pl.when((t & 1) != info[1])
        def _():
            gsend[t >> 1] = grad_h.astype(BF16)

        return carry

    lax.fori_loop(0, gkeep.shape[0] * 2, step, 0, unroll=True)


def input_body(info, gkeep, grecv, x, own_mid, gains, keep, send):
    for half in range(2):
        at = pl.ds(pl.multiple_of((half * 2 + info[1]) * TILE, TILE), TILE)
        xt = x[at, :].astype(F32)
        grad = gkeep[half] + grecv[half].astype(F32)
        inverse = lax.rsqrt(jnp.mean(xt * xt, axis=-1, keepdims=True) + EPSILON)
        scaled = grad * gains[0:1, :]
        share = inverse * inverse * inverse * jnp.mean(scaled * xt, axis=-1, keepdims=True)
        total = own_mid[half] + inverse * scaled - xt * share

        @pl.when(info[0] == half)
        def _():
            keep[...] = total

        @pl.when(info[0] != half)
        def _():
            send[...] = total.astype(BF16)


def plus(*values):
    total = values[0].astype(F32)
    for value in values[1:]:
        total = total + value.astype(F32)
    return total


class Steps(dict):
    __getattr__ = dict.__getitem__
    __setattr__ = dict.__setitem__


def on_device(
    tokens, first_values, seq_counts, norm1_gain, query_weight, key_weight, value_weight,
    out_weight, norm2_gain, gate_weight, up_weight, down_weight, output_cotangent,
):
    slots, piece, model = tokens.shape
    length = piece * lax.axis_size("seq")
    wide = lax.axis_size("dp") // BLOCKS
    s = lax.axis_index("seq")
    place = lax.axis_index("dp")
    y, c = s // 2, s % 2
    d = place // wide
    z, x_at = d // 2, d % 2
    info = jnp.stack([y, c, d, z, x_at, seq_counts[0]]).astype(jnp.int32)
    even = (z & 1) ^ c

    def pregather(shard):
        step = 1
        while step < wide:
            other = flip(shard, "dp", step)
            bit = (place // step) % 2
            shard = pick(
                bit, jnp.concatenate([other, shard]), jnp.concatenate([shard, other]))
            step *= 2
        return shard

    def postscatter(total):
        step = wide // 2
        while step >= 1:
            half = total.shape[0] // 2
            bit = (place // step) % 2
            lo, hi = total[:half], total[half:]
            total = pick(bit, hi, lo) + flip(pick(bit, lo, hi), "dp", step)
            step //= 2
        return total

    def far(v):
        return flip(v, "dp", ZM * wide)

    def near(v):
        return flip(v, "dp", Z1 * wide)

    def over_x(v):
        return flip(v, "dp", X1 * wide)

    def over_y(v):
        return flip(v, "seq", MESH_Y)

    def over_core(v):
        return flip(v, "seq", MESH_C)

    def other_slot(block):
        return pick(y, block[0], block[1])

    def mine_of(low, high):
        return jnp.stack([pick(even, low[1], low[0]), pick(even, high[0], high[1])])

    def theirs_of(low, high):
        return jnp.stack([pick(even, low[0], low[1]), pick(even, high[1], high[0])])

    def own_slot(block, recv):
        return jnp.stack([pick(y, block[1], block[0]), recv])

    def pack(*parts):
        rows = parts[0].shape[-2]
        (out,) = call(
            pack_body, [((4, rows, 256), BF16)], [("v", part) for part in parts], [],
            1000, 1 << 20, vmem=8)
        return out

    local = model // 2
    width = local // 2
    v = Steps()
    v.cosine, v.sine = turn_tables(length)
    v.a0 = jnp.concatenate(
        [pregather(query_weight), pregather(key_weight), pregather(value_weight),
         jnp.pad(jnp.concatenate([pregather(norm1_gain), pregather(norm2_gain)])[None],
                 ((0, 15), (0, 0)))])
    attn_rows = v.a0.shape[0]
    down = pregather(down_weight)
    part_a = down.shape[0] * 192 // 352 // 16 * 16
    part_b = down.shape[0] - part_a
    whole = down.shape[0]
    ffn = jnp.concatenate([pregather(gate_weight).T, pregather(up_weight).T], axis=1)
    v.b0 = jnp.concatenate([ffn[part_a:whole], ffn[whole + part_a :]])[None]
    v.g0 = jnp.concatenate([ffn[:part_a], ffn[whole : whole + part_a], down[:part_a]])
    v.r0 = jnp.concatenate([down[part_a:], pregather(out_weight)])
    out_rows = v.r0.shape[0] - part_b
    v.t_send = other_slot(tokens)
    v.f_send = other_slot(first_values)
    v.c_send = other_slot(output_cotangent)
    v.tokens, v.firsts, v.cots = tokens, first_values, output_cotangent

    v.a0, v.t_send, v.b0 = lax.optimization_barrier(
        (v.a0, v.t_send, v.b0))
    v.ty, v.af, v.an = over_y(v.t_send), far(v.a0), near(v.a0)
    v.bx = over_x(v.b0)
    v.a0, v.af, v.an, v.ty, v.tokens, v.b0, v.bx, v.f_send, v.c_send, v.firsts, v.cots, v.r0, v.g0 = lax.optimization_barrier(
        (v.a0, v.af, v.an, v.ty, v.tokens, v.b0, v.bx, v.f_send, v.c_send, v.firsts, v.cots, v.r0, v.g0))
    v.fy, v.anf, v.rf = over_y(v.f_send), near(v.af), far(v.r0)
    v.bf0 = far(v.b0)
    v.tc = over_core(own_slot(v.tokens, v.ty))
    v.a0, v.af, v.an, v.anf, v.fy, v.tc, v.firsts, v.b0, v.bx, v.bf0, v.r0, v.rf, v.g0, v.c_send, v.cots = lax.optimization_barrier(
        (v.a0, v.af, v.an, v.anf, v.fy, v.tc, v.firsts, v.b0, v.bx, v.bf0, v.r0, v.rf, v.g0, v.c_send, v.cots))
    v.z = pack(v.a0, v.af, v.an, v.anf)
    v.zx, v.zy = over_x(v.z), over_y(v.z)
    v.rlow = jnp.stack([v.r0, v.rf])
    v.rhigh, v.gf = near(v.rlow), far(v.g0)
    v.fc = over_core(own_slot(v.firsts, v.fy))
    v.z, v.zx, v.zy, v.rlow, v.rhigh, v.g0, v.gf, v.fc, v.b0, v.bx, v.bf0, v.c_send, v.cots = lax.optimization_barrier(
        (v.z, v.zx, v.zy, v.rlow, v.rhigh, v.g0, v.gf, v.fc, v.b0, v.bx, v.bf0, v.c_send, v.cots))
    v.zu, v.zv = over_y(v.zx[:SPLIT]), over_x(v.zy[SPLIT:])
    v.rmine = mine_of(v.rlow, v.rhigh)
    v.rother = over_core(theirs_of(v.rlow, v.rhigh))
    v.b10 = over_y(jnp.concatenate([v.b0, v.bx]))
    v.glow = jnp.stack([v.g0, v.gf])
    v.ghigh = near(v.glow)
    v.z, v.zx, v.zy, v.zu, v.zv, v.rmine, v.rother, v.b0, v.bx, v.b10, v.bf0, v.glow, v.ghigh, v.c_send, v.cots = lax.optimization_barrier(
        (v.z, v.zx, v.zy, v.zu, v.zv, v.rmine, v.rother, v.b0, v.bx, v.b10, v.bf0, v.glow, v.ghigh, v.c_send, v.cots))
    v.r = pack(v.rmine, v.rother)
    v.rx, v.ry = over_x(v.r), over_y(v.r)
    v.b3 = jnp.concatenate([v.bx, v.b10])
    v.bf3, v.bn3 = far(v.b3), near(v.b3)
    glow, ghigh = v.glow[:, 2 * part_a :], v.ghigh[:, 2 * part_a :]
    v.gmine, v.gother = mine_of(glow, ghigh), over_core(theirs_of(glow, ghigh))

    def anywhere(*arrays):
        return [("a", array) for array in arrays]

    def values(*arrays):
        return [("v", array) for array in arrays]

    square = ((length, model), BF16)
    tall = ((length, local), BF16)
    tile = (2, piece, model)
    w_scratch = pltpu.VMEM((2, BLOCKS, attn_rows, width), BF16)
    sem16 = pltpu.SemaphoreType.DMA((16,))
    narrow = 2 * length * model * local
    v.x, v.h1, v.q, v.k, v.b, v.gains = call(
        qkv_body, [square, square, tall, tall, tall, ((8, model), F32)],
        [("s", info)] + values(v.tokens, v.ty, v.tc, v.firsts, v.fy, v.fc, v.cosine, v.sine) + anywhere(v.z, v.zx, v.zy, v.zu, v.zv),
        [w_scratch, sem16], 3 * narrow, 14 << 20, vmem=26,
    )
    v.x, v.h1, v.q, v.k, v.b, v.gains, v.r, v.rx, v.ry, v.b0, v.b3, v.bf0, v.bf3, v.bn3, v.glow, v.ghigh, v.gmine, v.gother, v.c_send, v.cots = lax.optimization_barrier(
        (v.x, v.h1, v.q, v.k, v.b, v.gains, v.r, v.rx, v.ry, v.b0, v.b3, v.bf0, v.bf3, v.bn3, v.glow, v.ghigh, v.gmine, v.gother, v.c_send, v.cots))
    v.ru, v.rv = over_y(v.rx[:SPLIT]), over_x(v.ry[SPLIT:])
    v.gl = jnp.concatenate([v.glow[:, : 2 * part_a], v.gmine], axis=1)
    v.gh = jnp.concatenate([v.ghigh[:, : 2 * part_a], v.gother], axis=1)
    v.glx, v.ghy = over_x(v.gl), over_y(v.gh)
    v.bnf3 = near(v.bf3)
    head_specs = [pl.BlockSpec((length, 128), lambda i: (0, i))] * 3
    lse_spec = pl.BlockSpec((1, 2, length), lambda i: (i, 0, 0))
    pairs = local // 128
    v.att, v.lse = call(
        attend_body, [tall, ((pairs, 2, length), F32)], values(v.q, v.k, v.b), [],
        4 * length * length * local, 4 << 20, length * length * pairs * 2, vmem=20,
        grid=(pairs,), in_specs=head_specs, out_specs=[head_specs[0], lse_spec],
    )
    v.att, v.lse, v.r, v.rx, v.ry, v.ru, v.rv, v.gl, v.glx, v.gh, v.ghy, v.bnf3, v.c_send, v.bf0, v.b0 = lax.optimization_barrier(
        (v.att, v.lse, v.r, v.rx, v.ry, v.ru, v.rv, v.gl, v.glx, v.gh, v.ghy, v.bnf3, v.c_send, v.bf0, v.b0))
    v.cy = over_y(v.c_send)
    v.bnf0, v.bn0 = near(v.bf0), near(v.b0)
    (v.part,) = call(
        out_body, [square], [("s", info)] + values(v.att) + anywhere(v.r, v.rx, v.ry, v.ru, v.rv),
        [pltpu.VMEM((local, model), BF16), sem16], narrow, 5 << 20, vmem=12,
    )
    v.att, v.lse, v.r, v.rx, v.ry, v.ru, v.rv, v.part, v.cy, v.cots, v.gl, v.glx, v.gh, v.ghy, v.b0, v.b3, v.bf0, v.bn0, v.bf3, v.bn3, v.bnf0, v.bnf3 = lax.optimization_barrier(
        (v.att, v.lse, v.r, v.rx, v.ry, v.ru, v.rv, v.part, v.cy, v.cots, v.gl, v.glx, v.gh, v.ghy, v.b0, v.b3, v.bf0, v.bn0, v.bf3, v.bn3, v.bnf0, v.bnf3))
    v.precv, v.cc = over_core(v.part), over_core(own_slot(v.cots, v.cy))
    v.part, v.precv, v.cc, v.gl, v.glx, v.gh, v.ghy = lax.optimization_barrier(
        (v.part, v.precv, v.cc, v.gl, v.glx, v.gh, v.ghy))

    def five(rows):
        return [((count, rows, 256), BF16)
                for count in (2 * (4 - SPLIT), 2 * SPLIT, SPLIT, 4 - SPLIT, 4)]

    v.gly, v.glxy = over_y(v.gl), over_y(v.glx)
    v.ghx, v.ghxy = over_x(v.gh), over_x(v.ghy)
    def ffn_scratch(units):
        return [pltpu.VMEM((units, length), BF16), pltpu.VMEM((2 * units, length), BF16),
                pltpu.VMEM((2 * units, model), BF16), pltpu.VMEM((units, model), BF16),
                pltpu.SemaphoreType.DMA((48,))]

    ffn_flops = 36 * length * model
    v.h2, v.gy, v.gh2b, v.resb, v.bsx, v.bsy, v.bkx, v.bky, v.bown = call(
        functools.partial(ffn_body, True), [square] * 4 + five(3 * part_b),
        [("s", info)] + values(v.x, v.part, v.precv, v.gains, v.cots, v.cy, v.cc)
        + anywhere(v.b0, v.bf0, v.bn0, v.bnf0, v.b3, v.bf3, v.bn3, v.bnf3) + anywhere(v.r, v.rx, v.ry, v.ru, v.rv),
        ffn_scratch(4 * part_b), ffn_flops * 2 * part_b, 24 << 20, vmem=40,
    )
    v.h2, v.gy, v.gh2b, v.resb, v.bsx, v.bsy, v.bkx, v.bky, v.bown, v.gl, v.glx, v.gly, v.glxy, v.gh, v.ghx, v.ghy, v.ghxy = lax.optimization_barrier(
        (v.h2, v.gy, v.gh2b, v.resb, v.bsx, v.bsy, v.bkx, v.bky, v.bown, v.gl, v.glx, v.gly, v.glxy, v.gh, v.ghx, v.ghy, v.ghxy))
    v.brx, v.bry = over_x(v.bsx), over_y(v.bsy)
    quads = [((4, 2 * part_a, 256), BF16)] * 4 + [((2, 2, 4, part_a, 256), BF16)]
    (v.gh2, v.rkeep, v.rsend, v.n0, v.n1, v.n2, v.n3, v.dgrad) = call(
        functools.partial(ffn_body, False), [square, (tile, F32), (tile, BF16)] + quads,
        [("s", info)] + values(v.h2, v.gy, v.gh2b, v.resb)
        + anywhere(v.gl, v.glx, v.gly, v.glxy, v.gh, v.ghx, v.ghy, v.ghxy),
        ffn_scratch(4 * part_a), ffn_flops * 2 * part_a, 24 << 20, vmem=40,
    )
    v.gh2, v.rkeep, v.rsend, v.n0, v.n1, v.n2, v.n3, v.dgrad, v.brx, v.bry, v.bkx, v.bky, v.bown, v.part, v.precv = lax.optimization_barrier(
        (v.gh2, v.rkeep, v.rsend, v.n0, v.n1, v.n2, v.n3, v.dgrad, v.brx, v.bry, v.bkx, v.bky, v.bown, v.part, v.precv))

    def fold(name):
        v[name + "fx"] = plus(v[name + "kx"], v[name + "ry"][:SPLIT]).astype(BF16)
        v[name + "fy"] = plus(v[name + "ky"], v[name + "rx"][: 4 - SPLIT]).astype(BF16)

    def total_of(name):
        low = plus(v[name + "own"][:SPLIT], v[name + "ry"][SPLIT:], v[name + "rx2"])
        high = plus(v[name + "own"][SPLIT:], v[name + "rx"][4 - SPLIT :], v[name + "ry2"])
        return jnp.concatenate([low, high])

    def rows_out(name, total, first):
        v[name + "t"] = total
        v[name + "m"] = over_core(total[2:, first:].astype(BF16))

    def quarter(name, first, q):
        total, recv = v[name + "t"], v[name + "m"]
        rows = total[q >> 1, first:]
        other = recv[q >> 1].astype(F32)
        mine = pick(even, other, rows) if q in (0, 3) else pick(even, rows, other)
        return mine if first == 0 else jnp.concatenate([total[q, :first], mine])

    def owner_send(halves_of):
        return pick(y, halves_of[0], halves_of[1])

    def owner_keep(halves_of):
        return pick(y, halves_of[1], halves_of[0])

    def both_slots(keep, recv):
        return pick(y, jnp.stack([recv, keep]), jnp.stack([keep, recv]))

    def own_tokens(full):
        cut_up = full.reshape(2, 2, piece, full.shape[-1])
        return pick(c, cut_up[:, 1], cut_up[:, 0])

    v.gh2r = over_core(v.gh2)
    v.rrecv = over_core(v.rsend)
    fold("b")
    v.brx2, v.bry2 = over_x(v.bfx), over_y(v.bfy)
    v.nn3 = near(v.n3)
    (v.datt, v.mid, v.gain2,
     v.ssx, v.ssy, v.skx, v.sky, v.sown) = call(
        out_back_body, [tall, (tile, F32), ((8, model), F32)] + five(part_a + out_rows),
        [("s", info)] + values(v.gh2, v.gh2r, v.x, v.part, v.precv, v.gy, v.gains, v.att, v.dgrad) + anywhere(v.r, v.rx, v.ry, v.ru, v.rv),
        [pltpu.VMEM((local, model), BF16), pltpu.VMEM((length, model), BF16), sem16],
        2 * narrow, 20 << 20, vmem=56,
    )
    v.datt, v.mid, v.gain2, v.ssx, v.ssy, v.skx, v.sky, v.sown, v.bown, v.brx, v.bry, v.brx2, v.bry2, v.n0, v.n1, v.n2, v.nn3, v.rkeep, v.rrecv, v.part, v.precv = lax.optimization_barrier(
        (v.datt, v.mid, v.gain2, v.ssx, v.ssy, v.skx, v.sky, v.sown, v.bown, v.brx, v.bry, v.brx2, v.bry2, v.n0, v.n1, v.n2, v.nn3, v.rkeep, v.rrecv, v.part, v.precv))
    v.srx, v.sry = over_x(v.ssx), over_y(v.ssy)
    v.n1 = plus(v.n1, v.nn3).astype(BF16)
    v.nf1, v.nn2 = far(v.n1[2:]), near(v.n2)
    rows_out("b", total_of("b"), 2 * part_b)

    live_now = jnp.where(y < seq_counts[0], 1.0, 0.0)
    middle_own = own_tokens(v.x).astype(F32) + plus(
        own_tokens(v.part), own_tokens(v.precv))
    result = (live_now * (middle_own + plus(v.rkeep, v.rrecv))).astype(BF16)
    v.okeep, v.orecv = owner_keep(result), over_y(owner_send(result))
    def attend_back(side):
        first = side * (pairs // 2)
        column = pl.BlockSpec((length, 128), lambda i: (0, i + first))
        table = pl.BlockSpec((length, 128), lambda i: (0, 0))
        sums = pl.BlockSpec((1, 2, length), lambda i: (i + first, 0, 0))
        target = pl.BlockSpec((length, 128), lambda i: (0, i))
        return call(
            attend_back_body, [((length, width), BF16)] * 3,
            values(v.q, v.k, v.b, v.datt, v.lse, v.cosine, v.sine),
            [pltpu.VMEM((length, 128), F32), pltpu.VMEM((length, 128), F32)],
            5 * length * length * local, 4 << 20, length * length * pairs, vmem=16,
            grid=(pairs // 2,), in_specs=[column] * 4 + [sums, table, table],
            out_specs=[target] * 3,
        )

    def attn_grads(side):
        counts = (4 - SPLIT, 2 * SPLIT, 4 - SPLIT) if side else (4 - SPLIT, SPLIT, 4)
        arrays = (v.zy, v.zu, v.zv) if side else (v.z, v.zx)
        return call(
            functools.partial(qkv_grad_body, side),
            [((count, attn_rows, width), BF16) for count in counts],
            [("s", info)] + values(*(v.grads1 if side else v.grads0), v.h1, v.gains, v.gain2)
            + anywhere(*arrays),
            [pltpu.VMEM((BLOCKS, attn_rows, width), BF16), pltpu.VMEM((8, model), F32),
             pltpu.SemaphoreType.DMA((8,))], 3 * narrow // 2, 7 << 20, vmem=14,
        )

    v.grads1 = attend_back(1)
    v.qdx, v.qsy, v.qky = attn_grads(1)
    v.grads1, v.qdx, v.qsy, v.qky, v.q, v.k, v.b, v.datt, v.srx, v.sry, v.skx, v.sky, v.sown, v.n0, v.n1, v.nf1, v.nn2, v.bt, v.bm, v.okeep, v.orecv = lax.optimization_barrier(
        (v.grads1, v.qdx, v.qsy, v.qky, v.q, v.k, v.b, v.datt, v.srx, v.sry, v.skx, v.sky, v.sown, v.n0, v.n1, v.nf1, v.nn2, v.bt, v.bm, v.okeep, v.orecv))
    v.qry, v.qrd = over_y(v.qsy), over_x(v.qdx)
    fold("s")
    v.srx2 = over_x(v.sfx)
    v.nf0 = far(v.n1[:2])
    v.bzn = near(jnp.stack([quarter("b", 2 * part_b, 2), quarter("b", 2 * part_b, 3)]).astype(BF16))
    v.grads0 = attend_back(0)
    v.qsx, v.qkx, v.qown = attn_grads(0)
    v.grads0, v.grads1, v.qsx, v.qkx, v.qown, v.qry, v.qrd, v.qky, v.srx, v.sry, v.srx2, v.sfy, v.sown, v.n0, v.nf0, v.nf1, v.nn2, v.bzn, v.bt, v.bm, v.okeep, v.orecv = lax.optimization_barrier(
        (v.grads0, v.grads1, v.qsx, v.qkx, v.qown, v.qry, v.qrd, v.qky, v.srx, v.sry, v.srx2, v.sfy, v.sown, v.n0, v.nf0, v.nf1, v.nn2, v.bzn, v.bt, v.bm, v.okeep, v.orecv))
    v.qrx = over_x(v.qsx)
    v.sry2 = over_y(v.sfy)
    v.nt0 = plus(v.n0[:2], v.nf0, v.nn2[:2])
    v.nx = over_y(plus(v.n0[2:], v.nf1, v.nn2[2:]).astype(BF16))
    v.bt0 = plus(quarter("b", 2 * part_b, 0), v.bzn[0])
    v.bzf = far(plus(quarter("b", 2 * part_b, 1), v.bzn[1]).astype(BF16))
    v.gkeep, v.gsend = call(
        qkv_back_body, [(tile, F32), (tile, BF16)],
        [("s", info)] + values(*v.grads0, *v.grads1) + anywhere(v.z, v.zx, v.zy, v.zu, v.zv), [w_scratch, sem16],
        3 * narrow, 14 << 20, vmem=14,
    )
    v.gkeep, v.gsend, v.qry, v.qrd, v.qky, v.qrx, v.qkx, v.qown, v.bt0, v.bzf, v.nt0, v.nx, v.srx, v.sry, v.srx2, v.sry2, v.sown, v.grads0, v.grads1, v.okeep, v.orecv = lax.optimization_barrier(
        (v.gkeep, v.gsend, v.qry, v.qrd, v.qky, v.qrx, v.qkx, v.qown, v.bt0, v.bzf, v.nt0, v.nx, v.srx, v.sry, v.srx2, v.sry2, v.sown, v.grads0, v.grads1, v.okeep, v.orecv))
    output = both_slots(v.okeep, v.orecv)
    total_b = plus(v.bt0, v.bzf)
    v.grecv = over_core(v.gsend)
    v.qfx = plus(v.qkx, v.qry[:SPLIT]).astype(BF16)
    v.qfy = plus(v.qky, v.qrd).astype(BF16)
    v.qrx2, v.qry2 = over_x(v.qfx), over_y(v.qfy)
    rows_out("s", total_of("s"), 0)
    v.nt0 = plus(v.nt0, v.nx)
    v.ny = over_x(v.nt0[1].astype(BF16))
    v.ikeep, v.isend = call(
        input_body, [((piece, model), F32), ((piece, model), BF16)],
        [("s", info)] + values(v.gkeep, v.grecv, v.x, v.mid, v.gains), [], 1000, 8 << 20, vmem=12,
    )
    v.ikeep, v.isend, v.qrx, v.qry, v.qrx2, v.qry2, v.qown, v.st, v.sm, v.nt0, v.ny, v.grads0, v.grads1 = lax.optimization_barrier(
        (v.ikeep, v.isend, v.qrx, v.qry, v.qrx2, v.qry2, v.qown, v.st, v.sm, v.nt0, v.ny, v.grads0, v.grads1))
    total_a = plus(v.nt0[0], v.ny)
    low = plus(v.qown[:SPLIT], v.qry[SPLIT:], v.qrx2)
    high = plus(v.qown[SPLIT:], v.qrx, v.qry2)
    v.qt = jnp.concatenate([low, high])
    v.qz, v.sz = near(v.qt[3].astype(BF16)), near(quarter("s", 0, 3).astype(BF16))
    v.irecv = over_y(v.isend)
    cuts = [grads[2].reshape(2, 2, piece, width) for grads in (v.grads0, v.grads1)]
    dv_keep = [pick(c, cut[:, 1], cut[:, 0]) for cut in cuts]
    dv_recv = over_core(
        jnp.concatenate([pick(c, cut[:, 0], cut[:, 1]) for cut in cuts], axis=-1))
    dv_recv = [dv_recv[..., :width], dv_recv[..., width:]]
    blocks = []
    for column_y, column_c in bits(2):
        side = y ^ column_y
        mine = pick(side, dv_keep[1], dv_keep[0])
        theirs = pick(side, dv_recv[1], dv_recv[0])
        blocks.append(pick(c ^ column_c, theirs, mine))
    grad_rows = jnp.concatenate(blocks, axis=-1)
    v.fkeep, v.fsend = owner_keep(grad_rows), owner_send(grad_rows)
    v.qt, v.qz, v.st, v.sm, v.sz, v.irecv, v.ikeep, v.fkeep, v.fsend = lax.optimization_barrier(
        (v.qt, v.qz, v.st, v.sm, v.sz, v.irecv, v.ikeep, v.fkeep, v.fsend))
    v.qzf = far(plus(v.qt[1], v.qz).astype(BF16))
    v.szf = far(plus(quarter("s", 0, 1), v.sz).astype(BF16))
    v.qzn = near(v.qt[2].astype(BF16))
    v.szn = near(quarter("s", 0, 2).astype(BF16))
    v.frecv = over_y(v.fsend)
    v.qt0, v.st0 = v.qt[0], quarter("s", 0, 0)
    grad_input = both_slots(v.ikeep, v.irecv.astype(F32))
    v.qt0, v.st0, v.qzf, v.szf, v.qzn, v.szn, v.fkeep, v.frecv = lax.optimization_barrier(
        (v.qt0, v.st0, v.qzf, v.szf, v.qzn, v.szn, v.fkeep, v.frecv))
    total = plus(v.qt0, v.qzf, v.qzn)
    gain_total = total[384]
    gain_share = jnp.broadcast_to(gain_total[None, :128], (8, 128))
    gain_sum = gain_total[:128] + over_core(gain_share)[0] + (
        over_y(gain_share)[0] + flip(gain_share, "seq", MESH_Y | MESH_C)[0])
    total_s = plus(v.st0, v.szf, v.szn)
    grad_first = both_slots(v.fkeep, v.frecv).astype(F32)

    def weave(lanes):
        pieces = [total_a[:part_a, lanes], total_b[:part_b, lanes],
                  total_a[part_a:, lanes], total_b[part_b : 2 * part_b, lanes]]
        return jnp.concatenate(pieces).T

    return (
        output,
        grad_input,
        grad_first,
        postscatter(gain_sum),
        postscatter(total[:128]),
        postscatter(total[128:256]),
        postscatter(total[256:384]),
        postscatter(total_s[part_a:]),
        postscatter(gain_total[128:]),
        postscatter(weave(slice(0, 128))),
        postscatter(weave(slice(128, 256))),
        postscatter(jnp.concatenate([total_s[:part_a], total_b[2 * part_b :]])),
    )


def solution(mesh):
    cut = P("dp", "seq")
    flat = P("dp")
    whole = P("dp", "seq", None)
    return jax.shard_map(
        on_device,
        mesh=mesh,
        in_specs=(whole, whole, flat, flat, cut, cut, cut, cut, flat, cut, cut, cut, whole),
        out_specs=(whole, whole, whole, flat, cut, cut, cut, cut, flat, cut, cut, cut),
        check_vma=False,
    )
```
